512 devices in a mesh: gx: 32 (over y, z_lo, core), gy: 16 (over x, z_hi).
Axes of the slice: x: 4, y: 8, z: 8 (z_hi: 4, z_lo: 2; z = z_hi * 2 + z_lo), core: 2. Of those that a mesh axis runs over, the one named last changes fastest.
Arguments:
- checkpoint: float32 [512, 512, 256], P('gx', 'gy'), may hold values from -4 to 4
- terminal_adjoint: float32 [512, 512, 256], P('gx', 'gy'), may hold values from -6 to 6
- diffusivity: float32 [512, 512, 256], P('gx', 'gy'), may hold values from 0.3 to 2
- controls: float32 [4, 4096], P(None, ('gx', 'gy')), may hold values from -5 to 5
- owner_map: int32 [4096], replicated, may hold values from 0 to 4095, each once
- act_ids: int32 [8192], P(('gx', 'gy')), may hold values from 0 to 4095, as said below
- slot_tiles: int32 [8192], P(('gx', 'gy')), may hold values from 0 to 1023
- slot_count: int32 [512], P(('gx', 'gy')), may hold values from 0 to 16, as said below
- free_list: int32 [4, 2048], replicated, may hold values from 0 to 4095, as said below
Outputs:
- start_adjoint: float32 [512, 512, 256], P('gx', 'gy')
- gradient: float32 [4, 4096], P(None, ('gx', 'gy'))
The draws below stay inside these ranges and needn't reach their ends.
Inputs may be any that keep to these rules, and one draw needn't show every extreme that they name: `act_ids`: over all devices the live slots name every actuator exactly once; entries of slots that are not live are arbitrary actuators. `slot_count`: counts sum to 4096; some device has 16 live slots. `free_list`: each row names distinct actuators.
All inputs are finite; a program needn't handle non-finite values.
Results may differ from the reference program's by a relative error of at most 0.0001.
Values sent between devices are 32-bit elements; how exact they have to be, the bound alone decides.
No kernel may reach another device: no remote copies, remote signals or barrier semaphores. Data moves between devices by JAX's collectives and lax.ppermute only.
A program may use at most 64 MiB of HBM per device.

```python
import math
import jax
import jax.numpy as jnp
from jax import lax

CX = 16
CY = 32
TZ = 128
STEPS = 4
ACT_DEV = 8
SLOTS = 16
NDEV = 512
ACT = 4096
FREE = 2048
TILES = 1024
NX = 512
NY = 512
NZ = 256
N_GX = 32
N_GY = 16


def slot_layout(key):
    half = NDEV // 2
    spread = jax.random.randint(jax.random.fold_in(key, 11), (half,), 0, SLOTS - ACT_DEV + 1)
    forced = jax.random.randint(jax.random.fold_in(key, 12), (), 0, half)
    spread = jnp.where(jnp.arange(half) == forced, SLOTS - ACT_DEV, spread)
    counts = jnp.stack([ACT_DEV + spread, ACT_DEV - spread], axis=1).reshape(NDEV).astype(jnp.int32)
    starts = jnp.cumsum(counts) - counts
    shuffle = jax.random.permutation(jax.random.fold_in(key, 13), ACT).astype(jnp.int32)
    column = jnp.arange(SLOTS, dtype=jnp.int32)
    alive = column[None, :] < counts[:, None]
    target = jnp.clip(starts[:, None] + column[None, :], 0, ACT - 1)
    filler = jax.random.randint(jax.random.fold_in(key, 14), (NDEV, SLOTS), 0, ACT).astype(jnp.int32)
    ids = jnp.where(alive, shuffle[target], filler).reshape(-1)
    return (ids, counts)


def draw_act_ids(key, part):
    ids, counts = slot_layout(key)
    return ids


def draw_slot_count(key, part):
    ids, counts = slot_layout(key)
    return counts


def draw_free_list(key, part):
    key = jax.random.fold_in(key, 21)
    rows = [jax.random.permutation(jax.random.fold_in(key, step), ACT)[:FREE] for step in range(STEPS)]
    return jnp.stack(rows).astype(jnp.int32)


def touch_ends(result, rng, low, top_value):
    longest = result.shape.index(max(result.shape))
    spots = []
    for shift in (0, 1):
        where = [jax.random.randint(jax.random.fold_in(rng, axis), (), 0, length) for axis, length in enumerate(result.shape)]
        where[longest] = (where[longest] + shift) % result.shape[longest]
        spots.append(tuple(where))
    return result.at[spots[0]].set(low).at[spots[1]].set(top_value)


def levels(key, dims, pieces, least, top_value):
    gain, own = 1.0, jax.random.fold_in(key, 6)
    for dim, parts in pieces:
        heights = jnp.exp(jax.random.uniform(jax.random.fold_in(own, dim), (parts,), jnp.float32, least / len(pieces), top_value / len(pieces)))
        gain = gain * jnp.repeat(heights, dims[dim] // parts).reshape([-1 if axis == dim else 1 for axis in range(len(dims))])
    return gain


def gaussian(stream_key, shape, deviation, limit, pieces=(), held_as=jnp.bfloat16):
    values = deviation * jax.random.normal(stream_key, shape, jnp.float32)
    if pieces:
        values = values * levels(stream_key, shape, pieces, -0.22, 0.18)
    return jnp.clip(values, -limit, limit).astype(held_as)


def setup_inputs(seed: int = 0) -> dict:
    key_list = jax.random.split(jax.random.key(seed), 10)
    return {
        "checkpoint": gaussian(key_list[0], (NX, NY, NZ), 1.0, 4.0, ((0, 32), (1, 16)), jnp.float32),
        "terminal_adjoint": gaussian(key_list[1], (NX, NY, NZ), 1.0, 6.0, ((0, 32), (1, 16)), jnp.float32),
        "diffusivity": jnp.clip(jnp.exp(math.log(2.0) - 1.89712 * jax.random.uniform(key_list[2], (NX, NY, NZ), jnp.float32) ** levels(key_list[2], (NX, NY, NZ), ((0, 32), (1, 16)), -0.2, 0.2)), 0.3, 2.0),
        "controls": gaussian(key_list[3], (STEPS, ACT), 1.0, 5.0, ((1, 512),), jnp.float32),
        "owner_map": jax.random.permutation(key_list[4], ACT).astype(jnp.int32),
        "act_ids": draw_act_ids(jax.random.fold_in(key_list[9], 71), 0),
        "slot_tiles": touch_ends(jax.random.randint(key_list[6], (NDEV * SLOTS,), 0, TILES), jax.random.fold_in(key_list[6], 1), 0, TILES - 1).astype(jnp.int32),
        "slot_count": draw_slot_count(jax.random.fold_in(key_list[9], 71), 0),
        "free_list": draw_free_list(jax.random.fold_in(key_list[9], 71), 0),
    }


time_step = 0.05
velocity = (1.0, 0.7, 0.4)

def interior(padded, axis, offset):
    window = [slice(1, -1), slice(1, -1), slice(1, -1)]
    window[axis] = slice(1 + offset, padded.shape[axis] - 1 + offset)
    return padded[tuple(window)]

def evolve(padded, field, kappa, source):
    laplace = -6.0 * field
    advection = jnp.zeros_like(field)
    flux = 0.5 * padded * padded
    for axis in range(3):
        laplace = laplace + interior(padded, axis, 1) + interior(padded, axis, -1)
        advection = advection + velocity[axis] * 0.5 * (interior(flux, axis, 1) - interior(flux, axis, -1))
    return field + time_step * (kappa * laplace - advection + source)

def advance(field, kappa, source):
    return evolve(jnp.pad(field, 1), field, kappa, source)

def tile_view(field):
    shaped = field.reshape(N_GX, CX, N_GY, CY, NZ // TZ, TZ).transpose(0, 2, 1, 3, 4, 5)
    return shaped.reshape(NDEV, TILES, TZ)

def from_tiles(tiles):
    shaped = jnp.broadcast_to(tiles.reshape(N_GX, N_GY, CX, CY, NZ // TZ, 1), (N_GX, N_GY, CX, CY, NZ // TZ, TZ))
    shaped = shaped.reshape(N_GX, N_GY, CX, CY, NZ).transpose(0, 2, 1, 3, 4)
    return shaped.reshape(NX, NY, NZ)

def reference(checkpoint, terminal_adjoint, diffusivity, controls, owner_map, act_ids, slot_tiles, slot_count, free_list):
    alive_mask = (jnp.arange(SLOTS)[None, :] < slot_count[:, None]).reshape(-1).astype(jnp.float32)
    device_of = jnp.repeat(jnp.arange(NDEV, dtype=jnp.int32), SLOTS)
    owner_slot = owner_map[act_ids]
    slot_values = controls[:, owner_slot] * alive_mask[None, :]
    states = []
    state = checkpoint
    for step in range(STEPS):
        tiles = jnp.zeros((NDEV, TILES), jnp.float32).at[device_of, slot_tiles].add(slot_values[step])
        states.append(state)
        state = advance(state, diffusivity, from_tiles(tiles))
    adjoint = terminal_adjoint
    rows = [None] * STEPS
    for step in range(STEPS - 1, -1, -1):
        tile_sums = lax.optimization_barrier(jnp.sum(tile_view(adjoint), axis=-1))
        values = time_step * tile_sums[device_of, slot_tiles] * alive_mask
        rows[step] = jnp.zeros((ACT,), jnp.float32).at[owner_slot].add(values)
        zeros_source = jnp.zeros_like(adjoint)
        _, pullback = jax.vjp(lambda v: advance(v, diffusivity, zeros_source), states[step])
        adjoint = pullback(adjoint)[0]
    flags = jnp.zeros((STEPS, ACT), jnp.float32).at[jnp.arange(STEPS)[:, None], owner_map[free_list]].set(1.0)
    return (adjoint, jnp.stack(rows) * flags)
```

```python
import functools

import jax
import jax.numpy as jnp
from jax import lax
from jax.experimental import pallas as pl
from jax.experimental.pallas import tpu as pltpu
from jax.sharding import PartitionSpec as P

TZ = 128
DT = 0.05
VEL = (1.0, 0.7, 0.4)
AXES = ("gx", "gy")

WIDE = (6, 5, 4)
LAYERS = sum(WIDE)
XO = 6
YO = 12
YR = 56
LANES = 128
POS, TIL = 32, 48


def corner_pieces():
    pieces, row = [], 0
    for field, wide in enumerate(WIDE):
        for layer in range(1, wide):
            pieces.append((field, layer, wide - layer, row))
            row += wide - layer
    return pieces, -(-row // 8) * 8


CORNER, CORNER_ROWS = corner_pieces()


def pack_kernel(
    cx, cy, ck_ref, kp_ref, ta_ref, ctl_ref, own_ref, act_ref, til_ref, cnt_ref,
    yup_ref, ydn_ref, xup_ref, xdn_ref, uu_ref, ud_ref, du_ref, dd_ref, row_ref,
):
    fields = (ck_ref, kp_ref, ta_ref)
    lane = lax.broadcasted_iota(jnp.int32, (1, LANES), 1)
    row = jnp.zeros((1, LANES), jnp.float32)
    steps, owned = ctl_ref.shape
    for n in range(steps):
        for k in range(owned):
            row = jnp.where(lane == n * owned + k, ctl_ref[n, k], row)
    for j in range(act_ref.shape[0]):
        place = jnp.where(j < cnt_ref[0], own_ref[act_ref[j]], -1)
        row = jnp.where(lane == POS + j, place.astype(jnp.float32), row)
        row = jnp.where(lane == TIL + j, til_ref[j].astype(jnp.float32), row)
    row_ref[...] = jnp.broadcast_to(row, row_ref.shape)
    halves = (slice(0, LANES), slice(LANES, 2 * LANES))
    at = 0
    for field, wide in zip(fields, WIDE):
        for i in range(wide):
            for h in range(2):
                xup_ref[at + i, h] = field[cx - wide + i, :, halves[h]]
                xdn_ref[at + i, h] = field[i, :, halves[h]]
        at += wide

    def rows(x, carry):
        at = 0
        for field, wide in zip(fields, WIDE):
            for h in range(2):
                yup_ref[x, h, at : at + wide, :] = field[x, cy - wide : cy, halves[h]]
                ydn_ref[x, h, at : at + wide, :] = field[x, 0:wide, halves[h]]
            at += wide
        return carry

    lax.fori_loop(0, cx, rows, 0)
    for f, layer, count, start in CORNER:
        for h in range(2):
            for up_x, up_y, ref in ((1, 1, uu_ref), (1, 0, ud_ref), (0, 1, du_ref), (0, 0, dd_ref)):
                x = cx - layer if up_x else layer - 1
                y = cy - count if up_y else 0
                ref[h, start : start + count, :] = fields[f][x, y : y + count, halves[h]]


def window_kernel(
    cx, cy, nx, ny, ck_ref, kp_ref, ta_ref,
    yup_ref, ydn_ref, xup_ref, xdn_ref, uu_ref, ud_ref, du_ref, dd_ref, tab_ref,
    out_ref, msg_ref,
    s0, s1, s2, s3, kap, a4, a3, a2, a1, qa, qb,
    near_v, near_s, list_s, pick_v, which_v, amp_v, sum_v, sem,
):
    gx = lax.axis_index("gx")
    gy = lax.axis_index("gy")
    me = gx * ny + gy
    halves = (slice(0, LANES), slice(LANES, 2 * LANES))
    lane = lax.broadcasted_iota(jnp.int32, (1, LANES), 1)

    order = [(0, 0)] + [(a, b) for a in (-1, 0, 1) for b in (-1, 0, 1) if (a, b) != (0, 0)]
    for i, (a, b) in enumerate(order):
        there = (gx + a >= 0) & (gx + a < nx) & (gy + b >= 0) & (gy + b < ny)
        source = jnp.where(there, me + a * ny + b, me)
        seen = tab_ref[pl.ds(source, 1), :]
        near_v[i : i + 1, :] = jnp.where(there, seen, -1.0).astype(jnp.int32)
    ids = pltpu.make_async_copy(near_v, near_s, sem)
    ids.start()

    fields = ((ck_ref, s0), (kp_ref, kap), (ta_ref, a4))
    for f, (own, ext) in enumerate(fields):
        wide, at = WIDE[f], sum(WIDE[:f])

        def assemble(x, carry, own=own, ext=ext, wide=wide, at=at):
            for h in range(2):
                ext[XO + x, h, YO : YO + cy, :] = own[x, :, halves[h]]
                ext[XO + x, h, YO - wide : YO, :] = yup_ref[x, h, at : at + wide, :]
                ext[XO + x, h, YO + cy : YO + cy + wide, :] = ydn_ref[x, h, at : at + wide, :]
            return carry

        lax.fori_loop(0, cx, assemble, 0)
        for i in range(wide):
            for h in range(2):
                ext[XO - wide + i, h, YO : YO + cy, :] = xup_ref[at + i, h]
                ext[XO + cx + i, h, YO : YO + cy, :] = xdn_ref[at + i, h]
    for f, layer, count, start in CORNER:
        ext = fields[f][1]
        for h in range(2):
            for up_x, up_y, ref in ((1, 1, uu_ref), (1, 0, ud_ref), (0, 1, du_ref), (0, 0, dd_ref)):
                x = XO - layer if up_x else XO + cx + layer - 1
                y = YO - count if up_y else YO + cy
                ext[x, h, y : y + count, :] = ref[h, start : start + count, :]

    ids.wait()
    total = jnp.int32(0)
    own_total = jnp.int32(0)
    for i, (a, b) in enumerate(order):
        for j in range(16):
            place = near_s[i, POS + j]
            tile = near_s[i, TIL + j]
            x = lax.shift_right_logical(tile, 6) + (XO + a * cx)
            y = (lax.shift_right_logical(tile, 1) & (cy - 1)) + (YO + b * cy)
            keep = place >= 0
            if a != 0:
                keep &= (x >= XO - 5) & (x < XO + cx + 5)
            if b != 0:
                keep &= (y >= YO - 5) & (y < YO + cy + 5)
            list_s[0, total] = x
            list_s[1, total] = tile & 1
            list_s[2, total] = y
            list_s[3, total] = place
            total = total + keep.astype(jnp.int32)
        if i == 0:
            own_total = total

    def pick(e, carry):
        place = list_s[3, e]
        pick_v[pl.ds(e, 1), :] = tab_ref[pl.ds(lax.shift_right_logical(place, 3), 1), :]
        which_v[pl.ds(e, 1), :] = jnp.broadcast_to(place & 7, (1, LANES))
        return carry

    lax.fori_loop(0, total, pick, 0)
    lanes = lax.broadcasted_iota(jnp.int32, pick_v.shape, 1)
    for n in range(3):
        chosen = jnp.where(lanes - 8 * n == which_v[...], pick_v[...], 0.0)
        amp_v[n] = jnp.broadcast_to(DT * jnp.sum(chosen, axis=1, keepdims=True), pick_v.shape)

    lo_x, hi_x, lo_y, hi_y = gx == 0, gx == nx - 1, gy == 0, gy == ny - 1

    def clear_outside(ref):
        @pl.when(lo_x)
        def _():
            ref[XO - 1] = jnp.zeros(ref.shape[1:], jnp.float32)

        @pl.when(hi_x)
        def _():
            ref[XO + cx] = jnp.zeros(ref.shape[1:], jnp.float32)

        @pl.when(lo_y)
        def _():
            ref[:, :, YO - 1 : YO, :] = jnp.zeros((ref.shape[0], 2, 1, LANES), jnp.float32)

        @pl.when(hi_y)
        def _():
            ref[:, :, YO + cy : YO + cy + 1, :] = jnp.zeros((ref.shape[0], 2, 1, LANES), jnp.float32)

    def depth(v0, v1):
        first = lax.broadcasted_iota(jnp.int32, v0.shape, 1) == 0
        last = lax.broadcasted_iota(jnp.int32, v0.shape, 1) == LANES - 1
        f0, f1 = pltpu.roll(v0, 1, 1), pltpu.roll(v1, 1, 1)
        b0, b1 = pltpu.roll(v0, LANES - 1, 1), pltpu.roll(v1, LANES - 1, 1)
        before = (jnp.where(first, 0.0, f0), jnp.where(first, f0, f1))
        after = (jnp.where(last, b1, b0), jnp.where(last, 0.0, b1))
        return before, after

    def forward(src, dst, lo, hi, y0, rows):
        def plane(x, carry):
            mid = [src[x, h, pl.ds(y0, rows), :] for h in range(2)]
            before, after = depth(*mid)
            for h in range(2):
                f = mid[h]
                pairs = (
                    (src[x + 1, h, pl.ds(y0, rows), :], src[x - 1, h, pl.ds(y0, rows), :]),
                    (src[x, h, pl.ds(y0 + 1, rows), :], src[x, h, pl.ds(y0 - 1, rows), :]),
                    (after[h], before[h]),
                )
                lap, adv = -6.0 * f, 0.0
                for v, (p, m) in zip(VEL, pairs):
                    both = p + m
                    lap = lap + both
                    adv = adv + (0.25 * v) * (both * (p - m))
                kappa = kap[x, h, pl.ds(y0, rows), :]
                dst[x, h, pl.ds(y0, rows), :] = f + DT * (kappa * lap - adv)
            return carry

        lax.fori_loop(lo, hi, plane, 0)

    def actuate(n, dst):
        def one(e, carry):
            x, h, y = list_s[0, e], list_s[1, e], list_s[2, e]
            dst[x, h, pl.ds(y, 1), :] += amp_v[n, pl.ds(e, 1), :]
            return carry

        lax.fori_loop(0, total, one, 0)
        clear_outside(dst)

    forward(s0, s1, XO - 5, XO, 8, 40)
    forward(s0, s1, XO, XO + cx, 4, 48)
    forward(s0, s1, XO + cx, XO + cx + 5, 8, 40)
    actuate(0, s1)
    forward(s1, s2, XO - 4, XO + cx + 4, 8, 40)
    actuate(1, s2)
    forward(s2, s3, XO - 3, XO + cx + 3, 8, 40)
    actuate(2, s3)

    def scale(x, carry):
        for h in range(2):
            qa[x, h] = kap[x, h] * a4[x, h]
        return carry

    lax.fori_loop(XO - 4, XO + cx + 4, scale, 0)

    def step(adj, q, state, x, y0, rows):
        mid = [adj[x, h, pl.ds(y0, rows), :] for h in range(2)]
        qmid = [q[x, h, pl.ds(y0, rows), :] for h in range(2)]
        before, after = depth(*mid)
        qbefore, qafter = depth(*qmid)
        result = []
        for h in range(2):
            lap = (
                (q[x + 1, h, pl.ds(y0, rows), :] + q[x - 1, h, pl.ds(y0, rows), :])
                + (q[x, h, pl.ds(y0 + 1, rows), :] + q[x, h, pl.ds(y0 - 1, rows), :])
                + (qafter[h] + qbefore[h])
            ) - 6.0 * qmid[h]
            drift = (
                (0.5 * VEL[0]) * (adj[x + 1, h, pl.ds(y0, rows), :] - adj[x - 1, h, pl.ds(y0, rows), :])
                + (0.5 * VEL[1]) * (adj[x, h, pl.ds(y0 + 1, rows), :] - adj[x, h, pl.ds(y0 - 1, rows), :])
                + (0.5 * VEL[2]) * (after[h] - before[h])
            )
            result.append(mid[h] + DT * (lap + state[x, h, pl.ds(y0, rows), :] * drift))
        return result

    def backward(adj, q, state, dst, qdst, wide):
        def plane(x, carry):
            for h, value in enumerate(step(adj, q, state, x, 8, 40)):
                dst[x, h, pl.ds(8, 40), :] = value
                qdst[x, h, pl.ds(8, 40), :] = kap[x, h, pl.ds(8, 40), :] * value
            return carry

        lax.fori_loop(XO - wide, XO + cx + wide, plane, 0)
        clear_outside(dst)

    backward(a4, qa, s3, a3, qb, 3)
    backward(a3, qb, s2, a2, qa, 2)
    backward(a2, qa, s1, a1, qb, 1)

    def final(x, carry):
        for h, value in enumerate(step(a1, qb, s0, XO + x, YO, cy)):
            out_ref[x, :, halves[h]] = value
        return carry

    lax.fori_loop(0, cx, final, 0)

    msg_ref[...] = jnp.zeros(msg_ref.shape, jnp.float32)

    def foot(e, carry):
        x, h, y = list_s[0, e], list_s[1, e], list_s[2, e]
        for n, adj in enumerate((a1, a2, a3, a4)):
            sum_v[n, pl.ds(e, 1), :] = adj[x, h, pl.ds(y, 1), :]
        return carry

    lax.fori_loop(0, own_total, foot, 0)
    part = jnp.zeros((16, LANES), jnp.float32)
    for n in range(4):
        sums = DT * jnp.sum(sum_v[n], axis=1, keepdims=True)
        part = jnp.where(lanes[:16] - 8 * n == which_v[0:16, :], sums, part)
    sum_v[0] = part

    def post(e, carry):
        at = pl.ds(lax.shift_right_logical(list_s[3, e], 3), 1)
        msg_ref[at, :] += sum_v[0, pl.ds(e, 1), :]
        return carry

    lax.fori_loop(0, own_total, post, 0)


def gradient_kernel(ny, got_ref, own_ref, free_ref, out_ref):
    me = lax.axis_index("gx") * ny + lax.axis_index("gy")
    steps, owned = out_ref.shape
    total = jnp.sum(got_ref[...], axis=0, keepdims=True)
    flat = lax.broadcasted_iota(jnp.int32, own_ref.shape, 0) * LANES + lax.broadcasted_iota(
        jnp.int32, own_ref.shape, 1
    )
    listed = free_ref[...]
    column = lax.broadcasted_iota(jnp.int32, (steps, owned), 1)
    flags = jnp.zeros((steps, owned), jnp.float32)
    for k in range(owned):
        actuator = jnp.sum(jnp.where(own_ref[...] == me * owned + k, flat, 0))
        hit = jnp.max(jnp.where(listed == actuator, 1.0, 0.0), axis=1, keepdims=True)
        flags = jnp.where(column == k, hit, flags)
    for n in range(steps):
        out_ref[n : n + 1, :] = total[:, n * owned : (n + 1) * owned] * flags[n : n + 1, :]


VM = pl.BlockSpec(memory_space=pltpu.VMEM)
SM = pl.BlockSpec(memory_space=pltpu.SMEM)


def shards(
    checkpoint, terminal_adjoint, diffusivity, controls, owner_map, act_ids, slot_tiles, slot_count, free_list,
):
    cx, cy, cz = checkpoint.shape
    nx, ny = lax.axis_size("gx"), lax.axis_size("gy")
    ndev = nx * ny
    f32 = jnp.float32

    def shape(*dims):
        return jax.ShapeDtypeStruct(dims, f32)

    packed = pl.pallas_call(
        functools.partial(pack_kernel, cx, cy),
        out_shape=[shape(cx, 2, 16, LANES)] * 2
        + [shape(LAYERS, 2, cy, LANES)] * 2
        + [shape(2, CORNER_ROWS, LANES)] * 4
        + [shape(ndev, LANES)],
        in_specs=[VM] * 3 + [SM] * 5,
        out_specs=[VM] * 9,
        compiler_params=pltpu.CompilerParams(vmem_limit_bytes=32 << 20),
        name="pack",
    )(checkpoint, diffusivity, terminal_adjoint, controls, owner_map, act_ids, slot_tiles, slot_count)
    yup, ydn, xup, xdn, uu, ud, du, dd, row = packed

    def shift(value, a, b):
        pairs = [
            (i * ny + j, (i + a) * ny + j + b)
            for i in range(nx)
            for j in range(ny)
            if 0 <= i + a < nx and 0 <= j + b < ny
        ]
        return lax.ppermute(value, AXES, pairs)

    xup, xdn = shift(xup, 1, 0), shift(xdn, -1, 0)
    yup, ydn = shift(yup, 0, 1), shift(ydn, 0, -1)
    uu, ud, du, dd = shift(uu, 1, 1), shift(ud, 1, -1), shift(du, -1, 1), shift(dd, -1, -1)
    table = lax.all_to_all(row, AXES, 0, 0, tiled=True)

    ext = pltpu.VMEM((cx + 2 * XO, 2, YR, LANES), f32)
    start_adjoint, message = pl.pallas_call(
        functools.partial(window_kernel, cx, cy, nx, ny),
        out_shape=[shape(cx, cy, cz), shape(ndev, LANES)],
        in_specs=[VM] * 12,
        out_specs=[VM] * 2,
        scratch_shapes=[ext] * 11
        + [
            pltpu.VMEM((16, LANES), jnp.int32),
            pltpu.SMEM((16, LANES), jnp.int32),
            pltpu.SMEM((4, 160), jnp.int32),
            pltpu.VMEM((144, LANES), f32),
            pltpu.VMEM((144, LANES), jnp.int32),
            pltpu.VMEM((3, 144, LANES), f32),
            pltpu.VMEM((4, 16, LANES), f32),
            pltpu.SemaphoreType.DMA,
        ],
        compiler_params=pltpu.CompilerParams(vmem_limit_bytes=48 << 20),
        name="window",
    )(checkpoint, diffusivity, terminal_adjoint, yup, ydn, xup, xdn, uu, ud, du, dd, table)

    got = lax.all_to_all(message, AXES, 0, 0, tiled=True)
    gradient = pl.pallas_call(
        functools.partial(gradient_kernel, ny),
        out_shape=shape(*controls.shape),
        in_specs=[VM] * 3,
        out_specs=VM,
        name="gradient",
    )(got, owner_map.reshape(-1, LANES), free_list)
    return start_adjoint, gradient


def solution(mesh):
    placed = (
        P("gx", "gy", None),
        P("gx", "gy", None),
        P("gx", "gy", None),
        P(None, ("gx", "gy")),
        P(),
        P(("gx", "gy")),
        P(("gx", "gy")),
        P(("gx", "gy")),
        P(),
    )
    return jax.shard_map(
        shards,
        mesh=mesh,
        in_specs=placed,
        out_specs=(P("gx", "gy", None), P(None, ("gx", "gy"))),
        check_vma=False,
    )
```

```python
import functools

import jax
import jax.numpy as jnp
from jax import lax
from jax.experimental import pallas as pl
from jax.experimental.pallas import tpu as pltpu
from jax.sharding import PartitionSpec as P

TZ = 128
DT = 0.05
VEL = (1.0, 0.7, 0.4)
AXES = ("gx", "gy")

WIDE = (6, 5, 4)
LAYERS = sum(WIDE)
XO = 6
YO = 12
YR = 56
LANES = 128
GROUP = 32
CODE = 1024


def corner_pieces():
    pieces, row = [], 0
    for field, wide in enumerate(WIDE):
        for layer in range(1, wide):
            pieces.append((field, layer, wide - layer, row))
            row += wide - layer
    return pieces, -(-row // 8) * 8


CORNER, CORNER_ROWS = corner_pieces()


def table_rows(nx):
    return max(8, nx * GROUP // LANES)


def first_kernel(
    cx, cy, ck_ref, kp_ref, ta_ref, own_ref, ctl_ref, act_ref, til_ref, cnt_ref,
    yup_ref, ydn_ref, ids_ref, row_ref, low, high, own_s, sems,
):
    copies = [pltpu.make_async_copy(own_ref, own_s, sems.at[6])]
    for f, field in enumerate((ck_ref, kp_ref, ta_ref)):
        copies.append(pltpu.make_async_copy(field.at[:, 0:8, :], low.at[f], sems.at[2 * f]))
        copies.append(pltpu.make_async_copy(field.at[:, cy - 8 : cy, :], high.at[f], sems.at[2 * f + 1]))
    for copy in copies:
        copy.start()
    lane = lax.broadcasted_iota(jnp.int32, (1, LANES), 1)
    row = jnp.zeros((1, LANES), jnp.float32)
    steps, owned = ctl_ref.shape
    for n in range(steps):
        for k in range(owned):
            row = jnp.where(lane == n * owned + k, ctl_ref[n, k], row)
    row_ref[...] = jnp.broadcast_to(row, row_ref.shape)
    copies[0].wait()
    ids = jnp.zeros((1, LANES), jnp.int32)
    for j in range(act_ref.shape[0]):
        code = jnp.where(j < cnt_ref[0], own_s[act_ref[j]] * CODE + til_ref[j] + 1, 0)
        ids = jnp.where(lane == j, code, ids)
    ids = ids.astype(jnp.float32)
    ids_ref[...] = jnp.broadcast_to(ids, ids_ref.shape)
    for copy in copies[1:]:
        copy.wait()
    halves = (slice(0, LANES), slice(LANES, 2 * LANES))

    def rows(x, carry):
        at = 0
        for f, wide in enumerate(WIDE):
            for h in range(2):
                yup_ref[x, h, at : at + wide, :] = high[f, x, 8 - wide : 8, halves[h]]
                ydn_ref[x, h, at : at + wide, :] = low[f, x, 0:wide, halves[h]]
            at += wide
        return carry

    lax.fori_loop(0, cx, rows, 0)
    yup_ref[0, 0, LAYERS : LAYERS + 1, :] = ids
    ydn_ref[0, 0, LAYERS : LAYERS + 1, :] = ids


def second_kernel(
    cx, cy, nx, ny, ck_ref, kp_ref, ta_ref, yup_ref, ydn_ref, ids_ref, got_ref,
    xup_ref, xdn_ref, tab_ref, sems,
):
    copies = []
    at = 0
    for field, wide in zip((ck_ref, kp_ref, ta_ref), WIDE):
        for h in range(2):
            half = slice(h * LANES, (h + 1) * LANES)
            for ref, x in ((xup_ref, cx - wide), (xdn_ref, 0)):
                copies.append(
                    pltpu.make_async_copy(
                        field.at[x : x + wide, :, half], ref.at[at : at + wide, h], sems.at[len(copies)]
                    )
                )
        at += wide
    for copy in copies:
        copy.start()
    for f, layer, count, start in CORNER:
        top = sum(WIDE[: f + 1])
        at = top - WIDE[f]
        for ref, x in ((xup_ref, cx - layer), (xdn_ref, layer - 1)):
            for h in range(2):
                ref[LAYERS, h, start : start + count, :] = yup_ref[x, h, top - count : top, :]
                ref[LAYERS + 1, h, start : start + count, :] = ydn_ref[x, h, at : at + count, :]
    for ref in (xup_ref, xdn_ref):
        ref[LAYERS, 0, cy - 1 : cy, :] = ids_ref[0:1, :]
        ref[LAYERS, 1, cy - 1 : cy, :] = yup_ref[0, 0, LAYERS : LAYERS + 1, :]
        ref[LAYERS + 1, 0, cy - 1 : cy, :] = ydn_ref[0, 0, LAYERS : LAYERS + 1, :]
    rows = table_rows(nx)
    if nx < rows:
        for j in range(ny):
            tab_ref[j, 0:nx, :] = got_ref[...]
            tab_ref[j, nx:rows, :] = jnp.zeros((rows - nx, LANES), jnp.float32)
    else:
        lane = lax.broadcasted_iota(jnp.int32, (rows, LANES), 1)
        table = got_ref[0:rows, :]
        for g in range(1, nx // rows):
            part = pltpu.roll(got_ref[g * rows : (g + 1) * rows, :], g * GROUP, 1)
            table = jnp.where(lane < g * GROUP, table, part)
        tab_ref[...] = jnp.broadcast_to(table[None], tab_ref.shape)
    for copy in copies:
        copy.wait()


def window_kernel(
    cx, cy, nx, ny, ck_ref, kp_ref, ta_ref,
    yup_ref, ydn_ref, xup_ref, xdn_ref, ids_ref, tab_ref,
    out_ref, msg_ref,
    s0, s1, s2, s3, kap, a4, a3, a2, a1, qa, qb,
    near_v, near_s, list_s, pick_v, which_v, amp_v, sum_v, sem,
):
    gx = lax.axis_index("gx")
    gy = lax.axis_index("gy")
    halves = (slice(0, LANES), slice(LANES, 2 * LANES))
    lane = lax.broadcasted_iota(jnp.int32, (1, LANES), 1)

    spare = slice(LAYERS, LAYERS + 1)
    tail = slice(cy - 1, cy)
    near = (
        ((0, 0), ids_ref[0:1, :]),
        ((0, -1), yup_ref[0, 0, spare, :]),
        ((0, 1), ydn_ref[0, 0, spare, :]),
        ((-1, 0), xup_ref[LAYERS, 0, tail, :]),
        ((-1, -1), xup_ref[LAYERS, 1, tail, :]),
        ((-1, 1), xup_ref[LAYERS + 1, 0, tail, :]),
        ((1, 0), xdn_ref[LAYERS, 0, tail, :]),
        ((1, -1), xdn_ref[LAYERS, 1, tail, :]),
        ((1, 1), xdn_ref[LAYERS + 1, 0, tail, :]),
    )
    for i, (_, codes) in enumerate(near):
        near_v[i : i + 1, :] = codes.astype(jnp.int32) - 1
    ids = pltpu.make_async_copy(near_v, near_s, sem)
    ids.start()

    fields = ((ck_ref, s0), (kp_ref, kap), (ta_ref, a4))
    for f, (own, ext) in enumerate(fields):
        wide, at = WIDE[f], sum(WIDE[:f])

        def assemble(x, carry, own=own, ext=ext, wide=wide, at=at):
            for h in range(2):
                ext[XO + x, h, YO : YO + cy, :] = own[x, :, halves[h]]
                ext[XO + x, h, YO - wide : YO, :] = yup_ref[x, h, at : at + wide, :]
                ext[XO + x, h, YO + cy : YO + cy + wide, :] = ydn_ref[x, h, at : at + wide, :]
            return carry

        lax.fori_loop(0, cx, assemble, 0)
        for i in range(wide):
            for h in range(2):
                ext[XO - wide + i, h, YO : YO + cy, :] = xup_ref[at + i, h]
                ext[XO + cx + i, h, YO : YO + cy, :] = xdn_ref[at + i, h]
    for f, layer, count, start in CORNER:
        ext = fields[f][1]
        for ref, x in ((xup_ref, XO - layer), (xdn_ref, XO + cx + layer - 1)):
            for h in range(2):
                ext[x, h, YO - count : YO, :] = ref[LAYERS, h, start : start + count, :]
                ext[x, h, YO + cy : YO + cy + count, :] = ref[LAYERS + 1, h, start : start + count, :]

    ids.wait()
    total = jnp.int32(0)
    own_total = jnp.int32(0)
    for i, ((a, b), _) in enumerate(near):
        for j in range(16):
            code = near_s[i, j]
            place = lax.shift_right_arithmetic(code, 10)
            tile = code & (CODE - 1)
            x = lax.shift_right_logical(tile, 6) + (XO + a * cx)
            y = (lax.shift_right_logical(tile, 1) & (cy - 1)) + (YO + b * cy)
            keep = place >= 0
            if a != 0:
                keep &= (x >= XO - 5) & (x < XO + cx + 5)
            if b != 0:
                keep &= (y >= YO - 5) & (y < YO + cy + 5)
            list_s[0, total] = x
            list_s[1, total] = tile & 1
            list_s[2, total] = y
            list_s[3, total] = place
            total = total + keep.astype(jnp.int32)
        if i == 0:
            own_total = total

    rows = table_rows(nx)

    def pick(e, carry):
        place = list_s[3, e]
        owner = lax.shift_right_logical(place, 3)
        column, line = lax.rem(owner, ny), lax.div(owner, ny)
        at = column * rows + lax.rem(line, rows)
        pick_v[pl.ds(e, 1), :] = tab_ref[pl.ds(at, 1), :]
        which_v[pl.ds(e, 1), :] = jnp.broadcast_to(lax.div(line, rows) * GROUP + (place & 7), (1, LANES))
        return carry

    lax.fori_loop(0, total, pick, 0)
    lanes = lax.broadcasted_iota(jnp.int32, pick_v.shape, 1)
    for n in range(3):
        chosen = jnp.where(lanes - 8 * n == which_v[...], pick_v[...], 0.0)
        amp_v[n] = jnp.broadcast_to(DT * jnp.sum(chosen, axis=1, keepdims=True), pick_v.shape)

    lo_x, hi_x, lo_y, hi_y = gx == 0, gx == nx - 1, gy == 0, gy == ny - 1

    def clear_outside(ref):
        @pl.when(lo_x)
        def _():
            ref[XO - 1] = jnp.zeros(ref.shape[1:], jnp.float32)

        @pl.when(hi_x)
        def _():
            ref[XO + cx] = jnp.zeros(ref.shape[1:], jnp.float32)

        @pl.when(lo_y)
        def _():
            ref[:, :, YO - 1 : YO, :] = jnp.zeros((ref.shape[0], 2, 1, LANES), jnp.float32)

        @pl.when(hi_y)
        def _():
            ref[:, :, YO + cy : YO + cy + 1, :] = jnp.zeros((ref.shape[0], 2, 1, LANES), jnp.float32)

    def depth(v0, v1):
        first = lax.broadcasted_iota(jnp.int32, v0.shape, 1) == 0
        last = lax.broadcasted_iota(jnp.int32, v0.shape, 1) == LANES - 1
        f0, f1 = pltpu.roll(v0, 1, 1), pltpu.roll(v1, 1, 1)
        b0, b1 = pltpu.roll(v0, LANES - 1, 1), pltpu.roll(v1, LANES - 1, 1)
        before = (jnp.where(first, 0.0, f0), jnp.where(first, f0, f1))
        after = (jnp.where(last, b1, b0), jnp.where(last, 0.0, b1))
        return before, after

    def forward(src, dst, lo, hi, y0, rows):
        def plane(x, carry):
            mid = [src[x, h, pl.ds(y0, rows), :] for h in range(2)]
            before, after = depth(*mid)
            for h in range(2):
                f = mid[h]
                pairs = (
                    (src[x + 1, h, pl.ds(y0, rows), :], src[x - 1, h, pl.ds(y0, rows), :]),
                    (src[x, h, pl.ds(y0 + 1, rows), :], src[x, h, pl.ds(y0 - 1, rows), :]),
                    (after[h], before[h]),
                )
                lap, adv = -6.0 * f, 0.0
                for v, (p, m) in zip(VEL, pairs):
                    both = p + m
                    lap = lap + both
                    adv = adv + (0.25 * v) * (both * (p - m))
                kappa = kap[x, h, pl.ds(y0, rows), :]
                dst[x, h, pl.ds(y0, rows), :] = f + DT * (kappa * lap - adv)
            return carry

        lax.fori_loop(lo, hi, plane, 0)

    def actuate(n, dst):
        def one(e, carry):
            x, h, y = list_s[0, e], list_s[1, e], list_s[2, e]
            dst[x, h, pl.ds(y, 1), :] += amp_v[n, pl.ds(e, 1), :]
            return carry

        lax.fori_loop(0, total, one, 0)
        clear_outside(dst)

    forward(s0, s1, XO - 5, XO, 8, 40)
    forward(s0, s1, XO, XO + cx, 4, 48)
    forward(s0, s1, XO + cx, XO + cx + 5, 8, 40)
    actuate(0, s1)
    forward(s1, s2, XO - 4, XO + cx + 4, 8, 40)
    actuate(1, s2)
    forward(s2, s3, XO - 3, XO + cx + 3, 8, 40)
    actuate(2, s3)

    def scale(x, carry):
        for h in range(2):
            qa[x, h] = kap[x, h] * a4[x, h]
        return carry

    lax.fori_loop(XO - 4, XO + cx + 4, scale, 0)

    def step(adj, q, state, x, y0, rows):
        mid = [adj[x, h, pl.ds(y0, rows), :] for h in range(2)]
        qmid = [q[x, h, pl.ds(y0, rows), :] for h in range(2)]
        before, after = depth(*mid)
        qbefore, qafter = depth(*qmid)
        result = []
        for h in range(2):
            lap = (
                (q[x + 1, h, pl.ds(y0, rows), :] + q[x - 1, h, pl.ds(y0, rows), :])
                + (q[x, h, pl.ds(y0 + 1, rows), :] + q[x, h, pl.ds(y0 - 1, rows), :])
                + (qafter[h] + qbefore[h])
            ) - 6.0 * qmid[h]
            drift = (
                (0.5 * VEL[0]) * (adj[x + 1, h, pl.ds(y0, rows), :] - adj[x - 1, h, pl.ds(y0, rows), :])
                + (0.5 * VEL[1]) * (adj[x, h, pl.ds(y0 + 1, rows), :] - adj[x, h, pl.ds(y0 - 1, rows), :])
                + (0.5 * VEL[2]) * (after[h] - before[h])
            )
            result.append(mid[h] + DT * (lap + state[x, h, pl.ds(y0, rows), :] * drift))
        return result

    def backward(adj, q, state, dst, qdst, wide):
        def plane(x, carry):
            for h, value in enumerate(step(adj, q, state, x, 8, 40)):
                dst[x, h, pl.ds(8, 40), :] = value
                qdst[x, h, pl.ds(8, 40), :] = kap[x, h, pl.ds(8, 40), :] * value
            return carry

        lax.fori_loop(XO - wide, XO + cx + wide, plane, 0)
        clear_outside(dst)

    backward(a4, qa, s3, a3, qb, 3)
    backward(a3, qb, s2, a2, qa, 2)
    backward(a2, qa, s1, a1, qb, 1)

    def final(x, carry):
        for h, value in enumerate(step(a1, qb, s0, XO + x, YO, cy)):
            out_ref[x, :, halves[h]] = value
        return carry

    lax.fori_loop(0, cx, final, 0)

    msg_ref[...] = jnp.zeros(msg_ref.shape, jnp.float32)

    def foot(e, carry):
        x, h, y = list_s[0, e], list_s[1, e], list_s[2, e]
        for n, adj in enumerate((a1, a2, a3, a4)):
            sum_v[n, pl.ds(e, 1), :] = adj[x, h, pl.ds(y, 1), :]
        return carry

    lax.fori_loop(0, own_total, foot, 0)
    part = jnp.zeros((16, LANES), jnp.float32)
    for n in range(4):
        sums = DT * jnp.sum(sum_v[n], axis=1, keepdims=True)
        part = jnp.where(lanes[:16] - 8 * n == (which_v[0:16, :] & 7), sums, part)
    sum_v[0] = part

    def post(e, carry):
        at = pl.ds(lax.shift_right_logical(list_s[3, e], 3), 1)
        msg_ref[at, :] += sum_v[0, pl.ds(e, 1), :]
        return carry

    lax.fori_loop(0, own_total, post, 0)


def gradient_kernel(ny, got_ref, own_ref, free_ref, out_ref):
    me = lax.axis_index("gx") * ny + lax.axis_index("gy")
    steps, owned = out_ref.shape
    total = jnp.sum(got_ref[...], axis=0, keepdims=True)
    flat = lax.broadcasted_iota(jnp.int32, own_ref.shape, 0) * LANES + lax.broadcasted_iota(
        jnp.int32, own_ref.shape, 1
    )
    listed = free_ref[...]
    column = lax.broadcasted_iota(jnp.int32, (steps, owned), 1)
    flags = jnp.zeros((steps, owned), jnp.float32)
    for k in range(owned):
        actuator = jnp.sum(jnp.where(own_ref[...] == me * owned + k, flat, 0))
        hit = jnp.max(jnp.where(listed == actuator, 1.0, 0.0), axis=1, keepdims=True)
        flags = jnp.where(column == k, hit, flags)
    for n in range(steps):
        out_ref[n : n + 1, :] = total[:, n * owned : (n + 1) * owned] * flags[n : n + 1, :]


ANY = pl.BlockSpec(memory_space=pl.ANY)
VM = pl.BlockSpec(memory_space=pltpu.VMEM)
SM = pl.BlockSpec(memory_space=pltpu.SMEM)


def shards(
    checkpoint, terminal_adjoint, diffusivity, controls, owner_map, act_ids, slot_tiles, slot_count, free_list,
):
    cx, cy, cz = checkpoint.shape
    nx, ny = lax.axis_size("gx"), lax.axis_size("gy")
    ndev = nx * ny
    f32 = jnp.float32

    def shape(*dims):
        return jax.ShapeDtypeStruct(dims, f32)

    def shift(value, axis, way):
        size = lax.axis_size(axis)
        pairs = [(i, i + way) for i in range(size) if 0 <= i + way < size]
        return lax.ppermute(value, axis, pairs)

    fields = (checkpoint, diffusivity, terminal_adjoint)
    yup, ydn, ids, row = pl.pallas_call(
        functools.partial(first_kernel, cx, cy),
        out_shape=[shape(cx, 2, 16, LANES)] * 2 + [shape(8, LANES), shape(nx, LANES)],
        in_specs=[ANY] * 4 + [SM] * 4,
        out_specs=[VM] * 4,
        scratch_shapes=[
            pltpu.VMEM((3, cx, 8, cz), f32),
            pltpu.VMEM((3, cx, 8, cz), f32),
            pltpu.SMEM(owner_map.shape, jnp.int32),
            pltpu.SemaphoreType.DMA((7,)),
        ],
        compiler_params=pltpu.CompilerParams(vmem_limit_bytes=60 << 20),
        name="first",
    )(*fields, owner_map, controls, act_ids, slot_tiles, slot_count)
    yup, ydn = shift(yup, "gy", 1), shift(ydn, "gy", -1)
    got = lax.all_to_all(row, "gx", 0, 0, tiled=True)
    rows = table_rows(nx)
    xup, xdn, table = pl.pallas_call(
        functools.partial(second_kernel, cx, cy, nx, ny),
        out_shape=[shape(LAYERS + 2, 2, cy, LANES)] * 2 + [shape(ny, rows, LANES)],
        in_specs=[ANY] * 3 + [VM] * 4,
        out_specs=[VM] * 3,
        scratch_shapes=[pltpu.SemaphoreType.DMA((12,))],
        compiler_params=pltpu.CompilerParams(vmem_limit_bytes=32 << 20),
        name="second",
    )(*fields, yup, ydn, ids, got)
    xup, xdn = shift(xup, "gx", 1), shift(xdn, "gx", -1)
    table = lax.all_to_all(table, "gy", 0, 0, tiled=True).reshape(ny * rows, LANES)

    ext = pltpu.VMEM((cx + 2 * XO, 2, YR, LANES), f32)
    start_adjoint, message = pl.pallas_call(
        functools.partial(window_kernel, cx, cy, nx, ny),
        out_shape=[shape(cx, cy, cz), shape(ndev, LANES)],
        in_specs=[VM] * 9,
        out_specs=[VM] * 2,
        scratch_shapes=[ext] * 11
        + [
            pltpu.VMEM((16, LANES), jnp.int32),
            pltpu.SMEM((16, LANES), jnp.int32),
            pltpu.SMEM((4, 160), jnp.int32),
            pltpu.VMEM((144, LANES), f32),
            pltpu.VMEM((144, LANES), jnp.int32),
            pltpu.VMEM((3, 144, LANES), f32),
            pltpu.VMEM((4, 16, LANES), f32),
            pltpu.SemaphoreType.DMA,
        ],
        compiler_params=pltpu.CompilerParams(vmem_limit_bytes=48 << 20),
        name="window",
    )(*fields, yup, ydn, xup, xdn, ids, table)

    got = lax.all_to_all(message, AXES, 0, 0, tiled=True)
    gradient = pl.pallas_call(
        functools.partial(gradient_kernel, ny),
        out_shape=shape(*controls.shape),
        in_specs=[VM] * 3,
        out_specs=VM,
        name="gradient",
    )(got, owner_map.reshape(-1, LANES), free_list)
    return start_adjoint, gradient


def solution(mesh):
    placed = (
        P("gx", "gy", None),
        P("gx", "gy", None),
        P("gx", "gy", None),
        P(None, ("gx", "gy")),
        P(),
        P(("gx", "gy")),
        P(("gx", "gy")),
        P(("gx", "gy")),
        P(),
    )
    return jax.shard_map(
        shards,
        mesh=mesh,
        in_specs=placed,
        out_specs=(P("gx", "gy", None), P(None, ("gx", "gy"))),
        check_vma=False,
    )
```

```python
import functools

import jax
import jax.numpy as jnp
from jax import lax
from jax.experimental import pallas as pl
from jax.experimental.pallas import tpu as pltpu
from jax.sharding import PartitionSpec as P

TZ = 128
DT = 0.05
VEL = (1.0, 0.7, 0.4)
AXES = ("gx", "gy")

WIDE = (6, 5, 4)
LAYERS = sum(WIDE)
XO = 6
YO = 12
YR = 56
LANES = 128
GROUP = 32
BATCH = 4
CODE = 1024


def corner_pieces():
    pieces, row = [], 0
    for field, wide in enumerate(WIDE):
        for layer in range(1, wide):
            pieces.append((field, layer, wide - layer, row))
            row += wide - layer
    return pieces, -(-row // 8) * 8


CORNER, CORNER_ROWS = corner_pieces()


def table_rows(nx):
    return max(8, nx * GROUP // LANES)


def first_kernel(
    cx, cy, ck_ref, kp_ref, ta_ref, own_ref, ctl_ref, act_ref, til_ref, cnt_ref,
    yup_ref, ydn_ref, ids_ref, row_ref, low, high, own_s, sems,
):
    copies = [pltpu.make_async_copy(own_ref, own_s, sems.at[6])]
    for f, field in enumerate((ck_ref, kp_ref, ta_ref)):
        copies.append(pltpu.make_async_copy(field.at[:, 0:8, :], low.at[f], sems.at[2 * f]))
        copies.append(pltpu.make_async_copy(field.at[:, cy - 8 : cy, :], high.at[f], sems.at[2 * f + 1]))
    for copy in copies:
        copy.start()
    lane = lax.broadcasted_iota(jnp.int32, (1, LANES), 1)
    row = jnp.zeros((1, LANES), jnp.float32)
    steps, owned = ctl_ref.shape
    for n in range(steps):
        for k in range(owned):
            row = jnp.where(lane == n * owned + k, ctl_ref[n, k], row)
    row_ref[...] = jnp.broadcast_to(row, row_ref.shape)
    copies[0].wait()
    ids = jnp.zeros((1, LANES), jnp.int32)
    for j in range(act_ref.shape[0]):
        code = jnp.where(j < cnt_ref[0], own_s[act_ref[j]] * CODE + til_ref[j] + 1, 0)
        ids = jnp.where(lane == j, code, ids)
    ids = ids.astype(jnp.float32)
    ids_ref[...] = jnp.broadcast_to(ids, ids_ref.shape)
    for copy in copies[1:]:
        copy.wait()
    halves = (slice(0, LANES), slice(LANES, 2 * LANES))

    def rows(x, carry):
        at = 0
        for f, wide in enumerate(WIDE):
            for h in range(2):
                yup_ref[x, h, at : at + wide, :] = high[f, x, 8 - wide : 8, halves[h]]
                ydn_ref[x, h, at : at + wide, :] = low[f, x, 0:wide, halves[h]]
            at += wide
        return carry

    lax.fori_loop(0, cx, rows, 0, unroll=4)
    yup_ref[0, 0, LAYERS : LAYERS + 1, :] = ids
    ydn_ref[0, 0, LAYERS : LAYERS + 1, :] = ids


def second_kernel(
    cx, cy, nx, ny, ck_ref, kp_ref, ta_ref, yup_ref, ydn_ref, ids_ref, got_ref,
    xup_ref, xdn_ref, tab_ref, sems,
):
    copies = []
    at = 0
    for field, wide in zip((ck_ref, kp_ref, ta_ref), WIDE):
        for h in range(2):
            half = slice(h * LANES, (h + 1) * LANES)
            for ref, x in ((xup_ref, cx - wide), (xdn_ref, 0)):
                copies.append(
                    pltpu.make_async_copy(
                        field.at[x : x + wide, :, half], ref.at[at : at + wide, h], sems.at[len(copies)]
                    )
                )
        at += wide
    for copy in copies:
        copy.start()
    for f, layer, count, start in CORNER:
        top = sum(WIDE[: f + 1])
        at = top - WIDE[f]
        for ref, x in ((xup_ref, cx - layer), (xdn_ref, layer - 1)):
            for h in range(2):
                ref[LAYERS, h, start : start + count, :] = yup_ref[x, h, top - count : top, :]
                ref[LAYERS + 1, h, start : start + count, :] = ydn_ref[x, h, at : at + count, :]
    for ref in (xup_ref, xdn_ref):
        ref[LAYERS, 0, cy - 1 : cy, :] = ids_ref[0:1, :]
        ref[LAYERS, 1, cy - 1 : cy, :] = yup_ref[0, 0, LAYERS : LAYERS + 1, :]
        ref[LAYERS + 1, 0, cy - 1 : cy, :] = ydn_ref[0, 0, LAYERS : LAYERS + 1, :]
    rows = table_rows(nx)
    if nx < rows:
        for j in range(ny):
            tab_ref[j, 0:nx, :] = got_ref[...]
            tab_ref[j, nx:rows, :] = jnp.zeros((rows - nx, LANES), jnp.float32)
    else:
        lane = lax.broadcasted_iota(jnp.int32, (rows, LANES), 1)
        table = got_ref[0:rows, :]
        for g in range(1, nx // rows):
            part = pltpu.roll(got_ref[g * rows : (g + 1) * rows, :], g * GROUP, 1)
            table = jnp.where(lane < g * GROUP, table, part)
        tab_ref[...] = jnp.broadcast_to(table[None], tab_ref.shape)
    for copy in copies:
        copy.wait()


def window_kernel(
    cx, cy, nx, ny, ck_ref, kp_ref, ta_ref,
    yup_ref, ydn_ref, xup_ref, xdn_ref, ids_ref, tab_ref,
    out_ref, msg_ref,
    s0, s1, s2, s3, kap, a4, a3, a2, a1, qa, qb,
    near_v, near_s, list_s, pick_v, which_v, amp_v, sum_v, sem, res, out_sems,
):
    gx = lax.axis_index("gx")
    gy = lax.axis_index("gy")
    halves = (slice(0, LANES), slice(LANES, 2 * LANES))
    lane = lax.broadcasted_iota(jnp.int32, (1, LANES), 1)

    spare = slice(LAYERS, LAYERS + 1)
    tail = slice(cy - 1, cy)
    near = (
        ((0, 0), ids_ref[0:1, :]),
        ((0, -1), yup_ref[0, 0, spare, :]),
        ((0, 1), ydn_ref[0, 0, spare, :]),
        ((-1, 0), xup_ref[LAYERS, 0, tail, :]),
        ((-1, -1), xup_ref[LAYERS, 1, tail, :]),
        ((-1, 1), xup_ref[LAYERS + 1, 0, tail, :]),
        ((1, 0), xdn_ref[LAYERS, 0, tail, :]),
        ((1, -1), xdn_ref[LAYERS, 1, tail, :]),
        ((1, 1), xdn_ref[LAYERS + 1, 0, tail, :]),
    )
    for i, (_, codes) in enumerate(near):
        near_v[i : i + 1, :] = codes.astype(jnp.int32) - 1
    ids = pltpu.make_async_copy(near_v, near_s, sem)
    ids.start()

    fields = ((ck_ref, s0), (kp_ref, kap), (ta_ref, a4))
    for f, (own, ext) in enumerate(fields):
        wide, at = WIDE[f], sum(WIDE[:f])

        def take(value, f=f):
            return DT * value if f == 1 else value

        def assemble(x, carry, own=own, ext=ext, wide=wide, at=at, take=take):
            for h in range(2):
                ext[XO + x, h, YO : YO + cy, :] = take(own[x, :, halves[h]])
                ext[XO + x, h, YO - wide : YO, :] = take(yup_ref[x, h, at : at + wide, :])
                ext[XO + x, h, YO + cy : YO + cy + wide, :] = take(ydn_ref[x, h, at : at + wide, :])
            return carry

        lax.fori_loop(0, cx, assemble, 0, unroll=True)
        for i in range(wide):
            for h in range(2):
                ext[XO - wide + i, h, YO : YO + cy, :] = take(xup_ref[at + i, h])
                ext[XO + cx + i, h, YO : YO + cy, :] = take(xdn_ref[at + i, h])
        for c, layer, count, start in CORNER:
            if c != f:
                continue
            for ref, x in ((xup_ref, XO - layer), (xdn_ref, XO + cx + layer - 1)):
                for h in range(2):
                    ext[x, h, YO - count : YO, :] = take(ref[LAYERS, h, start : start + count, :])
                    ext[x, h, YO + cy : YO + cy + count, :] = take(ref[LAYERS + 1, h, start : start + count, :])

    ids.wait()
    total = jnp.int32(0)
    own_total = jnp.int32(0)
    for i, ((a, b), _) in enumerate(near):
        for j in range(16):
            code = near_s[i, j]
            place = lax.shift_right_arithmetic(code, 10)
            tile = code & (CODE - 1)
            x = lax.shift_right_logical(tile, 6) + (XO + a * cx)
            y = (lax.shift_right_logical(tile, 1) & (cy - 1)) + (YO + b * cy)
            keep = place >= 0
            if a != 0:
                keep &= (x >= XO - 5) & (x < XO + cx + 5)
            if b != 0:
                keep &= (y >= YO - 5) & (y < YO + cy + 5)
            list_s[0, total] = x
            list_s[1, total] = tile & 1
            list_s[2, total] = y
            list_s[3, total] = place
            total = total + keep.astype(jnp.int32)
        if i == 0:
            own_total = total
    for j in range(BATCH):
        for part in range(4):
            list_s[part, total + j] = 0
    batches = lax.div(total + BATCH - 1, BATCH)

    rows = table_rows(nx)

    def pick(batch, carry):
        for j in range(BATCH):
            pick_one(batch * BATCH + j)
        return carry

    def pick_one(e):
        place = list_s[3, e]
        owner = lax.shift_right_logical(place, 3)
        column, line = lax.rem(owner, ny), lax.div(owner, ny)
        at = column * rows + lax.rem(line, rows)
        pick_v[pl.ds(e, 1), :] = tab_ref[pl.ds(at, 1), :]
        which_v[pl.ds(e, 1), :] = jnp.broadcast_to(lax.div(line, rows) * GROUP + (place & 7), (1, LANES))

    lax.fori_loop(0, batches, pick, 0)
    lanes = lax.broadcasted_iota(jnp.int32, pick_v.shape, 1)
    for n in range(3):
        chosen = jnp.where(lanes - 8 * n == which_v[...], pick_v[...], 0.0)
        amp_v[n] = jnp.broadcast_to(DT * jnp.sum(chosen, axis=1, keepdims=True), pick_v.shape)

    lo_x, hi_x, lo_y, hi_y = gx == 0, gx == nx - 1, gy == 0, gy == ny - 1

    def clear_outside(ref):
        @pl.when(lo_x)
        def _():
            ref[XO - 1] = jnp.zeros(ref.shape[1:], jnp.float32)

        @pl.when(hi_x)
        def _():
            ref[XO + cx] = jnp.zeros(ref.shape[1:], jnp.float32)

        @pl.when(lo_y)
        def _():
            ref[:, :, YO - 1 : YO, :] = jnp.zeros((ref.shape[0], 2, 1, LANES), jnp.float32)

        @pl.when(hi_y)
        def _():
            ref[:, :, YO + cy : YO + cy + 1, :] = jnp.zeros((ref.shape[0], 2, 1, LANES), jnp.float32)

    first = lax.broadcasted_iota(jnp.int32, (8, LANES), 1) == 0
    last = lax.broadcasted_iota(jnp.int32, (8, LANES), 1) == LANES - 1

    def spread(ref, x, h, y, tiles, extra=0):
        return [ref[x, h, pl.ds(y + t, 8, stride=tiles), :] for t in range(-extra, tiles + extra)]

    def depth(v0, v1):
        f0, f1 = pltpu.roll(v0, 1, 1), pltpu.roll(v1, 1, 1)
        b0, b1 = pltpu.roll(v0, LANES - 1, 1), pltpu.roll(v1, LANES - 1, 1)
        before = (jnp.where(first, 0.0, f0), jnp.where(first, f0, f1))
        after = (jnp.where(last, b1, b0), jnp.where(last, 0.0, b1))
        return before, after

    def forward(src, dst, lo, hi, y, tiles):
        def plane(x, carry):
            mid = [spread(src, x, h, y, tiles, 1) for h in range(2)]
            nxt = [spread(src, x + 1, h, y, tiles) for h in range(2)]
            prv = [spread(src, x - 1, h, y, tiles) for h in range(2)]
            kappa = [spread(kap, x, h, y, tiles) for h in range(2)]
            for t in range(tiles):
                before, after = depth(mid[0][t + 1], mid[1][t + 1])
                for h in range(2):
                    f = mid[h][t + 1]
                    pairs = ((nxt[h][t], prv[h][t]), (mid[h][t + 2], mid[h][t]), (after[h], before[h]))
                    (sx, sy, sz), (dx, dy, dz) = zip(*[(p + m, p - m) for p, m in pairs])
                    lap = (sx + sy) + (sz - 6.0 * f)
                    adv = (0.25 * DT * VEL[0]) * (sx * dx) + ((0.25 * DT * VEL[1]) * (sy * dy) + (0.25 * DT * VEL[2]) * (sz * dz))
                    dst[x, h, pl.ds(y + t, 8, stride=tiles), :] = f + (kappa[h][t] * lap - adv)
            return carry

        lax.fori_loop(lo, hi, plane, 0, unroll=True)

    def actuate(n, dst):
        def some(batch, carry):
            for j in range(BATCH):
                e = batch * BATCH + j
                x, h, y = list_s[0, e], list_s[1, e], list_s[2, e]
                dst[x, h, pl.ds(y, 1), :] += amp_v[n, pl.ds(e, 1), :]
            return carry

        lax.fori_loop(0, batches, some, 0)
        clear_outside(dst)

    forward(s0, s1, XO - 5, XO, YO - 4, 5)
    forward(s0, s1, XO, XO + cx, YO - 5, 6)
    forward(s0, s1, XO + cx, XO + cx + 5, YO - 4, 5)
    actuate(0, s1)
    forward(s1, s2, XO - 4, XO + cx + 4, YO - 4, 5)
    actuate(1, s2)
    forward(s2, s3, XO - 3, XO + cx + 3, YO - 3, 5)
    actuate(2, s3)

    def scale(x, carry):
        for h in range(2):
            qa[x, h] = kap[x, h] * a4[x, h]
        return carry

    lax.fori_loop(XO - 4, XO + cx + 4, scale, 0, unroll=True)

    def step(adj, q, state, x, y, tiles, emit):
        mid = [spread(adj, x, h, y, tiles, 1) for h in range(2)]
        qmid = [spread(q, x, h, y, tiles, 1) for h in range(2)]
        for t in range(tiles):
            before, after = depth(mid[0][t + 1], mid[1][t + 1])
            qbefore, qafter = depth(qmid[0][t + 1], qmid[1][t + 1])
            for h in range(2):
                at = pl.ds(y + t, 8, stride=tiles)
                lap = (
                    (q[x + 1, h, at, :] + q[x - 1, h, at, :])
                    + (qmid[h][t + 2] + qmid[h][t])
                    + ((qafter[h] + qbefore[h]) - 6.0 * qmid[h][t + 1])
                )
                drift = (
                    (0.5 * DT * VEL[0]) * (adj[x + 1, h, at, :] - adj[x - 1, h, at, :])
                    + (0.5 * DT * VEL[1]) * (mid[h][t + 2] - mid[h][t])
                    + (0.5 * DT * VEL[2]) * (after[h] - before[h])
                )
                emit(h, t, at, mid[h][t + 1] + (lap + state[x, h, at, :] * drift))

    def backward(adj, q, state, dst, qdst, wide):
        y = YO - wide

        def plane(x, carry):
            def emit(h, t, at, value):
                dst[x, h, at, :] = value
                qdst[x, h, at, :] = kap[x, h, at, :] * value

            step(adj, q, state, x, y, 5, emit)
            return carry

        lax.fori_loop(XO - wide, XO + cx + wide, plane, 0, unroll=True)
        clear_outside(dst)

    backward(a4, qa, s3, a3, qb, 3)
    backward(a3, qb, s2, a2, qa, 2)
    backward(a2, qa, s1, a1, qb, 1)

    def final(x, carry):
        def emit(h, t, at, value):
            res[x, h, pl.ds(t, 8, stride=cy // 8), :] = value

        step(a1, qb, s0, XO + x, YO, cy // 8, emit)
        return carry

    lax.fori_loop(0, cx, final, 0, unroll=True)
    writes = [pltpu.make_async_copy(res.at[:, h], out_ref.at[:, :, halves[h]], out_sems.at[h]) for h in range(2)]
    for write in writes:
        write.start()

    msg_ref[...] = jnp.zeros(msg_ref.shape, jnp.float32)

    def foot(e, carry):
        x, h, y = list_s[0, e], list_s[1, e], list_s[2, e]
        for n, adj in enumerate((a1, a2, a3, a4)):
            sum_v[n, pl.ds(e, 1), :] = adj[x, h, pl.ds(y, 1), :]
        return carry

    lax.fori_loop(0, own_total, foot, 0)
    part = jnp.zeros((16, LANES), jnp.float32)
    for n in range(4):
        sums = DT * jnp.sum(sum_v[n], axis=1, keepdims=True)
        part = jnp.where(lanes[:16] - 8 * n == (which_v[0:16, :] & 7), sums, part)
    sum_v[0] = part

    def post(e, carry):
        at = pl.ds(lax.shift_right_logical(list_s[3, e], 3), 1)
        msg_ref[at, :] += sum_v[0, pl.ds(e, 1), :]
        return carry

    lax.fori_loop(0, own_total, post, 0)
    for write in writes:
        write.wait()


def gradient_kernel(ny, got_ref, own_ref, free_ref, out_ref):
    me = lax.axis_index("gx") * ny + lax.axis_index("gy")
    steps, owned = out_ref.shape
    total = jnp.sum(got_ref[...], axis=0, keepdims=True)
    flat = lax.broadcasted_iota(jnp.int32, own_ref.shape, 0) * LANES + lax.broadcasted_iota(
        jnp.int32, own_ref.shape, 1
    )
    listed = free_ref[...]
    column = lax.broadcasted_iota(jnp.int32, (steps, owned), 1)
    flags = jnp.zeros((steps, owned), jnp.float32)
    for k in range(owned):
        actuator = jnp.sum(jnp.where(own_ref[...] == me * owned + k, flat, 0))
        hit = jnp.max(jnp.where(listed == actuator, 1.0, 0.0), axis=1, keepdims=True)
        flags = jnp.where(column == k, hit, flags)
    for n in range(steps):
        out_ref[n : n + 1, :] = total[:, n * owned : (n + 1) * owned] * flags[n : n + 1, :]


ANY = pl.BlockSpec(memory_space=pl.ANY)
VM = pl.BlockSpec(memory_space=pltpu.VMEM)
SM = pl.BlockSpec(memory_space=pltpu.SMEM)


def shards(
    checkpoint, terminal_adjoint, diffusivity, controls, owner_map, act_ids, slot_tiles, slot_count, free_list,
):
    cx, cy, cz = checkpoint.shape
    nx, ny = lax.axis_size("gx"), lax.axis_size("gy")
    ndev = nx * ny
    f32 = jnp.float32

    def shape(*dims):
        return jax.ShapeDtypeStruct(dims, f32)

    def shift(value, axis, way):
        size = lax.axis_size(axis)
        pairs = [(i, i + way) for i in range(size) if 0 <= i + way < size]
        return lax.ppermute(value, axis, pairs)

    fields = (checkpoint, diffusivity, terminal_adjoint)
    yup, ydn, ids, row = pl.pallas_call(
        functools.partial(first_kernel, cx, cy),
        out_shape=[shape(cx, 2, 16, LANES)] * 2 + [shape(8, LANES), shape(nx, LANES)],
        in_specs=[ANY] * 4 + [SM] * 4,
        out_specs=[VM] * 4,
        scratch_shapes=[
            pltpu.VMEM((3, cx, 8, cz), f32),
            pltpu.VMEM((3, cx, 8, cz), f32),
            pltpu.SMEM(owner_map.shape, jnp.int32),
            pltpu.SemaphoreType.DMA((7,)),
        ],
        compiler_params=pltpu.CompilerParams(vmem_limit_bytes=60 << 20),
        name="first",
    )(*fields, owner_map, controls, act_ids, slot_tiles, slot_count)
    yup, ydn = shift(yup, "gy", 1), shift(ydn, "gy", -1)
    got = lax.all_to_all(row, "gx", 0, 0, tiled=True)
    rows = table_rows(nx)
    xup, xdn, table = pl.pallas_call(
        functools.partial(second_kernel, cx, cy, nx, ny),
        out_shape=[shape(LAYERS + 2, 2, cy, LANES)] * 2 + [shape(ny, rows, LANES)],
        in_specs=[ANY] * 3 + [VM] * 4,
        out_specs=[VM] * 3,
        scratch_shapes=[pltpu.SemaphoreType.DMA((12,))],
        compiler_params=pltpu.CompilerParams(vmem_limit_bytes=32 << 20),
        name="second",
    )(*fields, yup, ydn, ids, got)
    xup, xdn = shift(xup, "gx", 1), shift(xdn, "gx", -1)
    table = lax.all_to_all(table, "gy", 0, 0, tiled=True).reshape(ny * rows, LANES)

    ext = pltpu.VMEM((cx + 2 * XO, 2, YR, LANES), f32)
    start_adjoint, message = pl.pallas_call(
        functools.partial(window_kernel, cx, cy, nx, ny),
        out_shape=[shape(cx, cy, cz), shape(ndev, LANES)],
        in_specs=[VM] * 9,
        out_specs=[ANY, VM],
        scratch_shapes=[ext] * 11
        + [
            pltpu.VMEM((16, LANES), jnp.int32),
            pltpu.SMEM((16, LANES), jnp.int32),
            pltpu.SMEM((4, 160), jnp.int32),
            pltpu.VMEM((152, LANES), f32),
            pltpu.VMEM((152, LANES), jnp.int32),
            pltpu.VMEM((3, 152, LANES), f32),
            pltpu.VMEM((4, 16, LANES), f32),
            pltpu.SemaphoreType.DMA,
            pltpu.VMEM((cx, 2, cy, LANES), f32),
            pltpu.SemaphoreType.DMA((2,)),
        ],
        compiler_params=pltpu.CompilerParams(vmem_limit_bytes=48 << 20),
        name="window",
    )(*fields, yup, ydn, xup, xdn, ids, table)

    got = lax.all_to_all(message, AXES, 0, 0, tiled=True)
    gradient = pl.pallas_call(
        functools.partial(gradient_kernel, ny),
        out_shape=shape(*controls.shape),
        in_specs=[VM] * 3,
        out_specs=VM,
        name="gradient",
    )(got, owner_map.reshape(-1, LANES), free_list)
    return start_adjoint, gradient


def solution(mesh):
    placed = (
        P("gx", "gy", None),
        P("gx", "gy", None),
        P("gx", "gy", None),
        P(None, ("gx", "gy")),
        P(),
        P(("gx", "gy")),
        P(("gx", "gy")),
        P(("gx", "gy")),
        P(),
    )
    return jax.shard_map(
        shards,
        mesh=mesh,
        in_specs=placed,
        out_specs=(P("gx", "gy", None), P(None, ("gx", "gy"))),
        check_vma=False,
    )
```

```python
import functools

import jax
import jax.numpy as jnp
from jax import lax
from jax.experimental import pallas as pl
from jax.experimental.pallas import tpu as pltpu
from jax.sharding import PartitionSpec as P

TZ = 128
DT = 0.05
VEL = (1.0, 0.7, 0.4)
AXES = ("gx", "gy")

WIDE = (6, 5, 4)
LAYERS = sum(WIDE)
XO = 6
YO = 12
YR = 56
LANES = 128
ROW = 32
LISTED = 160
BATCH = 4
CODE = 1024


def corner_pieces():
    pieces, row = [], 0
    for field, wide in enumerate(WIDE):
        for layer in range(1, wide):
            pieces.append((field, layer, wide - layer, row))
            row += wide - layer
    return pieces, -(-row // 8) * 8


CORNER, CORNER_ROWS = corner_pieces()


def first_kernel(
    cx, cy, ck_ref, kp_ref, ta_ref, own_ref, act_ref, til_ref, cnt_ref,
    yup_ref, ydn_ref, xup_ref, xdn_ref, ids_ref, low, high, own_s, sems, plane_sems,
):
    planes = []
    at = 0
    for field, wide in zip((ck_ref, kp_ref, ta_ref), WIDE):
        for h in range(2):
            half = slice(h * LANES, (h + 1) * LANES)
            for ref, x in ((xup_ref, cx - wide), (xdn_ref, 0)):
                planes.append(
                    pltpu.make_async_copy(
                        field.at[x : x + wide, :, half], ref.at[at : at + wide, h], plane_sems.at[len(planes)]
                    )
                )
        at += wide
    copies = [pltpu.make_async_copy(own_ref, own_s, sems.at[6])]
    for f, field in enumerate((ck_ref, kp_ref, ta_ref)):
        copies.append(pltpu.make_async_copy(field.at[:, 0:8, :], low.at[f], sems.at[2 * f]))
        copies.append(pltpu.make_async_copy(field.at[:, cy - 8 : cy, :], high.at[f], sems.at[2 * f + 1]))
    for copy in copies + planes:
        copy.start()
    lane = lax.broadcasted_iota(jnp.int32, (1, LANES), 1)
    copies[0].wait()
    ids = jnp.zeros((1, LANES), jnp.int32)
    for j in range(act_ref.shape[0]):
        code = jnp.where(j < cnt_ref[0], own_s[act_ref[j]] * CODE + til_ref[j] + 1, 0)
        ids = jnp.where(lane == j, code, ids)
    ids = ids.astype(jnp.float32)
    ids_ref[...] = jnp.broadcast_to(ids, ids_ref.shape)
    for copy in copies[1:]:
        copy.wait()
    halves = (slice(0, LANES), slice(LANES, 2 * LANES))

    def rows(x, carry):
        at = 0
        for f, wide in enumerate(WIDE):
            for h in range(2):
                yup_ref[x, h, at : at + wide, :] = high[f, x, 8 - wide : 8, halves[h]]
                ydn_ref[x, h, at : at + wide, :] = low[f, x, 0:wide, halves[h]]
            at += wide
        return carry

    lax.fori_loop(0, cx, rows, 0, unroll=4)
    yup_ref[0, 0, LAYERS : LAYERS + 1, :] = ids
    ydn_ref[0, 0, LAYERS : LAYERS + 1, :] = ids
    for copy in planes:
        copy.wait()


def row_kernel(ctl_ref, ids_ref, row_ref):
    lane = lax.broadcasted_iota(jnp.int32, (1, ROW), 1)
    row = ids_ref[0:1, 0:ROW]
    steps, owned = ctl_ref.shape
    for n in range(steps):
        for k in range(owned):
            row = jnp.where(lane == n * owned + k, ctl_ref[n, k], row)
    row_ref[...] = jnp.broadcast_to(row, row_ref.shape)


def corner_kernel(cx, cy, yup_ref, ydn_ref, ids_ref, up_ref, dn_ref):
    for f, layer, count, start in CORNER:
        top = sum(WIDE[: f + 1])
        at = top - WIDE[f]
        for ref, x in ((up_ref, cx - layer), (dn_ref, layer - 1)):
            for h in range(2):
                ref[0, h, start : start + count, :] = yup_ref[x, h, top - count : top, :]
                ref[1, h, start : start + count, :] = ydn_ref[x, h, at : at + count, :]
    tail = slice(CORNER_ROWS - 1, CORNER_ROWS)
    for ref in (up_ref, dn_ref):
        ref[0, 0, tail, :] = ids_ref[0:1, :]
        ref[0, 1, tail, :] = yup_ref[0, 0, LAYERS : LAYERS + 1, :]
        ref[1, 0, tail, :] = ydn_ref[0, 0, LAYERS : LAYERS + 1, :]


def ends():
    lane = lax.broadcasted_iota(jnp.int32, (8, LANES), 1)
    return lane == 0, lane == LANES - 1


def spread(ref, x, h, y, tiles, extra=0):
    return [ref[x, h, pl.ds(y + t, 8, stride=tiles), :] for t in range(-extra, tiles + extra)]


def depth(v0, v1):
    first, last = ends()
    f0, f1 = pltpu.roll(v0, 1, 1), pltpu.roll(v1, 1, 1)
    b0, b1 = pltpu.roll(v0, LANES - 1, 1), pltpu.roll(v1, LANES - 1, 1)
    before = (jnp.where(first, 0.0, f0), jnp.where(first, f0, f1))
    after = (jnp.where(last, b1, b0), jnp.where(last, 0.0, b1))
    return before, after


def forward(src, dst, kap, lo, hi, y, tiles):
    def plane(x, carry):
        mid = [spread(src, x, h, y, tiles, 1) for h in range(2)]
        nxt = [spread(src, x + 1, h, y, tiles) for h in range(2)]
        prv = [spread(src, x - 1, h, y, tiles) for h in range(2)]
        kappa = [spread(kap, x, h, y, tiles) for h in range(2)]
        for t in range(tiles):
            before, after = depth(mid[0][t + 1], mid[1][t + 1])
            for h in range(2):
                f = mid[h][t + 1]
                pairs = ((nxt[h][t], prv[h][t]), (mid[h][t + 2], mid[h][t]), (after[h], before[h]))
                (sx, sy, sz), (dx, dy, dz) = zip(*[(p + m, p - m) for p, m in pairs])
                lap = (sx + sy) + (sz - 6.0 * f)
                adv = (0.25 * DT * VEL[0]) * (sx * dx) + ((0.25 * DT * VEL[1]) * (sy * dy) + (0.25 * DT * VEL[2]) * (sz * dz))
                dst[x, h, pl.ds(y + t, 8, stride=tiles), :] = f + (kappa[h][t] * lap - adv)
        return carry

    lax.fori_loop(lo, hi, plane, 0, unroll=True)


def step(adj, q, state, x, y, tiles, emit):
    mid = [spread(adj, x, h, y, tiles, 1) for h in range(2)]
    qmid = [spread(q, x, h, y, tiles, 1) for h in range(2)]
    for t in range(tiles):
        before, after = depth(mid[0][t + 1], mid[1][t + 1])
        qbefore, qafter = depth(qmid[0][t + 1], qmid[1][t + 1])
        for h in range(2):
            at = pl.ds(y + t, 8, stride=tiles)
            lap = (
                (q[x + 1, h, at, :] + q[x - 1, h, at, :])
                + (qmid[h][t + 2] + qmid[h][t])
                + ((qafter[h] + qbefore[h]) - 6.0 * qmid[h][t + 1])
            )
            drift = (
                (0.5 * DT * VEL[0]) * (adj[x + 1, h, at, :] - adj[x - 1, h, at, :])
                + (0.5 * DT * VEL[1]) * (mid[h][t + 2] - mid[h][t])
                + (0.5 * DT * VEL[2]) * (after[h] - before[h])
            )
            emit(h, t, at, mid[h][t + 1] + (lap + state[x, h, at, :] * drift))


def assemble_kernel(
    cx, cy, nx, ny, ck_ref, kp_ref, ta_ref,
    yup_ref, ydn_ref, xup_ref, xdn_ref, cup_ref, cdn_ref, ids_ref,
    s0, s1, kap, a4, qa, list_s, near_v, near_s, sem,
):
    halves = (slice(0, LANES), slice(LANES, 2 * LANES))

    spare = slice(LAYERS, LAYERS + 1)
    tail = slice(CORNER_ROWS - 1, CORNER_ROWS)
    near = (
        ((0, 0), ids_ref[0:1, :]),
        ((0, -1), yup_ref[0, 0, spare, :]),
        ((0, 1), ydn_ref[0, 0, spare, :]),
        ((-1, 0), cup_ref[0, 0, tail, :]),
        ((-1, -1), cup_ref[0, 1, tail, :]),
        ((-1, 1), cup_ref[1, 0, tail, :]),
        ((1, 0), cdn_ref[0, 0, tail, :]),
        ((1, -1), cdn_ref[0, 1, tail, :]),
        ((1, 1), cdn_ref[1, 0, tail, :]),
    )
    for i, (_, codes) in enumerate(near):
        near_v[i : i + 1, :] = codes.astype(jnp.int32) - 1
    ids = pltpu.make_async_copy(near_v, near_s, sem)
    ids.start()

    fields = ((ck_ref, s0), (kp_ref, kap), (ta_ref, a4))
    for f, (own, ext) in enumerate(fields):
        wide, at = WIDE[f], sum(WIDE[:f])

        def take(value, f=f):
            return DT * value if f == 1 else value

        def assemble(x, carry, own=own, ext=ext, wide=wide, at=at, take=take):
            for h in range(2):
                ext[XO + x, h, YO : YO + cy, :] = take(own[x, :, halves[h]])
                ext[XO + x, h, YO - wide : YO, :] = take(yup_ref[x, h, at : at + wide, :])
                ext[XO + x, h, YO + cy : YO + cy + wide, :] = take(ydn_ref[x, h, at : at + wide, :])
            return carry

        lax.fori_loop(0, cx, assemble, 0, unroll=True)
        for i in range(wide):
            for h in range(2):
                ext[XO - wide + i, h, YO : YO + cy, :] = take(xup_ref[at + i, h])
                ext[XO + cx + i, h, YO : YO + cy, :] = take(xdn_ref[at + i, h])
        for c, layer, count, start in CORNER:
            if c != f:
                continue
            for ref, x in ((cup_ref, XO - layer), (cdn_ref, XO + cx + layer - 1)):
                for h in range(2):
                    ext[x, h, YO - count : YO, :] = take(ref[0, h, start : start + count, :])
                    ext[x, h, YO + cy : YO + cy + count, :] = take(ref[1, h, start : start + count, :])

    ids.wait()
    total = jnp.int32(0)
    own_total = jnp.int32(0)
    for i, ((a, b), _) in enumerate(near):
        for j in range(16):
            code = near_s[i, j]
            place = lax.shift_right_arithmetic(code, 10)
            tile = code & (CODE - 1)
            x = lax.shift_right_logical(tile, 6) + (XO + a * cx)
            y = (lax.shift_right_logical(tile, 1) & (cy - 1)) + (YO + b * cy)
            keep = place >= 0
            if a != 0:
                keep &= (x >= XO - 5) & (x < XO + cx + 5)
            if b != 0:
                keep &= (y >= YO - 5) & (y < YO + cy + 5)
            list_s[0, total] = x
            list_s[1, total] = tile & 1
            list_s[2, total] = y
            list_s[3, total] = place
            total = total + keep.astype(jnp.int32)
        if i == 0:
            own_total = total
    for j in range(BATCH):
        for part in range(4):
            list_s[part, total + j] = 0
    list_s[0, LISTED] = total
    list_s[1, LISTED] = own_total

    forward(s0, s1, kap, XO - 5, XO, YO - 4, 5)
    forward(s0, s1, kap, XO, XO + cx, YO - 5, 6)
    forward(s0, s1, kap, XO + cx, XO + cx + 5, YO - 4, 5)

    def scale(x, carry):
        for h in range(2):
            qa[x, h] = kap[x, h] * a4[x, h]
        return carry

    lax.fori_loop(XO - 4, XO + cx + 4, scale, 0, unroll=True)


def window_kernel(
    cx, cy, nx, ny, s0, s1_ref, kap, a4, qa_ref, tab_ref, list_s,
    a1, qb, msg_ref, s1, s2, s3, a3, a2, qa, pick_v, which_v, amp_v, sum_v,
):
    gx = lax.axis_index("gx")
    gy = lax.axis_index("gy")
    total, own_total = list_s[0, LISTED], list_s[1, LISTED]
    batches = lax.div(total + BATCH - 1, BATCH)

    def pick(batch, carry):
        for j in range(BATCH):
            pick_one(batch * BATCH + j)
        return carry

    def pick_one(e):
        place = list_s[3, e]
        pick_v[pl.ds(e, 1), :] = tab_ref[pl.ds(lax.shift_right_logical(place, 3), 1), :]
        which_v[pl.ds(e, 1), :] = jnp.broadcast_to(place & 7, (1, ROW))

    lax.fori_loop(0, batches, pick, 0)
    lanes = lax.broadcasted_iota(jnp.int32, pick_v.shape, 1)
    for n in range(3):
        chosen = jnp.where(lanes - 8 * n == which_v[...], pick_v[...], 0.0)
        amp_v[n] = jnp.broadcast_to(DT * jnp.sum(chosen, axis=1, keepdims=True), amp_v.shape[1:])

    lo_x, hi_x, lo_y, hi_y = gx == 0, gx == nx - 1, gy == 0, gy == ny - 1

    def clear_outside(ref):
        @pl.when(lo_x)
        def _():
            ref[XO - 1] = jnp.zeros(ref.shape[1:], jnp.float32)

        @pl.when(hi_x)
        def _():
            ref[XO + cx] = jnp.zeros(ref.shape[1:], jnp.float32)

        @pl.when(lo_y)
        def _():
            ref[:, :, YO - 1 : YO, :] = jnp.zeros((ref.shape[0], 2, 1, LANES), jnp.float32)

        @pl.when(hi_y)
        def _():
            ref[:, :, YO + cy : YO + cy + 1, :] = jnp.zeros((ref.shape[0], 2, 1, LANES), jnp.float32)

    def actuate(n, dst):
        def some(batch, carry):
            for j in range(BATCH):
                e = batch * BATCH + j
                x, h, y = list_s[0, e], list_s[1, e], list_s[2, e]
                dst[x, h, pl.ds(y, 1), :] += amp_v[n, pl.ds(e, 1), :]
            return carry

        lax.fori_loop(0, batches, some, 0)
        clear_outside(dst)

    for x in range(XO - 5, XO + cx + 5):
        s1[x] = s1_ref[x]
    actuate(0, s1)
    forward(s1, s2, kap, XO - 4, XO + cx + 4, YO - 4, 5)
    actuate(1, s2)
    forward(s2, s3, kap, XO - 3, XO + cx + 3, YO - 3, 5)
    actuate(2, s3)

    def backward(adj, q, state, dst, qdst, wide):
        y = YO - wide

        def plane(x, carry):
            def emit(h, t, at, value):
                dst[x, h, at, :] = value
                qdst[x, h, at, :] = kap[x, h, at, :] * value

            step(adj, q, state, x, y, 5, emit)
            return carry

        lax.fori_loop(XO - wide, XO + cx + wide, plane, 0, unroll=True)
        clear_outside(dst)

    backward(a4, qa_ref, s3, a3, qb, 3)
    backward(a3, qb, s2, a2, qa, 2)
    backward(a2, qa, s1, a1, qb, 1)

    msg_ref[...] = jnp.zeros(msg_ref.shape, jnp.float32)

    def foot(e, carry):
        x, h, y = list_s[0, e], list_s[1, e], list_s[2, e]
        for n, adj in enumerate((a1, a2, a3, a4)):
            sum_v[n, pl.ds(e, 1), :] = adj[x, h, pl.ds(y, 1), :]
        return carry

    lax.fori_loop(0, own_total, foot, 0)
    part = jnp.zeros((16, ROW), jnp.float32)
    for n in range(4):
        sums = DT * jnp.sum(sum_v[n], axis=1, keepdims=True)
        part = jnp.where(lanes[:16] - 8 * n == which_v[0:16, :], sums, part)
    sum_v[0, :, 0:ROW] = part

    def post(e, carry):
        at = pl.ds(lax.shift_right_logical(list_s[3, e], 3), 1)
        msg_ref[at, :] += sum_v[0, pl.ds(e, 1), 0:ROW]
        return carry

    lax.fori_loop(0, own_total, post, 0)


def final_kernel(cx, cy, ny, a1, qb, s0, own_ref, free_ref, out_ref, flag_ref, res, out_sems):
    def final(x, carry):
        def emit(h, t, at, value):
            res[x, h, pl.ds(t, 8, stride=cy // 8), :] = value

        step(a1, qb, s0, XO + x, YO, cy // 8, emit)
        return carry

    lax.fori_loop(0, cx, final, 0, unroll=True)
    halves = (slice(0, LANES), slice(LANES, 2 * LANES))
    writes = [pltpu.make_async_copy(res.at[:, h], out_ref.at[:, :, halves[h]], out_sems.at[h]) for h in range(2)]
    for write in writes:
        write.start()
    me = lax.axis_index("gx") * ny + lax.axis_index("gy")
    steps, owned = flag_ref.shape
    flat = lax.broadcasted_iota(jnp.int32, own_ref.shape, 0) * LANES + lax.broadcasted_iota(
        jnp.int32, own_ref.shape, 1
    )
    listed = free_ref[...]
    column = lax.broadcasted_iota(jnp.int32, (steps, owned), 1)
    flags = jnp.zeros((steps, owned), jnp.float32)
    for k in range(owned):
        actuator = jnp.sum(jnp.where(own_ref[...] == me * owned + k, flat, 0))
        hit = jnp.max(jnp.where(listed == actuator, 1.0, 0.0), axis=1, keepdims=True)
        flags = jnp.where(column == k, hit, flags)
    flag_ref[...] = flags
    for write in writes:
        write.wait()


def gradient_kernel(got_ref, flag_ref, out_ref):
    steps, owned = out_ref.shape
    total = jnp.sum(got_ref[...], axis=0, keepdims=True)
    for n in range(steps):
        out_ref[n : n + 1, :] = total[:, n * owned : (n + 1) * owned] * flag_ref[n : n + 1, :]


ANY = pl.BlockSpec(memory_space=pl.ANY)
VM = pl.BlockSpec(memory_space=pltpu.VMEM)
SM = pl.BlockSpec(memory_space=pltpu.SMEM)


def shards(
    checkpoint, terminal_adjoint, diffusivity, controls, owner_map, act_ids, slot_tiles, slot_count, free_list,
):
    cx, cy, cz = checkpoint.shape
    nx, ny = lax.axis_size("gx"), lax.axis_size("gy")
    ndev = nx * ny
    f32 = jnp.float32

    def shape(*dims):
        return jax.ShapeDtypeStruct(dims, f32)

    def shift(value, axis, way):
        size = lax.axis_size(axis)
        pairs = [(i, i + way) for i in range(size) if 0 <= i + way < size]
        return lax.ppermute(value, axis, pairs)

    fields = (checkpoint, diffusivity, terminal_adjoint)
    yup, ydn, xup, xdn, ids = pl.pallas_call(
        functools.partial(first_kernel, cx, cy),
        out_shape=[shape(cx, 2, 16, LANES)] * 2 + [shape(LAYERS, 2, cy, LANES)] * 2 + [shape(8, LANES)],
        in_specs=[ANY] * 4 + [SM] * 3,
        out_specs=[VM] * 5,
        scratch_shapes=[
            pltpu.VMEM((3, cx, 8, cz), f32),
            pltpu.VMEM((3, cx, 8, cz), f32),
            pltpu.SMEM(owner_map.shape, jnp.int32),
            pltpu.SemaphoreType.DMA((7,)),
            pltpu.SemaphoreType.DMA((12,)),
        ],
        compiler_params=pltpu.CompilerParams(vmem_limit_bytes=36 << 20),
        name="first",
    )(*fields, owner_map, act_ids, slot_tiles, slot_count)
    yup, ydn = shift(yup, "gy", 1), shift(ydn, "gy", -1)
    xup, xdn = shift(xup, "gx", 1), shift(xdn, "gx", -1)
    row = pl.pallas_call(
        row_kernel, out_shape=shape(ndev, ROW), in_specs=[SM, VM], out_specs=VM, name="row"
    )(controls, ids)
    table = lax.all_to_all(row, AXES, 0, 0, tiled=True)
    cup, cdn = pl.pallas_call(
        functools.partial(corner_kernel, cx, cy),
        out_shape=[shape(2, 2, CORNER_ROWS, LANES)] * 2,
        in_specs=[VM] * 3,
        out_specs=[VM] * 2,
        name="corner",
    )(yup, ydn, ids)
    cup, cdn = shift(cup, "gx", 1), shift(cdn, "gx", -1)

    dims = (cx + 2 * XO, 2, YR, LANES)
    s0, s1, kap, a4, qa, listed = pl.pallas_call(
        functools.partial(assemble_kernel, cx, cy, nx, ny),
        out_shape=[shape(*dims)] * 5 + [jax.ShapeDtypeStruct((4, LISTED + 1), jnp.int32)],
        in_specs=[VM] * 10,
        out_specs=[VM] * 5 + [SM],
        scratch_shapes=[
            pltpu.VMEM((16, LANES), jnp.int32),
            pltpu.SMEM((16, LANES), jnp.int32),
            pltpu.SemaphoreType.DMA,
        ],
        compiler_params=pltpu.CompilerParams(vmem_limit_bytes=24 << 20),
        cost_estimate=pl.CostEstimate(flops=20 << 20, bytes_accessed=12 << 20, transcendentals=0),
        name="assemble",
    )(*fields, yup, ydn, xup, xdn, cup, cdn, ids)

    ext = pltpu.VMEM(dims, f32)
    a1, qb, message = pl.pallas_call(
        functools.partial(window_kernel, cx, cy, nx, ny),
        out_shape=[shape(*dims)] * 2 + [shape(ndev, ROW)],
        in_specs=[VM] * 6 + [SM],
        out_specs=[VM] * 3,
        scratch_shapes=[ext] * 6
        + [
            pltpu.VMEM((152, ROW), f32),
            pltpu.VMEM((152, ROW), jnp.int32),
            pltpu.VMEM((3, 152, LANES), f32),
            pltpu.VMEM((4, 16, LANES), f32),
        ],
        compiler_params=pltpu.CompilerParams(vmem_limit_bytes=32 << 20),
        name="window",
    )(s0, s1, kap, a4, qa, table, listed)

    got = lax.all_to_all(message, AXES, 0, 0, tiled=True)
    start_adjoint, flags = pl.pallas_call(
        functools.partial(final_kernel, cx, cy, ny),
        out_shape=[shape(cx, cy, cz), shape(*controls.shape)],
        in_specs=[VM] * 5,
        out_specs=[ANY, VM],
        scratch_shapes=[pltpu.VMEM((cx, 2, cy, LANES), f32), pltpu.SemaphoreType.DMA((2,))],
        compiler_params=pltpu.CompilerParams(vmem_limit_bytes=24 << 20),
        cost_estimate=pl.CostEstimate(flops=5 << 20, bytes_accessed=4 << 20, transcendentals=0),
        name="final",
    )(a1, qb, s0, owner_map.reshape(-1, LANES), free_list)
    gradient = pl.pallas_call(
        gradient_kernel, out_shape=shape(*controls.shape), in_specs=[VM] * 2, out_specs=VM, name="gradient"
    )(got, flags)
    return start_adjoint, gradient


def solution(mesh):
    placed = (
        P("gx", "gy", None),
        P("gx", "gy", None),
        P("gx", "gy", None),
        P(None, ("gx", "gy")),
        P(),
        P(("gx", "gy")),
        P(("gx", "gy")),
        P(("gx", "gy")),
        P(),
    )
    return jax.shard_map(
        shards,
        mesh=mesh,
        in_specs=placed,
        out_specs=(P("gx", "gy", None), P(None, ("gx", "gy"))),
        check_vma=False,
    )
```

```python
import functools

import jax
import jax.numpy as jnp
from jax import lax
from jax.experimental import pallas as pl
from jax.experimental.pallas import tpu as pltpu
from jax.sharding import PartitionSpec as P

TZ = 128
DT = 0.05
VEL = (1.0, 0.7, 0.4)
AXES = ("gx", "gy")

WIDE = (6, 5, 4)
LAYERS = sum(WIDE)
XO = 6
YO = 12
YR = 56
LANES = 128
GROUP = 32
BATCH = 4
CODE = 1024


def corner_pieces():
    pieces, row = [], 0
    for field, wide in enumerate(WIDE):
        for layer in range(1, wide):
            pieces.append((field, layer, wide - layer, row))
            row += wide - layer
    return pieces, -(-row // 8) * 8


CORNER, CORNER_ROWS = corner_pieces()


def lines(nx):
    return [[4 * y + 2 * low + core for y in range(nx // 4) for core in range(2)] for low in range(2)]


def sheets(nx, ny):
    return [
        [(4 * y + 2 * low + core) * ny + j for low in range(2) for j in range(ny)]
        for y in range(nx // 4)
        for core in range(2)
    ]


def fold(rows):
    count = rows.shape[0]
    if count < 8:
        return jnp.concatenate([rows, jnp.zeros((8 - count, LANES), jnp.float32)], axis=0)
    lane = lax.broadcasted_iota(jnp.int32, (8, LANES), 1)
    table = rows[0:8]
    for g in range(1, count // 8):
        table = jnp.where(lane < g * GROUP, table, pltpu.roll(rows[8 * g : 8 * g + 8], g * GROUP, 1))
    return table


def first_kernel(
    cx, cy, ck_ref, kp_ref, ta_ref, own_ref, ctl_ref, act_ref, til_ref, cnt_ref,
    yup_ref, ydn_ref, ids_ref, row_ref, low, high, own_s, sems,
):
    copies = [pltpu.make_async_copy(own_ref, own_s, sems.at[6])]
    for f, field in enumerate((ck_ref, kp_ref, ta_ref)):
        copies.append(pltpu.make_async_copy(field.at[:, 0:8, :], low.at[f], sems.at[2 * f]))
        copies.append(pltpu.make_async_copy(field.at[:, cy - 8 : cy, :], high.at[f], sems.at[2 * f + 1]))
    for copy in copies:
        copy.start()
    lane = lax.broadcasted_iota(jnp.int32, (1, LANES), 1)
    row = jnp.zeros((1, LANES), jnp.float32)
    steps, owned = ctl_ref.shape
    for n in range(steps):
        for k in range(owned):
            row = jnp.where(lane == n * owned + k, ctl_ref[n, k], row)
    row_ref[...] = jnp.broadcast_to(row, row_ref.shape)
    copies[0].wait()
    ids = jnp.zeros((1, LANES), jnp.int32)
    for j in range(act_ref.shape[0]):
        code = jnp.where(j < cnt_ref[0], own_s[act_ref[j]] * CODE + til_ref[j] + 1, 0)
        ids = jnp.where(lane == j, code, ids)
    ids = ids.astype(jnp.float32)
    ids_ref[...] = jnp.broadcast_to(ids, ids_ref.shape)
    for copy in copies[1:]:
        copy.wait()
    halves = (slice(0, LANES), slice(LANES, 2 * LANES))

    def rows(x, carry):
        at = 0
        for f, wide in enumerate(WIDE):
            for h in range(2):
                yup_ref[x, h, at : at + wide, :] = high[f, x, 8 - wide : 8, halves[h]]
                ydn_ref[x, h, at : at + wide, :] = low[f, x, 0:wide, halves[h]]
            at += wide
        return carry

    lax.fori_loop(0, cx, rows, 0, unroll=True)
    yup_ref[0, 0, LAYERS : LAYERS + 1, :] = ids
    ydn_ref[0, 0, LAYERS : LAYERS + 1, :] = ids


def second_kernel(
    cx, cy, nx, ny, ck_ref, kp_ref, ta_ref, yup_ref, ydn_ref, ids_ref, got_ref,
    xup_ref, xdn_ref, tab_ref, sems,
):
    copies = []
    at = 0
    for field, wide in zip((ck_ref, kp_ref, ta_ref), WIDE):
        for h in range(2):
            half = slice(h * LANES, (h + 1) * LANES)
            for ref, x in ((xup_ref, cx - wide), (xdn_ref, 0)):
                copies.append(
                    pltpu.make_async_copy(
                        field.at[x : x + wide, :, half], ref.at[at : at + wide, h], sems.at[len(copies)]
                    )
                )
        at += wide
    for copy in copies:
        copy.start()
    for f, layer, count, start in CORNER:
        top = sum(WIDE[: f + 1])
        at = top - WIDE[f]
        for ref, x in ((xup_ref, cx - layer), (xdn_ref, layer - 1)):
            for h in range(2):
                ref[LAYERS, h, start : start + count, :] = yup_ref[x, h, top - count : top, :]
                ref[LAYERS + 1, h, start : start + count, :] = ydn_ref[x, h, at : at + count, :]
    for ref in (xup_ref, xdn_ref):
        ref[LAYERS, 0, cy - 1 : cy, :] = ids_ref[0:1, :]
        ref[LAYERS, 1, cy - 1 : cy, :] = yup_ref[0, 0, LAYERS : LAYERS + 1, :]
        ref[LAYERS + 1, 0, cy - 1 : cy, :] = ydn_ref[0, 0, LAYERS : LAYERS + 1, :]
    tab_ref[...] = jnp.broadcast_to(fold(got_ref[...])[None], tab_ref.shape)
    for copy in copies:
        copy.wait()


def window_kernel(
    cx, cy, nx, ny, ck_ref, kp_ref, ta_ref,
    yup_ref, ydn_ref, xup_ref, xdn_ref, ids_ref, tab_ref, own_ref, free_ref,
    out_ref, msg_ref, flag_ref,
    s0, s1, s2, s3, kap, a4, a3, a2, a1, qa, qb,
    near_v, near_s, list_s, pick_v, which_v, amp_v, sum_v, sem, res, out_sems,
):
    gx = lax.axis_index("gx")
    gy = lax.axis_index("gy")
    halves = (slice(0, LANES), slice(LANES, 2 * LANES))
    lane = lax.broadcasted_iota(jnp.int32, (1, LANES), 1)

    spare = slice(LAYERS, LAYERS + 1)
    tail = slice(cy - 1, cy)
    near = (
        ((0, 0), ids_ref[0:1, :]),
        ((0, -1), yup_ref[0, 0, spare, :]),
        ((0, 1), ydn_ref[0, 0, spare, :]),
        ((-1, 0), xup_ref[LAYERS, 0, tail, :]),
        ((-1, -1), xup_ref[LAYERS, 1, tail, :]),
        ((-1, 1), xup_ref[LAYERS + 1, 0, tail, :]),
        ((1, 0), xdn_ref[LAYERS, 0, tail, :]),
        ((1, -1), xdn_ref[LAYERS, 1, tail, :]),
        ((1, 1), xdn_ref[LAYERS + 1, 0, tail, :]),
    )
    for i, (_, codes) in enumerate(near):
        near_v[i : i + 1, :] = codes.astype(jnp.int32) - 1
    ids = pltpu.make_async_copy(near_v, near_s, sem)
    ids.start()

    me = gx * ny + gy
    steps, owned = flag_ref.shape
    flat = lax.broadcasted_iota(jnp.int32, own_ref.shape, 0) * LANES + lax.broadcasted_iota(
        jnp.int32, own_ref.shape, 1
    )
    free = free_ref[...]
    column = lax.broadcasted_iota(jnp.int32, (steps, owned), 1)
    flags = jnp.zeros((steps, owned), jnp.float32)
    for k in range(owned):
        mine = jnp.where(own_ref[...] == me * owned + k, flat, 0)
        actuator = jnp.sum(jnp.sum(mine, axis=0, keepdims=True), axis=1, keepdims=True)
        hit = jnp.max(jnp.where(free == actuator, 1.0, 0.0), axis=1, keepdims=True)
        flags = jnp.where(column == k, hit, flags)
    flag_ref[...] = flags

    fields = ((ck_ref, s0), (kp_ref, kap), (ta_ref, a4))
    for f, (own, ext) in enumerate(fields):
        wide, at = WIDE[f], sum(WIDE[:f])

        def take(value, f=f):
            return DT * value if f == 1 else value

        def assemble(x, carry, own=own, ext=ext, wide=wide, at=at, take=take):
            for h in range(2):
                ext[XO + x, h, YO : YO + cy, :] = take(own[x, :, halves[h]])
                ext[XO + x, h, YO - wide : YO, :] = take(yup_ref[x, h, at : at + wide, :])
                ext[XO + x, h, YO + cy : YO + cy + wide, :] = take(ydn_ref[x, h, at : at + wide, :])
            return carry

        lax.fori_loop(0, cx, assemble, 0, unroll=True)
        for i in range(wide):
            for h in range(2):
                ext[XO - wide + i, h, YO : YO + cy, :] = take(xup_ref[at + i, h])
                ext[XO + cx + i, h, YO : YO + cy, :] = take(xdn_ref[at + i, h])
        for c, layer, count, start in CORNER:
            if c != f:
                continue
            for ref, x in ((xup_ref, XO - layer), (xdn_ref, XO + cx + layer - 1)):
                for h in range(2):
                    ext[x, h, YO - count : YO, :] = take(ref[LAYERS, h, start : start + count, :])
                    ext[x, h, YO + cy : YO + cy + count, :] = take(ref[LAYERS + 1, h, start : start + count, :])

    ids.wait()
    total = jnp.int32(0)
    own_total = jnp.int32(0)
    for i, ((a, b), _) in enumerate(near):
        for j in range(16):
            code = near_s[i, j]
            place = lax.shift_right_arithmetic(code, 10)
            tile = code & (CODE - 1)
            x = lax.shift_right_logical(tile, 6) + (XO + a * cx)
            y = (lax.shift_right_logical(tile, 1) & (cy - 1)) + (YO + b * cy)
            keep = place >= 0
            if a != 0:
                keep &= (x >= XO - 5) & (x < XO + cx + 5)
            if b != 0:
                keep &= (y >= YO - 5) & (y < YO + cy + 5)
            list_s[0, total] = x
            list_s[1, total] = tile & 1
            list_s[2, total] = y
            list_s[3, total] = place
            total = total + keep.astype(jnp.int32)
        if i == 0:
            own_total = total
    for j in range(BATCH):
        for part in range(4):
            list_s[part, total + j] = 0
    batches = lax.div(total + BATCH - 1, BATCH)

    def pick(batch, carry):
        for j in range(BATCH):
            pick_one(batch * BATCH + j)
        return carry

    def pick_one(e):
        place = list_s[3, e]
        owner = lax.shift_right_logical(place, 3)
        line, j = lax.div(owner, ny), lax.rem(owner, ny)
        q = 2 * lax.shift_right_logical(line, 2) + (line & 1)
        at = 8 * ((lax.shift_right_logical(line, 1) & 1) * ny + j) + (q & 7)
        list_s[3, e] = at
        pick_v[pl.ds(e, 1), :] = tab_ref[pl.ds(at, 1), :]
        column = GROUP * lax.shift_right_logical(q, 3) + (place & 7)
        which_v[pl.ds(e, 1), :] = jnp.broadcast_to(column, (1, LANES))

    lax.fori_loop(0, batches, pick, 0)
    lanes = lax.broadcasted_iota(jnp.int32, pick_v.shape, 1)
    for n in range(3):
        chosen = jnp.where(lanes - 8 * n == which_v[...], pick_v[...], 0.0)
        amp_v[n] = jnp.broadcast_to(DT * jnp.sum(chosen, axis=1, keepdims=True), pick_v.shape)

    lo_x, hi_x, lo_y, hi_y = gx == 0, gx == nx - 1, gy == 0, gy == ny - 1

    def clear_outside(ref):
        @pl.when(lo_x)
        def _():
            ref[XO - 1] = jnp.zeros(ref.shape[1:], jnp.float32)

        @pl.when(hi_x)
        def _():
            ref[XO + cx] = jnp.zeros(ref.shape[1:], jnp.float32)

        @pl.when(lo_y)
        def _():
            ref[:, :, YO - 1 : YO, :] = jnp.zeros((ref.shape[0], 2, 1, LANES), jnp.float32)

        @pl.when(hi_y)
        def _():
            ref[:, :, YO + cy : YO + cy + 1, :] = jnp.zeros((ref.shape[0], 2, 1, LANES), jnp.float32)

    first = lax.broadcasted_iota(jnp.int32, (8, LANES), 1) == 0
    last = lax.broadcasted_iota(jnp.int32, (8, LANES), 1) == LANES - 1

    def spread(ref, x, h, y, tiles, extra=0):
        return [ref[x, h, pl.ds(y + t, 8, stride=tiles), :] for t in range(-extra, tiles + extra)]

    def depth(v0, v1):
        f0, f1 = pltpu.roll(v0, 1, 1), pltpu.roll(v1, 1, 1)
        b0, b1 = pltpu.roll(v0, LANES - 1, 1), pltpu.roll(v1, LANES - 1, 1)
        before = (jnp.where(first, 0.0, f0), jnp.where(first, f0, f1))
        after = (jnp.where(last, b1, b0), jnp.where(last, 0.0, b1))
        return before, after

    def forward(src, dst, lo, hi, y, tiles):
        def plane(x, carry):
            mid = [spread(src, x, h, y, tiles, 1) for h in range(2)]
            nxt = [spread(src, x + 1, h, y, tiles) for h in range(2)]
            prv = [spread(src, x - 1, h, y, tiles) for h in range(2)]
            kappa = [spread(kap, x, h, y, tiles) for h in range(2)]
            for t in range(tiles):
                before, after = depth(mid[0][t + 1], mid[1][t + 1])
                for h in range(2):
                    f = mid[h][t + 1]
                    pairs = ((nxt[h][t], prv[h][t]), (mid[h][t + 2], mid[h][t]), (after[h], before[h]))
                    (sx, sy, sz), (dx, dy, dz) = zip(*[(p + m, p - m) for p, m in pairs])
                    lap = (sx + sy) + (sz - 6.0 * f)
                    adv = (0.25 * DT * VEL[0]) * (sx * dx) + ((0.25 * DT * VEL[1]) * (sy * dy) + (0.25 * DT * VEL[2]) * (sz * dz))
                    dst[x, h, pl.ds(y + t, 8, stride=tiles), :] = f + (kappa[h][t] * lap - adv)
            return carry

        lax.fori_loop(lo, hi, plane, 0, unroll=True)

    def actuate(n, dst):
        def some(batch, carry):
            for j in range(BATCH):
                e = batch * BATCH + j
                x, h, y = list_s[0, e], list_s[1, e], list_s[2, e]
                dst[x, h, pl.ds(y, 1), :] += amp_v[n, pl.ds(e, 1), :]
            return carry

        lax.fori_loop(0, batches, some, 0)
        clear_outside(dst)

    forward(s0, s1, XO - 5, XO, YO - 4, 5)
    forward(s0, s1, XO, XO + cx, YO - 5, 6)
    forward(s0, s1, XO + cx, XO + cx + 5, YO - 4, 5)
    actuate(0, s1)
    forward(s1, s2, XO - 4, XO + cx + 4, YO - 4, 5)
    actuate(1, s2)
    forward(s2, s3, XO - 3, XO + cx + 3, YO - 3, 5)
    actuate(2, s3)

    def scale(x, carry):
        for h in range(2):
            qa[x, h] = kap[x, h] * a4[x, h]
        return carry

    lax.fori_loop(XO - 4, XO + cx + 4, scale, 0, unroll=True)

    def step(adj, q, state, x, y, tiles, emit):
        mid = [spread(adj, x, h, y, tiles, 1) for h in range(2)]
        qmid = [spread(q, x, h, y, tiles, 1) for h in range(2)]
        for t in range(tiles):
            before, after = depth(mid[0][t + 1], mid[1][t + 1])
            qbefore, qafter = depth(qmid[0][t + 1], qmid[1][t + 1])
            for h in range(2):
                at = pl.ds(y + t, 8, stride=tiles)
                lap = (
                    (q[x + 1, h, at, :] + q[x - 1, h, at, :])
                    + (qmid[h][t + 2] + qmid[h][t])
                    + ((qafter[h] + qbefore[h]) - 6.0 * qmid[h][t + 1])
                )
                drift = (
                    (0.5 * DT * VEL[0]) * (adj[x + 1, h, at, :] - adj[x - 1, h, at, :])
                    + (0.5 * DT * VEL[1]) * (mid[h][t + 2] - mid[h][t])
                    + (0.5 * DT * VEL[2]) * (after[h] - before[h])
                )
                emit(h, t, at, mid[h][t + 1] + (lap + state[x, h, at, :] * drift))

    def backward(adj, q, state, dst, qdst, wide):
        y = YO - wide

        def plane(x, carry):
            def emit(h, t, at, value):
                dst[x, h, at, :] = value
                qdst[x, h, at, :] = kap[x, h, at, :] * value

            step(adj, q, state, x, y, 5, emit)
            return carry

        lax.fori_loop(XO - wide, XO + cx + wide, plane, 0, unroll=True)
        clear_outside(dst)

    backward(a4, qa, s3, a3, qb, 3)
    backward(a3, qb, s2, a2, qa, 2)
    backward(a2, qa, s1, a1, qb, 1)

    def final(x, carry):
        def emit(h, t, at, value):
            res[x, h, pl.ds(t, 8, stride=cy // 8), :] = value

        step(a1, qb, s0, XO + x, YO, cy // 8, emit)
        return carry

    lax.fori_loop(0, cx, final, 0, unroll=True)
    writes = [pltpu.make_async_copy(res.at[:, h], out_ref.at[:, :, halves[h]], out_sems.at[h]) for h in range(2)]
    for write in writes:
        write.start()

    msg_ref[...] = jnp.zeros(msg_ref.shape, jnp.float32)

    def foot(e, carry):
        x, h, y = list_s[0, e], list_s[1, e], list_s[2, e]
        for n, adj in enumerate((a1, a2, a3, a4)):
            sum_v[n, pl.ds(e, 1), :] = adj[x, h, pl.ds(y, 1), :]
        return carry

    lax.fori_loop(0, own_total, foot, 0)
    part = jnp.zeros((16, LANES), jnp.float32)
    for n in range(4):
        sums = DT * jnp.sum(sum_v[n], axis=1, keepdims=True)
        part = jnp.where(lanes[:16] - 8 * n == which_v[0:16, :], sums, part)
    sum_v[0] = part

    def post(e, carry):
        at = pl.ds(list_s[3, e], 1)
        msg_ref[at, :] += sum_v[0, pl.ds(e, 1), :]
        return carry

    lax.fori_loop(0, own_total, post, 0)
    for write in writes:
        write.wait()


def sum_kernel(got_ref, out_ref):
    total = jnp.sum(got_ref[...], axis=0)
    for at in range(0, out_ref.shape[0], 8):
        rows = min(8, out_ref.shape[0])
        out_ref[at : at + rows, :] = pltpu.roll(total, (LANES - GROUP * (at // 8)) % LANES, 1)[0:rows]


def gradient_kernel(got_ref, flag_ref, out_ref):
    steps, owned = out_ref.shape
    total = jnp.sum(got_ref[...], axis=0, keepdims=True)
    for n in range(steps):
        out_ref[n : n + 1, :] = total[:, n * owned : (n + 1) * owned] * flag_ref[n : n + 1, :]


ANY = pl.BlockSpec(memory_space=pl.ANY)
VM = pl.BlockSpec(memory_space=pltpu.VMEM)
SM = pl.BlockSpec(memory_space=pltpu.SMEM)


def shards(
    checkpoint, terminal_adjoint, diffusivity, controls, owner_map, act_ids, slot_tiles, slot_count, free_list,
):
    cx, cy, cz = checkpoint.shape
    nx, ny = lax.axis_size("gx"), lax.axis_size("gy")
    f32 = jnp.float32

    def shape(*dims):
        return jax.ShapeDtypeStruct(dims, f32)

    def shift(value, axis, way):
        size = lax.axis_size(axis)
        pairs = [(i, i + way) for i in range(size) if 0 <= i + way < size]
        return lax.ppermute(value, axis, pairs)

    fields = (checkpoint, diffusivity, terminal_adjoint)
    yup, ydn, ids, row = pl.pallas_call(
        functools.partial(first_kernel, cx, cy),
        out_shape=[shape(cx, 2, 16, LANES)] * 2 + [shape(8, LANES), shape(nx // 2, LANES)],
        in_specs=[ANY] * 4 + [SM] * 4,
        out_specs=[VM] * 4,
        scratch_shapes=[
            pltpu.VMEM((3, cx, 8, cz), f32),
            pltpu.VMEM((3, cx, 8, cz), f32),
            pltpu.SMEM(owner_map.shape, jnp.int32),
            pltpu.SemaphoreType.DMA((7,)),
        ],
        compiler_params=pltpu.CompilerParams(vmem_limit_bytes=60 << 20),
        name="first",
    )(*fields, owner_map, controls, act_ids, slot_tiles, slot_count)
    yup, ydn = shift(yup, "gy", 1), shift(ydn, "gy", -1)
    line, sheet = lines(nx), sheets(nx, ny)
    got = lax.all_to_all(row, "gx", 0, 0, axis_index_groups=line, tiled=True)
    xup, xdn, table = pl.pallas_call(
        functools.partial(second_kernel, cx, cy, nx, ny),
        out_shape=[shape(LAYERS + 2, 2, cy, LANES)] * 2 + [shape(2 * ny, 8, LANES)],
        in_specs=[ANY] * 3 + [VM] * 4,
        out_specs=[VM] * 3,
        scratch_shapes=[pltpu.SemaphoreType.DMA((12,))],
        compiler_params=pltpu.CompilerParams(vmem_limit_bytes=32 << 20),
        name="second",
    )(*fields, yup, ydn, ids, got)
    xup, xdn = shift(xup, "gx", 1), shift(xdn, "gx", -1)
    table = lax.all_to_all(table, AXES, 0, 0, axis_index_groups=sheet, tiled=True).reshape(16 * ny, LANES)

    ext = pltpu.VMEM((cx + 2 * XO, 2, YR, LANES), f32)
    start_adjoint, message, flags = pl.pallas_call(
        functools.partial(window_kernel, cx, cy, nx, ny),
        out_shape=[shape(cx, cy, cz), shape(16 * ny, LANES), shape(*controls.shape)],
        in_specs=[VM] * 11,
        out_specs=[ANY, VM, VM],
        scratch_shapes=[ext] * 11
        + [
            pltpu.VMEM((16, LANES), jnp.int32),
            pltpu.SMEM((16, LANES), jnp.int32),
            pltpu.SMEM((4, 160), jnp.int32),
            pltpu.VMEM((152, LANES), f32),
            pltpu.VMEM((152, LANES), jnp.int32),
            pltpu.VMEM((3, 152, LANES), f32),
            pltpu.VMEM((4, 16, LANES), f32),
            pltpu.SemaphoreType.DMA,
            pltpu.VMEM((cx, 2, cy, LANES), f32),
            pltpu.SemaphoreType.DMA((2,)),
        ],
        compiler_params=pltpu.CompilerParams(vmem_limit_bytes=48 << 20),
        name="window",
    )(*fields, yup, ydn, xup, xdn, ids, table, owner_map.reshape(-1, LANES), free_list)

    message = message.reshape(2 * ny, 8, LANES)
    got = lax.all_to_all(message, AXES, 0, 0, axis_index_groups=sheet, tiled=True)
    part = pl.pallas_call(
        sum_kernel, out_shape=shape(nx // 2, LANES), in_specs=[VM], out_specs=VM, name="partial_sums"
    )(got)
    got = lax.all_to_all(part, "gx", 0, 0, axis_index_groups=line, tiled=True)
    gradient = pl.pallas_call(
        gradient_kernel, out_shape=shape(*controls.shape), in_specs=[VM] * 2, out_specs=VM, name="gradient"
    )(got, flags)
    return start_adjoint, gradient


def solution(mesh):
    placed = (
        P("gx", "gy", None),
        P("gx", "gy", None),
        P("gx", "gy", None),
        P(None, ("gx", "gy")),
        P(),
        P(("gx", "gy")),
        P(("gx", "gy")),
        P(("gx", "gy")),
        P(),
    )
    return jax.shard_map(
        shards,
        mesh=mesh,
        in_specs=placed,
        out_specs=(P("gx", "gy", None), P(None, ("gx", "gy"))),
        check_vma=False,
    )
```

```python
import functools

import jax
import jax.numpy as jnp
from jax import lax
from jax.experimental import pallas as pl
from jax.experimental.pallas import tpu as pltpu
from jax.sharding import PartitionSpec as P

TZ = 128
DT = 0.05
VEL = (1.0, 0.7, 0.4)
AXES = ("gx", "gy")

WIDE = (6, 5, 4)
LAYERS = sum(WIDE)
XO = 6
YO = 12
YR = 56
LANES = 128
GROUP = 32
PIECE = 4
BATCH = 4
CODE = 1024


def corner_pieces():
    pieces, row = [], 0
    for field, wide in enumerate(WIDE):
        for layer in range(1, wide):
            pieces.append((field, layer, wide - layer, row))
            row += wide - layer
    return pieces, -(-row // 8) * 8


CORNER, CORNER_ROWS = corner_pieces()


def table_rows(nx):
    return max(8, nx * GROUP // LANES)


def first_kernel(
    cx, cy, ck_ref, kp_ref, ta_ref, own_ref, ctl_ref, act_ref, til_ref, cnt_ref,
    yup_ref, ydn_ref, ids_ref, row_ref, low, high, own_s, ctl_s, act_s, til_s, cnt_s, sems, small_sems,
):
    small = [
        pltpu.make_async_copy(source, place, small_sems.at[i])
        for i, (source, place) in enumerate(
            ((own_ref, own_s), (act_ref, act_s), (til_ref, til_s), (cnt_ref, cnt_s), (ctl_ref, ctl_s))
        )
    ]
    copies = []
    for f, field in enumerate((ck_ref, kp_ref, ta_ref)):
        copies.append(pltpu.make_async_copy(field.at[:, 0:8, :], low.at[f], sems.at[2 * f]))
        copies.append(pltpu.make_async_copy(field.at[:, cy - 8 : cy, :], high.at[f], sems.at[2 * f + 1]))
    for copy in small + copies:
        copy.start()
    lane = lax.broadcasted_iota(jnp.int32, (1, LANES), 1)
    for copy in small:
        copy.wait()
    row = jnp.zeros((1, LANES), jnp.float32)
    steps, owned = ctl_s.shape
    for n in range(steps):
        for k in range(owned):
            row = jnp.where(lane == n * owned + k, ctl_s[n, k], row)
    row_ref[...] = jnp.broadcast_to(row, row_ref.shape)
    ids = jnp.zeros((1, LANES), jnp.int32)
    for j in range(act_s.shape[0]):
        code = jnp.where(j < cnt_s[0], own_s[act_s[j]] * CODE + til_s[j] + 1, 0)
        ids = jnp.where(lane == j, code, ids)
    ids = ids.astype(jnp.float32)
    ids_ref[...] = jnp.broadcast_to(ids, ids_ref.shape)
    for copy in copies:
        copy.wait()
    halves = (slice(0, LANES), slice(LANES, 2 * LANES))

    def rows(x, carry):
        at = 0
        for f, wide in enumerate(WIDE):
            for h in range(2):
                yup_ref[x, h, at : at + wide, :] = high[f, x, 8 - wide : 8, halves[h]]
                ydn_ref[x, h, at : at + wide, :] = low[f, x, 0:wide, halves[h]]
            at += wide
        return carry

    lax.fori_loop(0, cx, rows, 0, unroll=True)
    yup_ref[0, 0, LAYERS : LAYERS + 1, :] = ids
    ydn_ref[0, 0, LAYERS : LAYERS + 1, :] = ids


def second_kernel(
    cx, cy, nx, ny, ck_ref, kp_ref, ta_ref, yup_ref, ydn_ref, ids_ref, got_ref,
    xup_ref, xdn_ref, tab_ref, sems,
):
    copies = []
    at = 0
    for field, wide in zip((ck_ref, kp_ref, ta_ref), WIDE):
        for h in range(2):
            half = slice(h * LANES, (h + 1) * LANES)
            for ref, x in ((xup_ref, cx - wide), (xdn_ref, 0)):
                copies.append(
                    pltpu.make_async_copy(
                        field.at[x : x + wide, :, half], ref.at[at : at + wide, h], sems.at[len(copies)]
                    )
                )
        at += wide
    for copy in copies:
        copy.start()
    for f, layer, count, start in CORNER:
        top = sum(WIDE[: f + 1])
        at = top - WIDE[f]
        for ref, x in ((xup_ref, cx - layer), (xdn_ref, layer - 1)):
            for h in range(2):
                ref[LAYERS, h, start : start + count, :] = yup_ref[x, h, top - count : top, :]
                ref[LAYERS + 1, h, start : start + count, :] = ydn_ref[x, h, at : at + count, :]
    for ref in (xup_ref, xdn_ref):
        ref[LAYERS, 0, cy - 1 : cy, :] = ids_ref[0:1, :]
        ref[LAYERS, 1, cy - 1 : cy, :] = yup_ref[0, 0, LAYERS : LAYERS + 1, :]
        ref[LAYERS + 1, 0, cy - 1 : cy, :] = ydn_ref[0, 0, LAYERS : LAYERS + 1, :]
    rows = table_rows(nx)
    if nx < rows:
        for j in range(ny):
            tab_ref[j, 0:nx, :] = got_ref[...]
            tab_ref[j, nx:rows, :] = jnp.zeros((rows - nx, LANES), jnp.float32)
    else:
        lane = lax.broadcasted_iota(jnp.int32, (rows, LANES), 1)
        table = got_ref[0:rows, :]
        for g in range(1, nx // rows):
            part = pltpu.roll(got_ref[g * rows : (g + 1) * rows, :], g * GROUP, 1)
            table = jnp.where(lane < g * GROUP, table, part)
        tab_ref[...] = jnp.broadcast_to(table[None], tab_ref.shape)
    for copy in copies:
        copy.wait()


def window_kernel(
    cx, cy, nx, ny, ck_ref, kp_ref, ta_ref,
    yup_ref, ydn_ref, xup_ref, xdn_ref, ids_ref, tab_ref, own_ref, free_ref,
    out_ref, msg_ref, flag_ref,
    s0, s1, s2, s3, kap, a4, a3, a2, a1, qa, qb,
    near_v, near_s, list_s, pick_v, which_v, amp_v, sum_v, sem, res, out_sems,
):
    gx = lax.axis_index("gx")
    gy = lax.axis_index("gy")
    halves = (slice(0, LANES), slice(LANES, 2 * LANES))
    lane = lax.broadcasted_iota(jnp.int32, (1, LANES), 1)

    spare = slice(LAYERS, LAYERS + 1)
    tail = slice(cy - 1, cy)
    near = (
        ((0, 0), ids_ref[0:1, :]),
        ((0, -1), yup_ref[0, 0, spare, :]),
        ((0, 1), ydn_ref[0, 0, spare, :]),
        ((-1, 0), xup_ref[LAYERS, 0, tail, :]),
        ((-1, -1), xup_ref[LAYERS, 1, tail, :]),
        ((-1, 1), xup_ref[LAYERS + 1, 0, tail, :]),
        ((1, 0), xdn_ref[LAYERS, 0, tail, :]),
        ((1, -1), xdn_ref[LAYERS, 1, tail, :]),
        ((1, 1), xdn_ref[LAYERS + 1, 0, tail, :]),
    )
    for i, (_, codes) in enumerate(near):
        near_v[i : i + 1, :] = codes.astype(jnp.int32) - 1
    ids = pltpu.make_async_copy(near_v, near_s, sem)
    ids.start()

    me = gx * ny + gy
    steps, owned = flag_ref.shape
    flat = lax.broadcasted_iota(jnp.int32, own_ref.shape, 0) * LANES + lax.broadcasted_iota(
        jnp.int32, own_ref.shape, 1
    )
    free = free_ref[...]
    column = lax.broadcasted_iota(jnp.int32, (steps, owned), 1)
    flags = jnp.zeros((steps, owned), jnp.float32)
    for k in range(owned):
        mine = jnp.where(own_ref[...] == me * owned + k, flat, 0)
        actuator = jnp.sum(jnp.sum(mine, axis=0, keepdims=True), axis=1, keepdims=True)
        hit = jnp.max(jnp.where(free == actuator, 1.0, 0.0), axis=1, keepdims=True)
        flags = jnp.where(column == k, hit, flags)
    flag_ref[...] = flags

    ids.wait()
    fields = ((ck_ref, s0), (kp_ref, kap), (ta_ref, a4))
    for f, (own, ext) in enumerate(fields):
        wide, at = WIDE[f], sum(WIDE[:f])

        def take(value, f=f):
            return DT * value if f == 1 else value

        def assemble(x, carry, own=own, ext=ext, wide=wide, at=at, take=take):
            for h in range(2):
                ext[XO + x, h, YO : YO + cy, :] = take(own[x, :, halves[h]])
                ext[XO + x, h, YO - wide : YO, :] = take(yup_ref[x, h, at : at + wide, :])
                ext[XO + x, h, YO + cy : YO + cy + wide, :] = take(ydn_ref[x, h, at : at + wide, :])
            return carry

        lax.fori_loop(0, cx, assemble, 0, unroll=True)
        for i in range(wide):
            for h in range(2):
                ext[XO - wide + i, h, YO : YO + cy, :] = take(xup_ref[at + i, h])
                ext[XO + cx + i, h, YO : YO + cy, :] = take(xdn_ref[at + i, h])
        for c, layer, count, start in CORNER:
            if c != f:
                continue
            for ref, x in ((xup_ref, XO - layer), (xdn_ref, XO + cx + layer - 1)):
                for h in range(2):
                    ext[x, h, YO - count : YO, :] = take(ref[LAYERS, h, start : start + count, :])
                    ext[x, h, YO + cy : YO + cy + count, :] = take(ref[LAYERS + 1, h, start : start + count, :])

    total = jnp.int32(0)
    own_total = jnp.int32(0)
    for i, ((a, b), _) in enumerate(near):
        for j in range(16):
            code = near_s[i, j]
            place = lax.shift_right_arithmetic(code, 10)
            tile = code & (CODE - 1)
            x = lax.shift_right_logical(tile, 6) + (XO + a * cx)
            y = (lax.shift_right_logical(tile, 1) & (cy - 1)) + (YO + b * cy)
            keep = place >= 0
            if a != 0:
                keep &= (x >= XO - 5) & (x < XO + cx + 5)
            if b != 0:
                keep &= (y >= YO - 5) & (y < YO + cy + 5)
            list_s[0, total] = x
            list_s[1, total] = tile & 1
            list_s[2, total] = y
            list_s[3, total] = place
            total = total + keep.astype(jnp.int32)
        if i == 0:
            own_total = total
    for j in range(BATCH):
        for part in range(4):
            list_s[part, total + j] = 0
    batches = lax.div(total + BATCH - 1, BATCH)

    rows = table_rows(nx)

    def pick(batch, carry):
        for j in range(BATCH):
            pick_one(batch * BATCH + j)
        return carry

    def pick_one(e):
        place = list_s[3, e]
        owner = lax.shift_right_logical(place, 3)
        column, line = lax.rem(owner, ny), lax.div(owner, ny)
        at = column * rows + lax.rem(line, rows)
        pick_v[pl.ds(e, 1), :] = tab_ref[pl.ds(at, 1), :]
        which_v[pl.ds(e, 1), :] = jnp.broadcast_to(lax.div(line, rows) * GROUP + (place & 7), (1, LANES))

    lax.fori_loop(0, batches, pick, 0)
    lanes = lax.broadcasted_iota(jnp.int32, pick_v.shape, 1)
    for n in range(3):
        chosen = jnp.where(lanes - 8 * n == which_v[...], pick_v[...], 0.0)
        amp_v[n] = jnp.broadcast_to(DT * jnp.sum(chosen, axis=1, keepdims=True), pick_v.shape)

    lo_x, hi_x, lo_y, hi_y = gx == 0, gx == nx - 1, gy == 0, gy == ny - 1

    def clear_outside(ref):
        @pl.when(lo_x)
        def _():
            ref[XO - 1] = jnp.zeros(ref.shape[1:], jnp.float32)

        @pl.when(hi_x)
        def _():
            ref[XO + cx] = jnp.zeros(ref.shape[1:], jnp.float32)

        @pl.when(lo_y)
        def _():
            ref[:, :, YO - 1 : YO, :] = jnp.zeros((ref.shape[0], 2, 1, LANES), jnp.float32)

        @pl.when(hi_y)
        def _():
            ref[:, :, YO + cy : YO + cy + 1, :] = jnp.zeros((ref.shape[0], 2, 1, LANES), jnp.float32)

    first = lax.broadcasted_iota(jnp.int32, (8, LANES), 1) == 0
    last = lax.broadcasted_iota(jnp.int32, (8, LANES), 1) == LANES - 1

    def spread(ref, x, h, y, tiles, extra=0):
        return [ref[x, h, pl.ds(y + t, 8, stride=tiles), :] for t in range(-extra, tiles + extra)]

    def depth(v0, v1):
        f0, f1 = pltpu.roll(v0, 1, 1), pltpu.roll(v1, 1, 1)
        b0, b1 = pltpu.roll(v0, LANES - 1, 1), pltpu.roll(v1, LANES - 1, 1)
        before = (jnp.where(first, 0.0, f0), jnp.where(first, f0, f1))
        after = (jnp.where(last, b1, b0), jnp.where(last, 0.0, b1))
        return before, after

    def forward(src, dst, lo, hi, y, tiles):
        def plane(x, carry):
            mid = [spread(src, x, h, y, tiles, 1) for h in range(2)]
            nxt = [spread(src, x + 1, h, y, tiles) for h in range(2)]
            prv = [spread(src, x - 1, h, y, tiles) for h in range(2)]
            kappa = [spread(kap, x, h, y, tiles) for h in range(2)]
            for t in range(tiles):
                before, after = depth(mid[0][t + 1], mid[1][t + 1])
                for h in range(2):
                    f = mid[h][t + 1]
                    pairs = ((nxt[h][t], prv[h][t]), (mid[h][t + 2], mid[h][t]), (after[h], before[h]))
                    (sx, sy, sz), (dx, dy, dz) = zip(*[(p + m, p - m) for p, m in pairs])
                    lap = (sx + sy) + (sz - 6.0 * f)
                    adv = (0.25 * DT * VEL[0]) * (sx * dx) + ((0.25 * DT * VEL[1]) * (sy * dy) + (0.25 * DT * VEL[2]) * (sz * dz))
                    dst[x, h, pl.ds(y + t, 8, stride=tiles), :] = f + (kappa[h][t] * lap - adv)
            return carry

        lax.fori_loop(lo, hi, plane, 0, unroll=True)

    def actuate(n, dst):
        def some(batch, carry):
            for j in range(BATCH):
                e = batch * BATCH + j
                x, h, y = list_s[0, e], list_s[1, e], list_s[2, e]
                dst[x, h, pl.ds(y, 1), :] += amp_v[n, pl.ds(e, 1), :]
            return carry

        lax.fori_loop(0, batches, some, 0)
        clear_outside(dst)

    forward(s0, s1, XO - 5, XO, YO - 4, 5)
    forward(s0, s1, XO, XO + cx, YO - 5, 6)
    forward(s0, s1, XO + cx, XO + cx + 5, YO - 4, 5)
    actuate(0, s1)
    forward(s1, s2, XO - 4, XO + cx + 4, YO - 4, 5)
    actuate(1, s2)
    forward(s2, s3, XO - 3, XO + cx + 3, YO - 3, 5)
    actuate(2, s3)

    def scale(x, carry):
        for h in range(2):
            qa[x, h] = kap[x, h] * a4[x, h]
        return carry

    lax.fori_loop(XO - 4, XO + cx + 4, scale, 0, unroll=True)

    def step(adj, q, state, x, y, tiles, emit):
        mid = [spread(adj, x, h, y, tiles, 1) for h in range(2)]
        qmid = [spread(q, x, h, y, tiles, 1) for h in range(2)]
        for t in range(tiles):
            before, after = depth(mid[0][t + 1], mid[1][t + 1])
            qbefore, qafter = depth(qmid[0][t + 1], qmid[1][t + 1])
            for h in range(2):
                at = pl.ds(y + t, 8, stride=tiles)
                lap = (
                    (q[x + 1, h, at, :] + q[x - 1, h, at, :])
                    + (qmid[h][t + 2] + qmid[h][t])
                    + ((qafter[h] + qbefore[h]) - 6.0 * qmid[h][t + 1])
                )
                drift = (
                    (0.5 * DT * VEL[0]) * (adj[x + 1, h, at, :] - adj[x - 1, h, at, :])
                    + (0.5 * DT * VEL[1]) * (mid[h][t + 2] - mid[h][t])
                    + (0.5 * DT * VEL[2]) * (after[h] - before[h])
                )
                emit(h, t, at, mid[h][t + 1] + (lap + state[x, h, at, :] * drift))

    def backward(adj, q, state, dst, qdst, wide):
        y = YO - wide

        def plane(x, carry):
            def emit(h, t, at, value):
                dst[x, h, at, :] = value
                qdst[x, h, at, :] = kap[x, h, at, :] * value

            step(adj, q, state, x, y, 5, emit)
            return carry

        lax.fori_loop(XO - wide, XO + cx + wide, plane, 0, unroll=True)
        clear_outside(dst)

    backward(a4, qa, s3, a3, qb, 3)
    backward(a3, qb, s2, a2, qa, 2)
    backward(a2, qa, s1, a1, qb, 1)

    writes = []
    for part in range(0, cx, PIECE):
        for x in range(part, part + PIECE):

            def emit(h, t, at, value, x=x):
                res[x, h, pl.ds(t, 8, stride=cy // 8), :] = value

            step(a1, qb, s0, XO + x, YO, cy // 8, emit)
        for h in range(2):
            there = out_ref.at[part : part + PIECE, :, halves[h]]
            writes.append(pltpu.make_async_copy(res.at[part : part + PIECE, h], there, out_sems.at[len(writes)]))
            writes[-1].start()

    msg_ref[...] = jnp.zeros(msg_ref.shape, jnp.float32)

    def foot(e, carry):
        x, h, y = list_s[0, e], list_s[1, e], list_s[2, e]
        for n, adj in enumerate((a1, a2, a3, a4)):
            sum_v[n, pl.ds(e, 1), :] = adj[x, h, pl.ds(y, 1), :]
        return carry

    lax.fori_loop(0, own_total, foot, 0)
    part = jnp.zeros((16, LANES), jnp.float32)
    for n in range(4):
        sums = DT * jnp.sum(sum_v[n], axis=1, keepdims=True)
        part = jnp.where(lanes[:16] - 8 * n == (which_v[0:16, :] & 7), sums, part)
    sum_v[0] = part

    def post(e, carry):
        at = pl.ds(lax.shift_right_logical(list_s[3, e], 3), 1)
        msg_ref[at, :] += sum_v[0, pl.ds(e, 1), :]
        return carry

    lax.fori_loop(0, own_total, post, 0)
    for write in writes:
        write.wait()


def gradient_kernel(got_ref, flag_ref, out_ref):
    steps, owned = out_ref.shape
    total = jnp.sum(got_ref[...], axis=0, keepdims=True)
    for n in range(steps):
        out_ref[n : n + 1, :] = total[:, n * owned : (n + 1) * owned] * flag_ref[n : n + 1, :]


ANY = pl.BlockSpec(memory_space=pl.ANY)
VM = pl.BlockSpec(memory_space=pltpu.VMEM)
SM = pl.BlockSpec(memory_space=pltpu.SMEM)


def shards(
    checkpoint, terminal_adjoint, diffusivity, controls, owner_map, act_ids, slot_tiles, slot_count, free_list,
):
    cx, cy, cz = checkpoint.shape
    nx, ny = lax.axis_size("gx"), lax.axis_size("gy")
    ndev = nx * ny
    f32 = jnp.float32

    def shape(*dims):
        return jax.ShapeDtypeStruct(dims, f32)

    def shift(value, axis, way):
        size = lax.axis_size(axis)
        pairs = [(i, i + way) for i in range(size) if 0 <= i + way < size]
        return lax.ppermute(value, axis, pairs)

    fields = (checkpoint, diffusivity, terminal_adjoint)
    yup, ydn, ids, row = pl.pallas_call(
        functools.partial(first_kernel, cx, cy),
        out_shape=[shape(cx, 2, 16, LANES)] * 2 + [shape(8, LANES), shape(nx, LANES)],
        in_specs=[ANY] * 8,
        out_specs=[VM] * 4,
        scratch_shapes=[
            pltpu.VMEM((3, cx, 8, cz), f32),
            pltpu.VMEM((3, cx, 8, cz), f32),
            pltpu.SMEM(owner_map.shape, jnp.int32),
            pltpu.SMEM(controls.shape, f32),
            pltpu.SMEM(act_ids.shape, jnp.int32),
            pltpu.SMEM(slot_tiles.shape, jnp.int32),
            pltpu.SMEM(slot_count.shape, jnp.int32),
            pltpu.SemaphoreType.DMA((6,)),
            pltpu.SemaphoreType.DMA((5,)),
        ],
        compiler_params=pltpu.CompilerParams(vmem_limit_bytes=60 << 20),
        name="first",
    )(*fields, owner_map, controls, act_ids, slot_tiles, slot_count)
    yup, ydn = shift(yup, "gy", 1), shift(ydn, "gy", -1)
    got = lax.all_to_all(row, "gx", 0, 0, tiled=True)
    rows = table_rows(nx)
    xup, xdn, table = pl.pallas_call(
        functools.partial(second_kernel, cx, cy, nx, ny),
        out_shape=[shape(LAYERS + 2, 2, cy, LANES)] * 2 + [shape(ny, rows, LANES)],
        in_specs=[ANY] * 3 + [VM] * 4,
        out_specs=[VM] * 3,
        scratch_shapes=[pltpu.SemaphoreType.DMA((12,))],
        compiler_params=pltpu.CompilerParams(vmem_limit_bytes=32 << 20),
        name="second",
    )(*fields, yup, ydn, ids, got)
    xup, xdn = shift(xup, "gx", 1), shift(xdn, "gx", -1)
    table = lax.all_to_all(table, "gy", 0, 0, tiled=True).reshape(ny * rows, LANES)

    ext = pltpu.VMEM((cx + 2 * XO, 2, YR, LANES), f32)
    start_adjoint, message, flags = pl.pallas_call(
        functools.partial(window_kernel, cx, cy, nx, ny),
        out_shape=[shape(cx, cy, cz), shape(ndev, LANES), shape(*controls.shape)],
        in_specs=[VM] * 11,
        out_specs=[ANY, VM, VM],
        scratch_shapes=[ext] * 11
        + [
            pltpu.VMEM((16, LANES), jnp.int32),
            pltpu.SMEM((16, LANES), jnp.int32),
            pltpu.SMEM((4, 160), jnp.int32),
            pltpu.VMEM((152, LANES), f32),
            pltpu.VMEM((152, LANES), jnp.int32),
            pltpu.VMEM((3, 152, LANES), f32),
            pltpu.VMEM((4, 16, LANES), f32),
            pltpu.SemaphoreType.DMA,
            pltpu.VMEM((cx, 2, cy, LANES), f32),
            pltpu.SemaphoreType.DMA((2 * cx // PIECE,)),
        ],
        compiler_params=pltpu.CompilerParams(vmem_limit_bytes=48 << 20),
        name="window",
    )(*fields, yup, ydn, xup, xdn, ids, table, owner_map.reshape(-1, LANES), free_list)

    got = lax.all_to_all(message, AXES, 0, 0, tiled=True)
    gradient = pl.pallas_call(
        gradient_kernel, out_shape=shape(*controls.shape), in_specs=[VM] * 2, out_specs=VM, name="gradient"
    )(got, flags)
    return start_adjoint, gradient


def solution(mesh):
    placed = (
        P("gx", "gy", None),
        P("gx", "gy", None),
        P("gx", "gy", None),
        P(None, ("gx", "gy")),
        P(),
        P(("gx", "gy")),
        P(("gx", "gy")),
        P(("gx", "gy")),
        P(),
    )
    return jax.shard_map(
        shards,
        mesh=mesh,
        in_specs=placed,
        out_specs=(P("gx", "gy", None), P(None, ("gx", "gy"))),
        check_vma=False,
    )
```

```python
import functools

import jax
import jax.numpy as jnp
from jax import lax
from jax.experimental import pallas as pl
from jax.experimental.pallas import tpu as pltpu
from jax.sharding import PartitionSpec as P

TZ = 128
DT = 0.05
VEL = (1.0, 0.7, 0.4)
AXES = ("gx", "gy")

WIDE = (6, 5, 4)
LAYERS = sum(WIDE)
XO = 6
YO = 12
YR = 56
LANES = 128
FOLD = 8
GROUP = 32
PIECE = 4
BATCH = 4
CODE = 1024


def corner_pieces():
    pieces, row = [], 0
    for field, wide in enumerate(WIDE):
        for layer in range(1, wide):
            pieces.append((field, layer, wide - layer, row))
            row += wide - layer
    return pieces, -(-row // 8) * 8


CORNER, CORNER_ROWS = corner_pieces()


def table_rows(nx):
    return max(8, nx * GROUP // LANES)


def first_kernel(
    cx, cy, ck_ref, kp_ref, ta_ref, own_ref, ctl_ref, act_ref, til_ref, cnt_ref,
    yup_ref, ydn_ref, ids_ref, row_ref, low, high, own_s, ctl_s, act_s, til_s, cnt_s, sems, small_sems,
):
    small = [
        pltpu.make_async_copy(source, place, small_sems.at[i])
        for i, (source, place) in enumerate(
            ((own_ref, own_s), (act_ref, act_s), (til_ref, til_s), (cnt_ref, cnt_s), (ctl_ref, ctl_s))
        )
    ]
    copies = []
    for f, field in enumerate((ck_ref, kp_ref, ta_ref)):
        copies.append(pltpu.make_async_copy(field.at[:, 0:8, :], low.at[f], sems.at[2 * f]))
        copies.append(pltpu.make_async_copy(field.at[:, cy - 8 : cy, :], high.at[f], sems.at[2 * f + 1]))
    for copy in small + copies:
        copy.start()
    lane = lax.broadcasted_iota(jnp.int32, (1, LANES), 1)
    for copy in small:
        copy.wait()
    row = jnp.zeros((1, LANES), jnp.float32)
    steps, owned = ctl_s.shape
    for n in range(steps):
        for k in range(owned):
            row = jnp.where(lane == n * owned + k, ctl_s[n, k], row)
    row_ref[...] = jnp.broadcast_to(row, row_ref.shape)
    ids = jnp.zeros((1, LANES), jnp.int32)
    for j in range(act_s.shape[0]):
        code = jnp.where(j < cnt_s[0], own_s[act_s[j]] * CODE + til_s[j] + 1, 0)
        ids = jnp.where(lane == j, code, ids)
    ids = ids.astype(jnp.float32)
    ids_ref[...] = jnp.broadcast_to(ids, ids_ref.shape)
    for copy in copies:
        copy.wait()
    halves = (slice(0, LANES), slice(LANES, 2 * LANES))

    def rows(x, carry):
        at = 0
        for f, wide in enumerate(WIDE):
            for h in range(2):
                yup_ref[x, h, at : at + wide, :] = high[f, x, 8 - wide : 8, halves[h]]
                ydn_ref[x, h, at : at + wide, :] = low[f, x, 0:wide, halves[h]]
            at += wide
        return carry

    lax.fori_loop(0, cx, rows, 0, unroll=True)
    yup_ref[0, 0, LAYERS : LAYERS + 1, :] = ids
    ydn_ref[0, 0, LAYERS : LAYERS + 1, :] = ids


def second_kernel(
    cx, cy, nx, ny, ck_ref, kp_ref, ta_ref, yup_ref, ydn_ref, ids_ref, got_ref,
    xup_ref, xdn_ref, tab_ref, sems,
):
    copies = []
    at = 0
    for field, wide in zip((ck_ref, kp_ref, ta_ref), WIDE):
        for h in range(2):
            half = slice(h * LANES, (h + 1) * LANES)
            for ref, x in ((xup_ref, cx - wide), (xdn_ref, 0)):
                copies.append(
                    pltpu.make_async_copy(
                        field.at[x : x + wide, :, half], ref.at[at : at + wide, h], sems.at[len(copies)]
                    )
                )
        at += wide
    for copy in copies:
        copy.start()
    for f, layer, count, start in CORNER:
        top = sum(WIDE[: f + 1])
        at = top - WIDE[f]
        for ref, x in ((xup_ref, cx - layer), (xdn_ref, layer - 1)):
            for h in range(2):
                ref[LAYERS, h, start : start + count, :] = yup_ref[x, h, top - count : top, :]
                ref[LAYERS + 1, h, start : start + count, :] = ydn_ref[x, h, at : at + count, :]
    for ref in (xup_ref, xdn_ref):
        ref[LAYERS, 0, cy - 1 : cy, :] = ids_ref[0:1, :]
        ref[LAYERS, 1, cy - 1 : cy, :] = yup_ref[0, 0, LAYERS : LAYERS + 1, :]
        ref[LAYERS + 1, 0, cy - 1 : cy, :] = ydn_ref[0, 0, LAYERS : LAYERS + 1, :]
    rows = table_rows(nx)
    if nx < rows:
        for j in range(ny):
            tab_ref[j, 0:nx, :] = got_ref[...]
            tab_ref[j, nx:rows, :] = jnp.zeros((rows - nx, LANES), jnp.float32)
    else:
        lane = lax.broadcasted_iota(jnp.int32, (rows, LANES), 1)
        table = got_ref[0:rows, :]
        for g in range(1, nx // rows):
            part = pltpu.roll(got_ref[g * rows : (g + 1) * rows, :], g * GROUP, 1)
            table = jnp.where(lane < g * GROUP, table, part)
        tab_ref[...] = jnp.broadcast_to(table[None], tab_ref.shape)
    for copy in copies:
        copy.wait()


def window_kernel(
    cx, cy, nx, ny, ck_ref, kp_ref, ta_ref,
    yup_ref, ydn_ref, xup_ref, xdn_ref, ids_ref, tab_ref, own_ref, free_ref,
    out_ref, msg_ref, flag_ref,
    s0, s1, s2, s3, kap, a4, a3, a2, a1, qa, qb,
    near_v, near_s, list_s, pick_v, which_v, amp_v, sum_v, sem, res, out_sems,
):
    gx = lax.axis_index("gx")
    gy = lax.axis_index("gy")
    halves = (slice(0, LANES), slice(LANES, 2 * LANES))
    lane = lax.broadcasted_iota(jnp.int32, (1, LANES), 1)

    spare = slice(LAYERS, LAYERS + 1)
    tail = slice(cy - 1, cy)
    near = (
        ((0, 0), ids_ref[0:1, :]),
        ((0, -1), yup_ref[0, 0, spare, :]),
        ((0, 1), ydn_ref[0, 0, spare, :]),
        ((-1, 0), xup_ref[LAYERS, 0, tail, :]),
        ((-1, -1), xup_ref[LAYERS, 1, tail, :]),
        ((-1, 1), xup_ref[LAYERS + 1, 0, tail, :]),
        ((1, 0), xdn_ref[LAYERS, 0, tail, :]),
        ((1, -1), xdn_ref[LAYERS, 1, tail, :]),
        ((1, 1), xdn_ref[LAYERS + 1, 0, tail, :]),
    )
    for i, ((a, b), codes) in enumerate(near):
        code = codes.astype(jnp.int32) - 1
        place, tile = lax.shift_right_arithmetic(code, 10), code & (CODE - 1)
        x = lax.shift_right_logical(tile, 6) + (XO + a * cx)
        y = (lax.shift_right_logical(tile, 1) & (cy - 1)) + (YO + b * cy)
        keep = code >= 0
        if a != 0:
            keep &= (x >= XO - 5) & (x < XO + cx + 5)
        if b != 0:
            keep &= (y >= YO - 5) & (y < YO + cy + 5)
        near_v[i : i + 1, :] = jnp.where(keep, place * 4096 + x * 128 + (tile & 1) * 64 + y, -1)
    ids = pltpu.make_async_copy(near_v, near_s, sem)
    ids.start()

    wide_lane = lax.broadcasted_iota(jnp.int32, (8, LANES), 1)
    sub = lax.broadcasted_iota(jnp.int32, (8, LANES), 0)
    owner = (gx * ny + gy) * 8 + sub
    found = jnp.zeros((8, LANES), jnp.int32)
    for r in range(own_ref.shape[0]):
        found = found + jnp.where(own_ref[r : r + 1, :] == owner, r * LANES + wide_lane, 0)
    actuator = jnp.broadcast_to(jnp.sum(found, axis=1, keepdims=True), (8, LANES))
    flags = jnp.zeros((8, LANES), jnp.float32)
    for n in range(free_ref.shape[0]):
        hit = jnp.zeros((8, LANES), jnp.float32)
        for c in range(free_ref.shape[1] // LANES):
            hit = jnp.where(free_ref[n : n + 1, c * LANES : (c + 1) * LANES] == actuator, 1.0, hit)
        hit = jnp.broadcast_to(jnp.max(hit, axis=1, keepdims=True), (8, LANES))
        flags = jnp.where(wide_lane == 8 * n + sub, hit, flags)
    flag_ref[...] = jnp.broadcast_to(jnp.sum(flags, axis=0, keepdims=True), (8, LANES))

    ids.wait()
    fields = ((ck_ref, s0), (kp_ref, kap), (ta_ref, a4))
    for f, (own, ext) in enumerate(fields):
        wide, at = WIDE[f], sum(WIDE[:f])

        def take(value, f=f):
            return DT * value if f == 1 else value

        def assemble(x, carry, own=own, ext=ext, wide=wide, at=at, take=take):
            for h in range(2):
                ext[XO + x, h, YO : YO + cy, :] = take(own[x, :, halves[h]])
                ext[XO + x, h, YO - wide : YO, :] = take(yup_ref[x, h, at : at + wide, :])
                ext[XO + x, h, YO + cy : YO + cy + wide, :] = take(ydn_ref[x, h, at : at + wide, :])
            return carry

        lax.fori_loop(0, cx, assemble, 0, unroll=True)
        for i in range(wide):
            for h in range(2):
                ext[XO - wide + i, h, YO : YO + cy, :] = take(xup_ref[at + i, h])
                ext[XO + cx + i, h, YO : YO + cy, :] = take(xdn_ref[at + i, h])
        for c, layer, count, start in CORNER:
            if c != f:
                continue
            for ref, x in ((xup_ref, XO - layer), (xdn_ref, XO + cx + layer - 1)):
                for h in range(2):
                    ext[x, h, YO - count : YO, :] = take(ref[LAYERS, h, start : start + count, :])
                    ext[x, h, YO + cy : YO + cy + count, :] = take(ref[LAYERS + 1, h, start : start + count, :])

    total = jnp.int32(0)
    own_total = jnp.int32(0)
    for i in range(len(near)):
        for j in range(16):
            entry = near_s[i, j]
            list_s[total] = entry
            total = total + (entry >= 0).astype(jnp.int32)
        if i == 0:
            own_total = total
    for j in range(BATCH):
        list_s[total + j] = 0
    batches = lax.div(total + BATCH - 1, BATCH)

    def locate(e):
        entry = list_s[e]
        return lax.shift_right_logical(entry, 7) & 31, lax.shift_right_logical(entry, 6) & 1, entry & 63

    def posted(e):
        place = lax.shift_right_logical(list_s[e], 12)
        owner = lax.shift_right_logical(place, 3)
        return lax.rem(owner, ny), lax.div(owner, ny), place & 7

    rows = table_rows(nx)

    def pick(batch, carry):
        for j in range(BATCH):
            pick_one(batch * BATCH + j)
        return carry

    def pick_one(e):
        column, line, k = posted(e)
        at = column * rows + lax.rem(line, rows)
        pick_v[pl.ds(e, 1), :] = tab_ref[pl.ds(at, 1), :]
        which_v[pl.ds(e, 1), :] = jnp.broadcast_to(lax.div(line, rows) * GROUP + k, (1, LANES))

    lax.fori_loop(0, batches, pick, 0)
    lanes = lax.broadcasted_iota(jnp.int32, pick_v.shape, 1)
    for n in range(3):
        chosen = jnp.where(lanes - 8 * n == which_v[...], pick_v[...], 0.0)
        amp_v[n] = jnp.broadcast_to(DT * jnp.sum(chosen, axis=1, keepdims=True), pick_v.shape)

    lo_x, hi_x, lo_y, hi_y = gx == 0, gx == nx - 1, gy == 0, gy == ny - 1

    def clear_outside(ref):
        @pl.when(lo_x)
        def _():
            ref[XO - 1] = jnp.zeros(ref.shape[1:], jnp.float32)

        @pl.when(hi_x)
        def _():
            ref[XO + cx] = jnp.zeros(ref.shape[1:], jnp.float32)

        @pl.when(lo_y)
        def _():
            ref[:, :, YO - 1 : YO, :] = jnp.zeros((ref.shape[0], 2, 1, LANES), jnp.float32)

        @pl.when(hi_y)
        def _():
            ref[:, :, YO + cy : YO + cy + 1, :] = jnp.zeros((ref.shape[0], 2, 1, LANES), jnp.float32)

    first = lax.broadcasted_iota(jnp.int32, (8, LANES), 1) == 0
    last = lax.broadcasted_iota(jnp.int32, (8, LANES), 1) == LANES - 1

    def spread(ref, x, h, y, tiles, extra=0):
        return [ref[x, h, pl.ds(y + t, 8, stride=tiles), :] for t in range(-extra, tiles + extra)]

    def depth(v0, v1):
        f0, f1 = pltpu.roll(v0, 1, 1), pltpu.roll(v1, 1, 1)
        b0, b1 = pltpu.roll(v0, LANES - 1, 1), pltpu.roll(v1, LANES - 1, 1)
        before = (jnp.where(first, 0.0, f0), jnp.where(first, f0, f1))
        after = (jnp.where(last, b1, b0), jnp.where(last, 0.0, b1))
        return before, after

    def forward(src, dst, lo, hi, y, tiles):
        def plane(x, carry):
            mid = [spread(src, x, h, y, tiles, 1) for h in range(2)]
            nxt = [spread(src, x + 1, h, y, tiles) for h in range(2)]
            prv = [spread(src, x - 1, h, y, tiles) for h in range(2)]
            kappa = [spread(kap, x, h, y, tiles) for h in range(2)]
            for t in range(tiles):
                before, after = depth(mid[0][t + 1], mid[1][t + 1])
                for h in range(2):
                    f = mid[h][t + 1]
                    pairs = ((nxt[h][t], prv[h][t]), (mid[h][t + 2], mid[h][t]), (after[h], before[h]))
                    (sx, sy, sz), (dx, dy, dz) = zip(*[(p + m, p - m) for p, m in pairs])
                    lap = (sx + sy) + (sz - 6.0 * f)
                    adv = (0.25 * DT * VEL[0]) * (sx * dx) + ((0.25 * DT * VEL[1]) * (sy * dy) + (0.25 * DT * VEL[2]) * (sz * dz))
                    dst[x, h, pl.ds(y + t, 8, stride=tiles), :] = f + (kappa[h][t] * lap - adv)
            return carry

        lax.fori_loop(lo, hi, plane, 0, unroll=True)

    def actuate(n, dst):
        def some(batch, carry):
            for j in range(BATCH):
                e = batch * BATCH + j
                x, h, y = locate(e)
                dst[x, h, pl.ds(y, 1), :] += amp_v[n, pl.ds(e, 1), :]
            return carry

        lax.fori_loop(0, batches, some, 0)
        clear_outside(dst)

    forward(s0, s1, XO - 5, XO, YO - 4, 5)
    forward(s0, s1, XO, XO + cx, YO - 5, 6)
    forward(s0, s1, XO + cx, XO + cx + 5, YO - 4, 5)
    actuate(0, s1)
    forward(s1, s2, XO - 4, XO + cx + 4, YO - 4, 5)
    actuate(1, s2)
    forward(s2, s3, XO - 3, XO + cx + 3, YO - 3, 5)
    actuate(2, s3)

    def scale(x, carry):
        for h in range(2):
            qa[x, h] = kap[x, h] * a4[x, h]
        return carry

    lax.fori_loop(XO - 4, XO + cx + 4, scale, 0, unroll=True)

    def step(adj, q, state, x, y, tiles, emit):
        mid = [spread(adj, x, h, y, tiles, 1) for h in range(2)]
        qmid = [spread(q, x, h, y, tiles, 1) for h in range(2)]
        for t in range(tiles):
            before, after = depth(mid[0][t + 1], mid[1][t + 1])
            qbefore, qafter = depth(qmid[0][t + 1], qmid[1][t + 1])
            for h in range(2):
                at = pl.ds(y + t, 8, stride=tiles)
                lap = (
                    (q[x + 1, h, at, :] + q[x - 1, h, at, :])
                    + (qmid[h][t + 2] + qmid[h][t])
                    + ((qafter[h] + qbefore[h]) - 6.0 * qmid[h][t + 1])
                )
                drift = (
                    (0.5 * DT * VEL[0]) * (adj[x + 1, h, at, :] - adj[x - 1, h, at, :])
                    + (0.5 * DT * VEL[1]) * (mid[h][t + 2] - mid[h][t])
                    + (0.5 * DT * VEL[2]) * (after[h] - before[h])
                )
                emit(h, t, at, mid[h][t + 1] + (lap + state[x, h, at, :] * drift))

    def backward(adj, q, state, dst, qdst, wide):
        y = YO - wide

        def plane(x, carry):
            def emit(h, t, at, value):
                dst[x, h, at, :] = value
                qdst[x, h, at, :] = kap[x, h, at, :] * value

            step(adj, q, state, x, y, 5, emit)
            return carry

        lax.fori_loop(XO - wide, XO + cx + wide, plane, 0, unroll=True)
        clear_outside(dst)

    backward(a4, qa, s3, a3, qb, 3)
    backward(a3, qb, s2, a2, qa, 2)
    backward(a2, qa, s1, a1, qb, 1)

    writes = []
    for part in range(0, cx, PIECE):
        for x in range(part, part + PIECE):

            def emit(h, t, at, value, x=x):
                res[x, h, pl.ds(t, 8, stride=cy // 8), :] = value

            step(a1, qb, s0, XO + x, YO, cy // 8, emit)
        for h in range(2):
            there = out_ref.at[part : part + PIECE, :, halves[h]]
            writes.append(pltpu.make_async_copy(res.at[part : part + PIECE, h], there, out_sems.at[len(writes)]))
            writes[-1].start()

    msg_ref[...] = jnp.zeros(msg_ref.shape, jnp.float32)

    def foot(e, carry):
        x, h, y = locate(e)
        for n, adj in enumerate((a1, a2, a3, a4)):
            sum_v[n, pl.ds(e, 1), :] = adj[x, h, pl.ds(y, 1), :]
        column, line, k = posted(e)
        which_v[pl.ds(e, 1), :] = jnp.broadcast_to(lax.div(column, 8) * GROUP + k, (1, LANES))
        return carry

    lax.fori_loop(0, own_total, foot, 0)
    part = jnp.zeros((16, LANES), jnp.float32)
    for n in range(4):
        sums = DT * jnp.sum(sum_v[n], axis=1, keepdims=True)
        part = jnp.where(lanes[:16] - 8 * n == which_v[0:16, :], sums, part)
    sum_v[0] = part

    def post(e, carry):
        column, line, k = posted(e)
        msg_ref[pl.ds(line * FOLD + lax.rem(column, 8), 1), :] += sum_v[0, pl.ds(e, 1), :]
        return carry

    lax.fori_loop(0, own_total, post, 0)
    for write in writes:
        write.wait()


def sum_kernel(got_ref, out_ref):
    total = jnp.sum(got_ref[...], axis=0)
    for at in range(0, out_ref.shape[0], 8):
        rows = min(8, out_ref.shape[0])
        out_ref[at : at + rows, :] = pltpu.roll(total, (LANES - GROUP * (at // 8)) % LANES, 1)[0:rows]


def gradient_kernel(got_ref, flag_ref, out_ref):
    steps, owned = out_ref.shape
    total = jnp.sum(got_ref[...], axis=0, keepdims=True) * flag_ref[0:1, :]
    for n in range(steps):
        out_ref[n : n + 1, :] = total[:, n * owned : (n + 1) * owned]


ANY = pl.BlockSpec(memory_space=pl.ANY)
VM = pl.BlockSpec(memory_space=pltpu.VMEM)
SM = pl.BlockSpec(memory_space=pltpu.SMEM)


def shards(
    checkpoint, terminal_adjoint, diffusivity, controls, owner_map, act_ids, slot_tiles, slot_count, free_list,
):
    cx, cy, cz = checkpoint.shape
    nx, ny = lax.axis_size("gx"), lax.axis_size("gy")
    f32 = jnp.float32

    def shape(*dims):
        return jax.ShapeDtypeStruct(dims, f32)

    def shift(value, axis, way):
        size = lax.axis_size(axis)
        pairs = [(i, i + way) for i in range(size) if 0 <= i + way < size]
        return lax.ppermute(value, axis, pairs)

    fields = (checkpoint, diffusivity, terminal_adjoint)
    yup, ydn, ids, row = pl.pallas_call(
        functools.partial(first_kernel, cx, cy),
        out_shape=[shape(cx, 2, 16, LANES)] * 2 + [shape(8, LANES), shape(nx, LANES)],
        in_specs=[ANY] * 8,
        out_specs=[VM] * 4,
        scratch_shapes=[
            pltpu.VMEM((3, cx, 8, cz), f32),
            pltpu.VMEM((3, cx, 8, cz), f32),
            pltpu.SMEM(owner_map.shape, jnp.int32),
            pltpu.SMEM(controls.shape, f32),
            pltpu.SMEM(act_ids.shape, jnp.int32),
            pltpu.SMEM(slot_tiles.shape, jnp.int32),
            pltpu.SMEM(slot_count.shape, jnp.int32),
            pltpu.SemaphoreType.DMA((6,)),
            pltpu.SemaphoreType.DMA((5,)),
        ],
        compiler_params=pltpu.CompilerParams(vmem_limit_bytes=60 << 20),
        name="first",
    )(*fields, owner_map, controls, act_ids, slot_tiles, slot_count)
    yup, ydn = shift(yup, "gy", 1), shift(ydn, "gy", -1)
    got = lax.all_to_all(row, "gx", 0, 0, tiled=True)
    rows = table_rows(nx)
    xup, xdn, table = pl.pallas_call(
        functools.partial(second_kernel, cx, cy, nx, ny),
        out_shape=[shape(LAYERS + 2, 2, cy, LANES)] * 2 + [shape(ny, rows, LANES)],
        in_specs=[ANY] * 3 + [VM] * 4,
        out_specs=[VM] * 3,
        scratch_shapes=[pltpu.SemaphoreType.DMA((12,))],
        compiler_params=pltpu.CompilerParams(vmem_limit_bytes=32 << 20),
        name="second",
    )(*fields, yup, ydn, ids, got)
    xup, xdn = shift(xup, "gx", 1), shift(xdn, "gx", -1)
    table = lax.all_to_all(table, "gy", 0, 0, tiled=True).reshape(ny * rows, LANES)

    ext = pltpu.VMEM((cx + 2 * XO, 2, YR, LANES), f32)
    start_adjoint, message, flags = pl.pallas_call(
        functools.partial(window_kernel, cx, cy, nx, ny),
        out_shape=[shape(cx, cy, cz), shape(nx * FOLD, LANES), shape(8, LANES)],
        in_specs=[VM] * 11,
        out_specs=[ANY, VM, VM],
        scratch_shapes=[ext] * 11
        + [
            pltpu.VMEM((16, LANES), jnp.int32),
            pltpu.SMEM((16, LANES), jnp.int32),
            pltpu.SMEM((160,), jnp.int32),
            pltpu.VMEM((152, LANES), f32),
            pltpu.VMEM((152, LANES), jnp.int32),
            pltpu.VMEM((3, 152, LANES), f32),
            pltpu.VMEM((4, 16, LANES), f32),
            pltpu.SemaphoreType.DMA,
            pltpu.VMEM((cx, 2, cy, LANES), f32),
            pltpu.SemaphoreType.DMA((2 * cx // PIECE,)),
        ],
        compiler_params=pltpu.CompilerParams(vmem_limit_bytes=48 << 20),
        name="window",
    )(*fields, yup, ydn, xup, xdn, ids, table, owner_map.reshape(-1, LANES), free_list)

    got = lax.all_to_all(message.reshape(nx, FOLD, LANES), "gx", 0, 0, tiled=True)
    part = pl.pallas_call(
        sum_kernel, out_shape=shape(ny, LANES), in_specs=[VM], out_specs=VM, name="partial_sums"
    )(got)
    got = lax.all_to_all(part, "gy", 0, 0, tiled=True)
    gradient = pl.pallas_call(
        gradient_kernel, out_shape=shape(*controls.shape), in_specs=[VM] * 2, out_specs=VM, name="gradient"
    )(got, flags)
    return start_adjoint, gradient


def solution(mesh):
    placed = (
        P("gx", "gy", None),
        P("gx", "gy", None),
        P("gx", "gy", None),
        P(None, ("gx", "gy")),
        P(),
        P(("gx", "gy")),
        P(("gx", "gy")),
        P(("gx", "gy")),
        P(),
    )
    return jax.shard_map(
        shards,
        mesh=mesh,
        in_specs=placed,
        out_specs=(P("gx", "gy", None), P(None, ("gx", "gy"))),
        check_vma=False,
    )
```

```python
import functools

import jax
import jax.numpy as jnp
from jax import lax
from jax.experimental import pallas as pl
from jax.experimental.pallas import tpu as pltpu
from jax.sharding import PartitionSpec as P

TZ = 128
DT = 0.05
VEL = (1.0, 0.7, 0.4)
AXES = ("gx", "gy")

WIDE = (6, 5, 4)
LAYERS = sum(WIDE)
XO = 6
YO = 12
YR = 56
LANES = 128
GROUP = 32
PIECE = 4
BATCH = 4
CODE = 1024


def corner_pieces():
    pieces, row = [], 0
    for field, wide in enumerate(WIDE):
        for layer in range(1, wide):
            pieces.append((field, layer, wide - layer, row))
            row += wide - layer
    return pieces, -(-row // 8) * 8


CORNER, CORNER_ROWS = corner_pieces()


def table_rows(nx):
    return max(8, nx * GROUP // LANES)


def first_kernel(
    cx, cy, ck_ref, kp_ref, ta_ref, own_ref, ctl_ref, act_ref, til_ref, cnt_ref,
    yup_ref, ydn_ref, ids_ref, row_ref, low, high, own_s, ctl_s, act_s, til_s, cnt_s, sems, small_sems,
):
    small = [
        pltpu.make_async_copy(source, place, small_sems.at[i])
        for i, (source, place) in enumerate(
            ((own_ref, own_s), (act_ref, act_s), (til_ref, til_s), (cnt_ref, cnt_s), (ctl_ref, ctl_s))
        )
    ]
    copies = []
    for f, field in enumerate((ck_ref, kp_ref, ta_ref)):
        copies.append(pltpu.make_async_copy(field.at[:, 0:8, :], low.at[f], sems.at[2 * f]))
        copies.append(pltpu.make_async_copy(field.at[:, cy - 8 : cy, :], high.at[f], sems.at[2 * f + 1]))
    for copy in small + copies:
        copy.start()
    lane = lax.broadcasted_iota(jnp.int32, (1, LANES), 1)
    for copy in small:
        copy.wait()
    row = jnp.zeros((1, LANES), jnp.float32)
    steps, owned = ctl_s.shape
    for n in range(steps):
        for k in range(owned):
            row = jnp.where(lane == n * owned + k, ctl_s[n, k], row)
    row_ref[...] = jnp.broadcast_to(row, row_ref.shape)
    ids = jnp.zeros((1, LANES), jnp.int32)
    for j in range(act_s.shape[0]):
        code = jnp.where(j < cnt_s[0], own_s[act_s[j]] * CODE + til_s[j] + 1, 0)
        ids = jnp.where(lane == j, code, ids)
    ids = ids.astype(jnp.float32)
    ids_ref[...] = jnp.broadcast_to(ids, ids_ref.shape)
    for copy in copies:
        copy.wait()
    halves = (slice(0, LANES), slice(LANES, 2 * LANES))

    def rows(x, carry):
        at = 0
        for f, wide in enumerate(WIDE):
            for h in range(2):
                yup_ref[x, h, at : at + wide, :] = high[f, x, 8 - wide : 8, halves[h]]
                ydn_ref[x, h, at : at + wide, :] = low[f, x, 0:wide, halves[h]]
            at += wide
        return carry

    lax.fori_loop(0, cx, rows, 0, unroll=True)
    yup_ref[0, 0, LAYERS : LAYERS + 1, :] = ids
    ydn_ref[0, 0, LAYERS : LAYERS + 1, :] = ids


def second_kernel(
    cx, cy, nx, ny, ck_ref, kp_ref, ta_ref, yup_ref, ydn_ref, ids_ref, got_ref,
    xup_ref, xdn_ref, tab_ref, sems,
):
    copies = []
    at = 0
    for field, wide in zip((ck_ref, kp_ref, ta_ref), WIDE):
        for h in range(2):
            half = slice(h * LANES, (h + 1) * LANES)
            for ref, x in ((xup_ref, cx - wide), (xdn_ref, 0)):
                copies.append(
                    pltpu.make_async_copy(
                        field.at[x : x + wide, :, half], ref.at[at : at + wide, h], sems.at[len(copies)]
                    )
                )
        at += wide
    for copy in copies:
        copy.start()
    for f, layer, count, start in CORNER:
        top = sum(WIDE[: f + 1])
        at = top - WIDE[f]
        for ref, x in ((xup_ref, cx - layer), (xdn_ref, layer - 1)):
            for h in range(2):
                ref[LAYERS, h, start : start + count, :] = yup_ref[x, h, top - count : top, :]
                ref[LAYERS + 1, h, start : start + count, :] = ydn_ref[x, h, at : at + count, :]
    for ref in (xup_ref, xdn_ref):
        ref[LAYERS, 0, cy - 1 : cy, :] = ids_ref[0:1, :]
        ref[LAYERS, 1, cy - 1 : cy, :] = yup_ref[0, 0, LAYERS : LAYERS + 1, :]
        ref[LAYERS + 1, 0, cy - 1 : cy, :] = ydn_ref[0, 0, LAYERS : LAYERS + 1, :]
    rows = table_rows(nx)
    if nx < rows:
        for j in range(ny):
            tab_ref[j, 0:nx, :] = got_ref[...]
            tab_ref[j, nx:rows, :] = jnp.zeros((rows - nx, LANES), jnp.float32)
    else:
        lane = lax.broadcasted_iota(jnp.int32, (rows, LANES), 1)
        table = got_ref[0:rows, :]
        for g in range(1, nx // rows):
            part = pltpu.roll(got_ref[g * rows : (g + 1) * rows, :], g * GROUP, 1)
            table = jnp.where(lane < g * GROUP, table, part)
        tab_ref[...] = jnp.broadcast_to(table[None], tab_ref.shape)
    for copy in copies:
        copy.wait()


def window_kernel(
    cx, cy, nx, ny, ck_ref, kp_ref, ta_ref,
    yup_ref, ydn_ref, xup_ref, xdn_ref, ids_ref, tab_ref, own_ref, free_ref,
    out_ref, msg_ref, flag_ref,
    s0, s1, s2, s3, kap, a4, a3, a2, a1, qa, qb,
    near_v, near_s, list_s, pick_v, which_v, amp_v, sum_v, sem, res, out_sems,
):
    gx = lax.axis_index("gx")
    gy = lax.axis_index("gy")
    halves = (slice(0, LANES), slice(LANES, 2 * LANES))
    lane = lax.broadcasted_iota(jnp.int32, (1, LANES), 1)

    spare = slice(LAYERS, LAYERS + 1)
    tail = slice(cy - 1, cy)
    near = (
        ((0, 0), ids_ref[0:1, :]),
        ((0, -1), yup_ref[0, 0, spare, :]),
        ((0, 1), ydn_ref[0, 0, spare, :]),
        ((-1, 0), xup_ref[LAYERS, 0, tail, :]),
        ((-1, -1), xup_ref[LAYERS, 1, tail, :]),
        ((-1, 1), xup_ref[LAYERS + 1, 0, tail, :]),
        ((1, 0), xdn_ref[LAYERS, 0, tail, :]),
        ((1, -1), xdn_ref[LAYERS, 1, tail, :]),
        ((1, 1), xdn_ref[LAYERS + 1, 0, tail, :]),
    )
    for i, ((a, b), codes) in enumerate(near):
        code = codes.astype(jnp.int32) - 1
        place, tile = lax.shift_right_arithmetic(code, 10), code & (CODE - 1)
        x = lax.shift_right_logical(tile, 6) + (XO + a * cx)
        y = (lax.shift_right_logical(tile, 1) & (cy - 1)) + (YO + b * cy)
        keep = code >= 0
        if a != 0:
            keep &= (x >= XO - 5) & (x < XO + cx + 5)
        if b != 0:
            keep &= (y >= YO - 5) & (y < YO + cy + 5)
        near_v[i : i + 1, :] = jnp.where(keep, place * 4096 + x * 128 + (tile & 1) * 64 + y, -1)
    ids = pltpu.make_async_copy(near_v, near_s, sem)
    ids.start()

    wide_lane = lax.broadcasted_iota(jnp.int32, (8, LANES), 1)
    sub = lax.broadcasted_iota(jnp.int32, (8, LANES), 0)
    owner = (gx * ny + gy) * 8 + sub
    found = jnp.zeros((8, LANES), jnp.int32)
    for r in range(own_ref.shape[0]):
        found = found + jnp.where(own_ref[r : r + 1, :] == owner, r * LANES + wide_lane, 0)
    actuator = jnp.broadcast_to(jnp.sum(found, axis=1, keepdims=True), (8, LANES))
    flags = jnp.zeros((8, LANES), jnp.float32)
    for n in range(free_ref.shape[0]):
        hit = jnp.zeros((8, LANES), jnp.float32)
        for c in range(free_ref.shape[1] // LANES):
            hit = jnp.where(free_ref[n : n + 1, c * LANES : (c + 1) * LANES] == actuator, 1.0, hit)
        hit = jnp.broadcast_to(jnp.max(hit, axis=1, keepdims=True), (8, LANES))
        flags = jnp.where(wide_lane == 8 * n + sub, hit, flags)
    flag_ref[...] = jnp.broadcast_to(jnp.sum(flags, axis=0, keepdims=True), (8, LANES))

    ids.wait()
    fields = ((ck_ref, s0), (kp_ref, kap), (ta_ref, a4))
    for f, (own, ext) in enumerate(fields):
        wide, at = WIDE[f], sum(WIDE[:f])

        def take(value, f=f):
            return DT * value if f == 1 else value

        def assemble(x, carry, own=own, ext=ext, wide=wide, at=at, take=take):
            for h in range(2):
                ext[XO + x, h, YO : YO + cy, :] = take(own[x, :, halves[h]])
                ext[XO + x, h, YO - wide : YO, :] = take(yup_ref[x, h, at : at + wide, :])
                ext[XO + x, h, YO + cy : YO + cy + wide, :] = take(ydn_ref[x, h, at : at + wide, :])
            return carry

        lax.fori_loop(0, cx, assemble, 0, unroll=True)
        for i in range(wide):
            for h in range(2):
                ext[XO - wide + i, h, YO : YO + cy, :] = take(xup_ref[at + i, h])
                ext[XO + cx + i, h, YO : YO + cy, :] = take(xdn_ref[at + i, h])
        for c, layer, count, start in CORNER:
            if c != f:
                continue
            for ref, x in ((xup_ref, XO - layer), (xdn_ref, XO + cx + layer - 1)):
                for h in range(2):
                    ext[x, h, YO - count : YO, :] = take(ref[LAYERS, h, start : start + count, :])
                    ext[x, h, YO + cy : YO + cy + count, :] = take(ref[LAYERS + 1, h, start : start + count, :])

    total = jnp.int32(0)
    own_total = jnp.int32(0)
    for i in range(len(near)):
        for j in range(16):
            entry = near_s[i, j]
            list_s[total] = entry
            total = total + (entry >= 0).astype(jnp.int32)
        if i == 0:
            own_total = total
    for j in range(BATCH):
        list_s[total + j] = 0
    batches = lax.div(total + BATCH - 1, BATCH)

    def locate(e):
        entry = list_s[e]
        return lax.shift_right_logical(entry, 7) & 31, lax.shift_right_logical(entry, 6) & 1, entry & 63

    def posted(e):
        place = lax.shift_right_logical(list_s[e], 12)
        owner = lax.shift_right_logical(place, 3)
        return lax.rem(owner, ny), lax.div(owner, ny), place & 7

    rows = table_rows(nx)

    def pick(batch, carry):
        for j in range(BATCH):
            pick_one(batch * BATCH + j)
        return carry

    def pick_one(e):
        column, line, k = posted(e)
        at = column * rows + lax.rem(line, rows)
        pick_v[pl.ds(e, 1), :] = tab_ref[pl.ds(at, 1), :]
        which_v[pl.ds(e, 1), :] = jnp.broadcast_to(lax.div(line, rows) * GROUP + k, (1, LANES))

    lax.fori_loop(0, batches, pick, 0)
    lanes = lax.broadcasted_iota(jnp.int32, pick_v.shape, 1)
    for n in range(3):
        chosen = jnp.where(lanes - 8 * n == which_v[...], pick_v[...], 0.0)
        amp_v[n] = jnp.broadcast_to(DT * jnp.sum(chosen, axis=1, keepdims=True), pick_v.shape)

    lo_x, hi_x, lo_y, hi_y = gx == 0, gx == nx - 1, gy == 0, gy == ny - 1

    def clear_outside(ref):
        @pl.when(lo_x)
        def _():
            ref[XO - 1] = jnp.zeros(ref.shape[1:], jnp.float32)

        @pl.when(hi_x)
        def _():
            ref[XO + cx] = jnp.zeros(ref.shape[1:], jnp.float32)

        @pl.when(lo_y)
        def _():
            ref[:, :, YO - 1 : YO, :] = jnp.zeros((ref.shape[0], 2, 1, LANES), jnp.float32)

        @pl.when(hi_y)
        def _():
            ref[:, :, YO + cy : YO + cy + 1, :] = jnp.zeros((ref.shape[0], 2, 1, LANES), jnp.float32)

    first = lax.broadcasted_iota(jnp.int32, (8, LANES), 1) == 0
    last = lax.broadcasted_iota(jnp.int32, (8, LANES), 1) == LANES - 1

    def spread(ref, x, h, y, tiles, extra=0):
        return [ref[x, h, pl.ds(y + t, 8, stride=tiles), :] for t in range(-extra, tiles + extra)]

    def depth(v0, v1):
        f0, f1 = pltpu.roll(v0, 1, 1), pltpu.roll(v1, 1, 1)
        b0, b1 = pltpu.roll(v0, LANES - 1, 1), pltpu.roll(v1, LANES - 1, 1)
        before = (jnp.where(first, 0.0, f0), jnp.where(first, f0, f1))
        after = (jnp.where(last, b1, b0), jnp.where(last, 0.0, b1))
        return before, after

    def forward(src, dst, lo, hi, y, tiles):
        def plane(x, carry):
            mid = [spread(src, x, h, y, tiles, 1) for h in range(2)]
            nxt = [spread(src, x + 1, h, y, tiles) for h in range(2)]
            prv = [spread(src, x - 1, h, y, tiles) for h in range(2)]
            kappa = [spread(kap, x, h, y, tiles) for h in range(2)]
            for t in range(tiles):
                before, after = depth(mid[0][t + 1], mid[1][t + 1])
                for h in range(2):
                    f = mid[h][t + 1]
                    pairs = ((nxt[h][t], prv[h][t]), (mid[h][t + 2], mid[h][t]), (after[h], before[h]))
                    (sx, sy, sz), (dx, dy, dz) = zip(*[(p + m, p - m) for p, m in pairs])
                    lap = (sx + sy) + (sz - 6.0 * f)
                    adv = (0.25 * DT * VEL[0]) * (sx * dx) + ((0.25 * DT * VEL[1]) * (sy * dy) + (0.25 * DT * VEL[2]) * (sz * dz))
                    dst[x, h, pl.ds(y + t, 8, stride=tiles), :] = f + (kappa[h][t] * lap - adv)
            return carry

        lax.fori_loop(lo, hi, plane, 0, unroll=True)

    def actuate(n, dst):
        def some(batch, carry):
            for j in range(BATCH):
                e = batch * BATCH + j
                x, h, y = locate(e)
                dst[x, h, pl.ds(y, 1), :] += amp_v[n, pl.ds(e, 1), :]
            return carry

        lax.fori_loop(0, batches, some, 0)
        clear_outside(dst)

    forward(s0, s1, XO - 5, XO, YO - 4, 5)
    forward(s0, s1, XO, XO + cx, YO - 5, 6)
    forward(s0, s1, XO + cx, XO + cx + 5, YO - 4, 5)
    actuate(0, s1)
    forward(s1, s2, XO - 4, XO + cx + 4, YO - 4, 5)
    actuate(1, s2)
    forward(s2, s3, XO - 3, XO + cx + 3, YO - 3, 5)
    actuate(2, s3)

    def scale(x, carry):
        for h in range(2):
            qa[x, h] = kap[x, h] * a4[x, h]
        return carry

    lax.fori_loop(XO - 4, XO + cx + 4, scale, 0, unroll=True)

    def step(adj, q, state, x, y, tiles, emit):
        mid = [spread(adj, x, h, y, tiles, 1) for h in range(2)]
        qmid = [spread(q, x, h, y, tiles, 1) for h in range(2)]
        for t in range(tiles):
            before, after = depth(mid[0][t + 1], mid[1][t + 1])
            qbefore, qafter = depth(qmid[0][t + 1], qmid[1][t + 1])
            for h in range(2):
                at = pl.ds(y + t, 8, stride=tiles)
                lap = (
                    (q[x + 1, h, at, :] + q[x - 1, h, at, :])
                    + (qmid[h][t + 2] + qmid[h][t])
                    + ((qafter[h] + qbefore[h]) - 6.0 * qmid[h][t + 1])
                )
                drift = (
                    (0.5 * DT * VEL[0]) * (adj[x + 1, h, at, :] - adj[x - 1, h, at, :])
                    + (0.5 * DT * VEL[1]) * (mid[h][t + 2] - mid[h][t])
                    + (0.5 * DT * VEL[2]) * (after[h] - before[h])
                )
                emit(h, t, at, mid[h][t + 1] + (lap + state[x, h, at, :] * drift))

    def backward(adj, q, state, dst, qdst, wide):
        y = YO - wide

        def plane(x, carry):
            def emit(h, t, at, value):
                dst[x, h, at, :] = value
                qdst[x, h, at, :] = kap[x, h, at, :] * value

            step(adj, q, state, x, y, 5, emit)
            return carry

        lax.fori_loop(XO - wide, XO + cx + wide, plane, 0, unroll=True)
        clear_outside(dst)

    backward(a4, qa, s3, a3, qb, 3)
    backward(a3, qb, s2, a2, qa, 2)
    backward(a2, qa, s1, a1, qb, 1)

    writes = []
    for part in range(0, cx, PIECE):
        for x in range(part, part + PIECE):

            def emit(h, t, at, value, x=x):
                res[x, h, pl.ds(t, 8, stride=cy // 8), :] = value

            step(a1, qb, s0, XO + x, YO, cy // 8, emit)
        for h in range(2):
            there = out_ref.at[part : part + PIECE, :, halves[h]]
            writes.append(pltpu.make_async_copy(res.at[part : part + PIECE, h], there, out_sems.at[len(writes)]))
            writes[-1].start()

    msg_ref[...] = jnp.zeros(msg_ref.shape, jnp.float32)

    def foot(e, carry):
        x, h, y = locate(e)
        for n, adj in enumerate((a1, a2, a3, a4)):
            sum_v[n, pl.ds(e, 1), :] = adj[x, h, pl.ds(y, 1), :]
        return carry

    lax.fori_loop(0, own_total, foot, 0)
    part = jnp.zeros((16, LANES), jnp.float32)
    for n in range(4):
        sums = DT * jnp.sum(sum_v[n], axis=1, keepdims=True)
        part = jnp.where(lanes[:16] - 8 * n == which_v[0:16, :], sums, part)
    sum_v[0] = part

    def post(e, carry):
        column, line, k = posted(e)
        msg_ref[pl.ds(column * rows + lax.rem(line, rows), 1), :] += sum_v[0, pl.ds(e, 1), :]
        return carry

    lax.fori_loop(0, own_total, post, 0)
    for write in writes:
        write.wait()


def sum_kernel(got_ref, out_ref):
    total = jnp.sum(got_ref[...], axis=0)
    for at in range(0, out_ref.shape[0], 8):
        rows = min(8, out_ref.shape[0])
        out_ref[at : at + rows, :] = pltpu.roll(total, (LANES - GROUP * (at // 8)) % LANES, 1)[0:rows]


def gradient_kernel(got_ref, flag_ref, out_ref):
    steps, owned = out_ref.shape
    total = jnp.sum(got_ref[...], axis=0, keepdims=True) * flag_ref[0:1, :]
    for n in range(steps):
        out_ref[n : n + 1, :] = total[:, n * owned : (n + 1) * owned]


ANY = pl.BlockSpec(memory_space=pl.ANY)
VM = pl.BlockSpec(memory_space=pltpu.VMEM)
SM = pl.BlockSpec(memory_space=pltpu.SMEM)


def shards(
    checkpoint, terminal_adjoint, diffusivity, controls, owner_map, act_ids, slot_tiles, slot_count, free_list,
):
    cx, cy, cz = checkpoint.shape
    nx, ny = lax.axis_size("gx"), lax.axis_size("gy")
    f32 = jnp.float32

    def shape(*dims):
        return jax.ShapeDtypeStruct(dims, f32)

    def shift(value, axis, way):
        size = lax.axis_size(axis)
        pairs = [(i, i + way) for i in range(size) if 0 <= i + way < size]
        return lax.ppermute(value, axis, pairs)

    fields = (checkpoint, diffusivity, terminal_adjoint)
    yup, ydn, ids, row = pl.pallas_call(
        functools.partial(first_kernel, cx, cy),
        out_shape=[shape(cx, 2, 16, LANES)] * 2 + [shape(8, LANES), shape(nx, LANES)],
        in_specs=[ANY] * 8,
        out_specs=[VM] * 4,
        scratch_shapes=[
            pltpu.VMEM((3, cx, 8, cz), f32),
            pltpu.VMEM((3, cx, 8, cz), f32),
            pltpu.SMEM(owner_map.shape, jnp.int32),
            pltpu.SMEM(controls.shape, f32),
            pltpu.SMEM(act_ids.shape, jnp.int32),
            pltpu.SMEM(slot_tiles.shape, jnp.int32),
            pltpu.SMEM(slot_count.shape, jnp.int32),
            pltpu.SemaphoreType.DMA((6,)),
            pltpu.SemaphoreType.DMA((5,)),
        ],
        compiler_params=pltpu.CompilerParams(vmem_limit_bytes=60 << 20),
        name="first",
    )(*fields, owner_map, controls, act_ids, slot_tiles, slot_count)
    yup, ydn = shift(yup, "gy", 1), shift(ydn, "gy", -1)
    got = lax.all_to_all(row, "gx", 0, 0, tiled=True)
    rows = table_rows(nx)
    xup, xdn, table = pl.pallas_call(
        functools.partial(second_kernel, cx, cy, nx, ny),
        out_shape=[shape(LAYERS + 2, 2, cy, LANES)] * 2 + [shape(ny, rows, LANES)],
        in_specs=[ANY] * 3 + [VM] * 4,
        out_specs=[VM] * 3,
        scratch_shapes=[pltpu.SemaphoreType.DMA((12,))],
        compiler_params=pltpu.CompilerParams(vmem_limit_bytes=32 << 20),
        name="second",
    )(*fields, yup, ydn, ids, got)
    xup, xdn = shift(xup, "gx", 1), shift(xdn, "gx", -1)
    table = lax.all_to_all(table, "gy", 0, 0, tiled=True).reshape(ny * rows, LANES)

    ext = pltpu.VMEM((cx + 2 * XO, 2, YR, LANES), f32)
    start_adjoint, message, flags = pl.pallas_call(
        functools.partial(window_kernel, cx, cy, nx, ny),
        out_shape=[shape(cx, cy, cz), shape(ny * rows, LANES), shape(8, LANES)],
        in_specs=[VM] * 11,
        out_specs=[ANY, VM, VM],
        scratch_shapes=[ext] * 11
        + [
            pltpu.VMEM((16, LANES), jnp.int32),
            pltpu.SMEM((16, LANES), jnp.int32),
            pltpu.SMEM((160,), jnp.int32),
            pltpu.VMEM((152, LANES), f32),
            pltpu.VMEM((152, LANES), jnp.int32),
            pltpu.VMEM((3, 152, LANES), f32),
            pltpu.VMEM((4, 16, LANES), f32),
            pltpu.SemaphoreType.DMA,
            pltpu.VMEM((cx, 2, cy, LANES), f32),
            pltpu.SemaphoreType.DMA((2 * cx // PIECE,)),
        ],
        compiler_params=pltpu.CompilerParams(vmem_limit_bytes=48 << 20),
        name="window",
    )(*fields, yup, ydn, xup, xdn, ids, table, owner_map.reshape(-1, LANES), free_list)

    got = lax.all_to_all(message.reshape(ny, rows, LANES), "gy", 0, 0, tiled=True)
    part = pl.pallas_call(
        sum_kernel, out_shape=shape(nx, LANES), in_specs=[VM], out_specs=VM, name="partial_sums"
    )(got)
    got = lax.all_to_all(part, "gx", 0, 0, tiled=True)
    gradient = pl.pallas_call(
        gradient_kernel, out_shape=shape(*controls.shape), in_specs=[VM] * 2, out_specs=VM, name="gradient"
    )(got, flags)
    return start_adjoint, gradient


def solution(mesh):
    placed = (
        P("gx", "gy", None),
        P("gx", "gy", None),
        P("gx", "gy", None),
        P(None, ("gx", "gy")),
        P(),
        P(("gx", "gy")),
        P(("gx", "gy")),
        P(("gx", "gy")),
        P(),
    )
    return jax.shard_map(
        shards,
        mesh=mesh,
        in_specs=placed,
        out_specs=(P("gx", "gy", None), P(None, ("gx", "gy"))),
        check_vma=False,
    )
```

```python
import functools

import jax
import jax.numpy as jnp
from jax import lax
from jax.experimental import pallas as pl
from jax.experimental.pallas import tpu as pltpu
from jax.sharding import PartitionSpec as P

TZ = 128
DT = 0.05
VEL = (1.0, 0.7, 0.4)
AXES = ("gx", "gy")

WIDE = (6, 5, 4)
LAYERS = sum(WIDE)
XO = 6
YO = 12
YR = 56
LANES = 128
FOLD = 2
GROUP = 32
PIECE = 4
BATCH = 4
CODE = 1024


def corner_pieces():
    pieces, row = [], 0
    for field, wide in enumerate(WIDE):
        for layer in range(1, wide):
            pieces.append((field, layer, wide - layer, row))
            row += wide - layer
    return pieces, -(-row // 8) * 8


CORNER, CORNER_ROWS = corner_pieces()


def lines(nx):
    return [[4 * y + c for y in range(nx // 4)] for c in range(4)]


def sheets(nx, ny):
    return [[(4 * y + c) * ny + j for c in range(4) for j in range(ny)] for y in range(nx // 4)]


def place_of(line, column, ny):
    y = lax.shift_right_logical(line, 2)
    return FOLD * ((line & 3) * ny + column) + (y & (FOLD - 1)), lax.div(y, FOLD) * GROUP


def first_kernel(
    cx, cy, ck_ref, kp_ref, ta_ref, own_ref, ctl_ref, act_ref, til_ref, cnt_ref,
    yup_ref, ydn_ref, ids_ref, row_ref, low, high, own_s, ctl_s, act_s, til_s, cnt_s, sems, small_sems,
):
    small = [
        pltpu.make_async_copy(source, place, small_sems.at[i])
        for i, (source, place) in enumerate(
            ((own_ref, own_s), (act_ref, act_s), (til_ref, til_s), (cnt_ref, cnt_s), (ctl_ref, ctl_s))
        )
    ]
    copies = []
    for f, field in enumerate((ck_ref, kp_ref, ta_ref)):
        copies.append(pltpu.make_async_copy(field.at[:, 0:8, :], low.at[f], sems.at[2 * f]))
        copies.append(pltpu.make_async_copy(field.at[:, cy - 8 : cy, :], high.at[f], sems.at[2 * f + 1]))
    for copy in small + copies:
        copy.start()
    lane = lax.broadcasted_iota(jnp.int32, (1, LANES), 1)
    for copy in small:
        copy.wait()
    row = jnp.zeros((1, LANES), jnp.float32)
    steps, owned = ctl_s.shape
    for n in range(steps):
        for k in range(owned):
            row = jnp.where(lane == n * owned + k, ctl_s[n, k], row)
    row_ref[...] = jnp.broadcast_to(row, row_ref.shape)
    ids = jnp.zeros((1, LANES), jnp.int32)
    for j in range(act_s.shape[0]):
        code = jnp.where(j < cnt_s[0], own_s[act_s[j]] * CODE + til_s[j] + 1, 0)
        ids = jnp.where(lane == j, code, ids)
    ids = ids.astype(jnp.float32)
    ids_ref[...] = jnp.broadcast_to(ids, ids_ref.shape)
    for copy in copies:
        copy.wait()
    halves = (slice(0, LANES), slice(LANES, 2 * LANES))

    def rows(x, carry):
        at = 0
        for f, wide in enumerate(WIDE):
            for h in range(2):
                yup_ref[x, h, at : at + wide, :] = high[f, x, 8 - wide : 8, halves[h]]
                ydn_ref[x, h, at : at + wide, :] = low[f, x, 0:wide, halves[h]]
            at += wide
        return carry

    lax.fori_loop(0, cx, rows, 0, unroll=True)
    yup_ref[0, 0, LAYERS : LAYERS + 1, :] = ids
    ydn_ref[0, 0, LAYERS : LAYERS + 1, :] = ids


def second_kernel(
    cx, cy, nx, ny, ck_ref, kp_ref, ta_ref, yup_ref, ydn_ref, ids_ref, got_ref,
    xup_ref, xdn_ref, tab_ref, sems,
):
    copies = []
    at = 0
    for field, wide in zip((ck_ref, kp_ref, ta_ref), WIDE):
        for h in range(2):
            half = slice(h * LANES, (h + 1) * LANES)
            for ref, x in ((xup_ref, cx - wide), (xdn_ref, 0)):
                copies.append(
                    pltpu.make_async_copy(
                        field.at[x : x + wide, :, half], ref.at[at : at + wide, h], sems.at[len(copies)]
                    )
                )
        at += wide
    for copy in copies:
        copy.start()
    for f, layer, count, start in CORNER:
        top = sum(WIDE[: f + 1])
        at = top - WIDE[f]
        for ref, x in ((xup_ref, cx - layer), (xdn_ref, layer - 1)):
            for h in range(2):
                ref[LAYERS, h, start : start + count, :] = yup_ref[x, h, top - count : top, :]
                ref[LAYERS + 1, h, start : start + count, :] = ydn_ref[x, h, at : at + count, :]
    for ref in (xup_ref, xdn_ref):
        ref[LAYERS, 0, cy - 1 : cy, :] = ids_ref[0:1, :]
        ref[LAYERS, 1, cy - 1 : cy, :] = yup_ref[0, 0, LAYERS : LAYERS + 1, :]
        ref[LAYERS + 1, 0, cy - 1 : cy, :] = ydn_ref[0, 0, LAYERS : LAYERS + 1, :]
    lane = lax.broadcasted_iota(jnp.int32, (FOLD, LANES), 1)
    table = got_ref[0:FOLD, :]
    for g in range(1, nx // 4 // FOLD):
        part = pltpu.roll(got_ref[g * FOLD : (g + 1) * FOLD, :], g * GROUP, 1)
        table = jnp.where(lane < g * GROUP, table, part)
    table = jnp.concatenate([table] * (8 // FOLD), axis=0)
    for at in range(0, tab_ref.shape[0], 8):
        tab_ref[at : at + 8, :] = table
    for copy in copies:
        copy.wait()


def window_kernel(
    cx, cy, nx, ny, ck_ref, kp_ref, ta_ref,
    yup_ref, ydn_ref, xup_ref, xdn_ref, ids_ref, tab_ref, own_ref, free_ref,
    out_ref, msg_ref, flag_ref,
    s0, s1, s2, s3, kap, a4, a3, a2, a1, qa, qb,
    near_v, near_s, list_s, pick_v, which_v, amp_v, sum_v, sem, res, out_sems,
):
    gx = lax.axis_index("gx")
    gy = lax.axis_index("gy")
    halves = (slice(0, LANES), slice(LANES, 2 * LANES))
    lane = lax.broadcasted_iota(jnp.int32, (1, LANES), 1)

    spare = slice(LAYERS, LAYERS + 1)
    tail = slice(cy - 1, cy)
    near = (
        ((0, 0), ids_ref[0:1, :]),
        ((0, -1), yup_ref[0, 0, spare, :]),
        ((0, 1), ydn_ref[0, 0, spare, :]),
        ((-1, 0), xup_ref[LAYERS, 0, tail, :]),
        ((-1, -1), xup_ref[LAYERS, 1, tail, :]),
        ((-1, 1), xup_ref[LAYERS + 1, 0, tail, :]),
        ((1, 0), xdn_ref[LAYERS, 0, tail, :]),
        ((1, -1), xdn_ref[LAYERS, 1, tail, :]),
        ((1, 1), xdn_ref[LAYERS + 1, 0, tail, :]),
    )
    for i, ((a, b), codes) in enumerate(near):
        code = codes.astype(jnp.int32) - 1
        place, tile = lax.shift_right_arithmetic(code, 10), code & (CODE - 1)
        x = lax.shift_right_logical(tile, 6) + (XO + a * cx)
        y = (lax.shift_right_logical(tile, 1) & (cy - 1)) + (YO + b * cy)
        keep = code >= 0
        if a != 0:
            keep &= (x >= XO - 5) & (x < XO + cx + 5)
        if b != 0:
            keep &= (y >= YO - 5) & (y < YO + cy + 5)
        near_v[i : i + 1, :] = jnp.where(keep, place * 4096 + x * 128 + (tile & 1) * 64 + y, -1)
    ids = pltpu.make_async_copy(near_v, near_s, sem)
    ids.start()

    wide_lane = lax.broadcasted_iota(jnp.int32, (8, LANES), 1)
    sub = lax.broadcasted_iota(jnp.int32, (8, LANES), 0)
    owner = (gx * ny + gy) * 8 + sub
    found = jnp.zeros((8, LANES), jnp.int32)
    for r in range(own_ref.shape[0]):
        found = found + jnp.where(own_ref[r : r + 1, :] == owner, r * LANES + wide_lane, 0)
    actuator = jnp.broadcast_to(jnp.sum(found, axis=1, keepdims=True), (8, LANES))
    flags = jnp.zeros((8, LANES), jnp.float32)
    for n in range(free_ref.shape[0]):
        hit = jnp.zeros((8, LANES), jnp.float32)
        for c in range(free_ref.shape[1] // LANES):
            hit = jnp.where(free_ref[n : n + 1, c * LANES : (c + 1) * LANES] == actuator, 1.0, hit)
        hit = jnp.broadcast_to(jnp.max(hit, axis=1, keepdims=True), (8, LANES))
        flags = jnp.where(wide_lane == 8 * n + sub, hit, flags)
    flag_ref[...] = jnp.broadcast_to(jnp.sum(flags, axis=0, keepdims=True), (8, LANES))

    ids.wait()
    fields = ((ck_ref, s0), (kp_ref, kap), (ta_ref, a4))
    for f, (own, ext) in enumerate(fields):
        wide, at = WIDE[f], sum(WIDE[:f])

        def take(value, f=f):
            return DT * value if f == 1 else value

        def assemble(x, carry, own=own, ext=ext, wide=wide, at=at, take=take):
            for h in range(2):
                ext[XO + x, h, YO : YO + cy, :] = take(own[x, :, halves[h]])
                ext[XO + x, h, YO - wide : YO, :] = take(yup_ref[x, h, at : at + wide, :])
                ext[XO + x, h, YO + cy : YO + cy + wide, :] = take(ydn_ref[x, h, at : at + wide, :])
            return carry

        lax.fori_loop(0, cx, assemble, 0, unroll=True)
        for i in range(wide):
            for h in range(2):
                ext[XO - wide + i, h, YO : YO + cy, :] = take(xup_ref[at + i, h])
                ext[XO + cx + i, h, YO : YO + cy, :] = take(xdn_ref[at + i, h])
        for c, layer, count, start in CORNER:
            if c != f:
                continue
            for ref, x in ((xup_ref, XO - layer), (xdn_ref, XO + cx + layer - 1)):
                for h in range(2):
                    ext[x, h, YO - count : YO, :] = take(ref[LAYERS, h, start : start + count, :])
                    ext[x, h, YO + cy : YO + cy + count, :] = take(ref[LAYERS + 1, h, start : start + count, :])

    total = jnp.int32(0)
    own_total = jnp.int32(0)
    for i in range(len(near)):
        for j in range(16):
            entry = near_s[i, j]
            list_s[total] = entry
            total = total + (entry >= 0).astype(jnp.int32)
        if i == 0:
            own_total = total
    for j in range(BATCH):
        list_s[total + j] = 0
    batches = lax.div(total + BATCH - 1, BATCH)

    def locate(e):
        entry = list_s[e]
        return lax.shift_right_logical(entry, 7) & 31, lax.shift_right_logical(entry, 6) & 1, entry & 63

    def posted(e):
        place = lax.shift_right_logical(list_s[e], 12)
        owner = lax.shift_right_logical(place, 3)
        at, first = place_of(lax.div(owner, ny), lax.rem(owner, ny), ny)
        return at, first, place & 7

    def pick(batch, carry):
        for j in range(BATCH):
            pick_one(batch * BATCH + j)
        return carry

    def pick_one(e):
        at, first, k = posted(e)
        pick_v[pl.ds(e, 1), :] = tab_ref[pl.ds(at, 1), :]
        which_v[pl.ds(e, 1), :] = jnp.broadcast_to(first + k, (1, LANES))

    lax.fori_loop(0, batches, pick, 0)
    lanes = lax.broadcasted_iota(jnp.int32, pick_v.shape, 1)
    for n in range(3):
        chosen = jnp.where(lanes - 8 * n == which_v[...], pick_v[...], 0.0)
        amp_v[n] = jnp.broadcast_to(DT * jnp.sum(chosen, axis=1, keepdims=True), pick_v.shape)

    lo_x, hi_x, lo_y, hi_y = gx == 0, gx == nx - 1, gy == 0, gy == ny - 1

    def clear_outside(ref):
        @pl.when(lo_x)
        def _():
            ref[XO - 1] = jnp.zeros(ref.shape[1:], jnp.float32)

        @pl.when(hi_x)
        def _():
            ref[XO + cx] = jnp.zeros(ref.shape[1:], jnp.float32)

        @pl.when(lo_y)
        def _():
            ref[:, :, YO - 1 : YO, :] = jnp.zeros((ref.shape[0], 2, 1, LANES), jnp.float32)

        @pl.when(hi_y)
        def _():
            ref[:, :, YO + cy : YO + cy + 1, :] = jnp.zeros((ref.shape[0], 2, 1, LANES), jnp.float32)

    first = lax.broadcasted_iota(jnp.int32, (8, LANES), 1) == 0
    last = lax.broadcasted_iota(jnp.int32, (8, LANES), 1) == LANES - 1

    def spread(ref, x, h, y, tiles, extra=0):
        return [ref[x, h, pl.ds(y + t, 8, stride=tiles), :] for t in range(-extra, tiles + extra)]

    def depth(v0, v1):
        f0, f1 = pltpu.roll(v0, 1, 1), pltpu.roll(v1, 1, 1)
        b0, b1 = pltpu.roll(v0, LANES - 1, 1), pltpu.roll(v1, LANES - 1, 1)
        before = (jnp.where(first, 0.0, f0), jnp.where(first, f0, f1))
        after = (jnp.where(last, b1, b0), jnp.where(last, 0.0, b1))
        return before, after

    def forward(src, dst, lo, hi, y, tiles):
        def plane(x, carry):
            mid = [spread(src, x, h, y, tiles, 1) for h in range(2)]
            nxt = [spread(src, x + 1, h, y, tiles) for h in range(2)]
            prv = [spread(src, x - 1, h, y, tiles) for h in range(2)]
            kappa = [spread(kap, x, h, y, tiles) for h in range(2)]
            for t in range(tiles):
                before, after = depth(mid[0][t + 1], mid[1][t + 1])
                for h in range(2):
                    f = mid[h][t + 1]
                    pairs = ((nxt[h][t], prv[h][t]), (mid[h][t + 2], mid[h][t]), (after[h], before[h]))
                    (sx, sy, sz), (dx, dy, dz) = zip(*[(p + m, p - m) for p, m in pairs])
                    lap = (sx + sy) + (sz - 6.0 * f)
                    adv = (0.25 * DT * VEL[0]) * (sx * dx) + ((0.25 * DT * VEL[1]) * (sy * dy) + (0.25 * DT * VEL[2]) * (sz * dz))
                    dst[x, h, pl.ds(y + t, 8, stride=tiles), :] = f + (kappa[h][t] * lap - adv)
            return carry

        lax.fori_loop(lo, hi, plane, 0, unroll=True)

    def actuate(n, dst):
        def some(batch, carry):
            for j in range(BATCH):
                e = batch * BATCH + j
                x, h, y = locate(e)
                dst[x, h, pl.ds(y, 1), :] += amp_v[n, pl.ds(e, 1), :]
            return carry

        lax.fori_loop(0, batches, some, 0)
        clear_outside(dst)

    forward(s0, s1, XO - 5, XO, YO - 4, 5)
    forward(s0, s1, XO, XO + cx, YO - 5, 6)
    forward(s0, s1, XO + cx, XO + cx + 5, YO - 4, 5)
    actuate(0, s1)
    forward(s1, s2, XO - 4, XO + cx + 4, YO - 4, 5)
    actuate(1, s2)
    forward(s2, s3, XO - 3, XO + cx + 3, YO - 3, 5)
    actuate(2, s3)

    def scale(x, carry):
        for h in range(2):
            qa[x, h] = kap[x, h] * a4[x, h]
        return carry

    lax.fori_loop(XO - 4, XO + cx + 4, scale, 0, unroll=True)

    def step(adj, q, state, x, y, tiles, emit):
        mid = [spread(adj, x, h, y, tiles, 1) for h in range(2)]
        qmid = [spread(q, x, h, y, tiles, 1) for h in range(2)]
        for t in range(tiles):
            before, after = depth(mid[0][t + 1], mid[1][t + 1])
            qbefore, qafter = depth(qmid[0][t + 1], qmid[1][t + 1])
            for h in range(2):
                at = pl.ds(y + t, 8, stride=tiles)
                lap = (
                    (q[x + 1, h, at, :] + q[x - 1, h, at, :])
                    + (qmid[h][t + 2] + qmid[h][t])
                    + ((qafter[h] + qbefore[h]) - 6.0 * qmid[h][t + 1])
                )
                drift = (
                    (0.5 * DT * VEL[0]) * (adj[x + 1, h, at, :] - adj[x - 1, h, at, :])
                    + (0.5 * DT * VEL[1]) * (mid[h][t + 2] - mid[h][t])
                    + (0.5 * DT * VEL[2]) * (after[h] - before[h])
                )
                emit(h, t, at, mid[h][t + 1] + (lap + state[x, h, at, :] * drift))

    def backward(adj, q, state, dst, qdst, wide):
        y = YO - wide

        def plane(x, carry):
            def emit(h, t, at, value):
                dst[x, h, at, :] = value
                qdst[x, h, at, :] = kap[x, h, at, :] * value

            step(adj, q, state, x, y, 5, emit)
            return carry

        lax.fori_loop(XO - wide, XO + cx + wide, plane, 0, unroll=True)
        clear_outside(dst)

    backward(a4, qa, s3, a3, qb, 3)
    backward(a3, qb, s2, a2, qa, 2)
    backward(a2, qa, s1, a1, qb, 1)

    writes = []
    for part in range(0, cx, PIECE):
        for x in range(part, part + PIECE):

            def emit(h, t, at, value, x=x):
                res[x, h, pl.ds(t, 8, stride=cy // 8), :] = value

            step(a1, qb, s0, XO + x, YO, cy // 8, emit)
        for h in range(2):
            there = out_ref.at[part : part + PIECE, :, halves[h]]
            writes.append(pltpu.make_async_copy(res.at[part : part + PIECE, h], there, out_sems.at[len(writes)]))
            writes[-1].start()

    msg_ref[...] = jnp.zeros(msg_ref.shape, jnp.float32)

    def foot(e, carry):
        x, h, y = locate(e)
        for n, adj in enumerate((a1, a2, a3, a4)):
            sum_v[n, pl.ds(e, 1), :] = adj[x, h, pl.ds(y, 1), :]
        return carry

    lax.fori_loop(0, own_total, foot, 0)
    part = jnp.zeros((16, LANES), jnp.float32)
    for n in range(4):
        sums = DT * jnp.sum(sum_v[n], axis=1, keepdims=True)
        part = jnp.where(lanes[:16] - 8 * n == which_v[0:16, :], sums, part)
    sum_v[0] = part

    def post(e, carry):
        at, first, k = posted(e)
        msg_ref[pl.ds(at, 1), :] += sum_v[0, pl.ds(e, 1), :]
        return carry

    lax.fori_loop(0, own_total, post, 0)
    for write in writes:
        write.wait()


def sum_kernel(got_ref, out_ref):
    total = got_ref[0:8, :]
    for at in range(8, got_ref.shape[0], 8):
        total = total + got_ref[at : at + 8, :]
    total = sum(total[at : at + FOLD] for at in range(0, 8, FOLD))
    for at in range(0, out_ref.shape[0], FOLD):
        out_ref[at : at + FOLD, :] = pltpu.roll(total, (LANES - GROUP * (at // FOLD)) % LANES, 1)


def gradient_kernel(got_ref, flag_ref, out_ref):
    steps, owned = out_ref.shape
    total = jnp.sum(got_ref[...], axis=0, keepdims=True) * flag_ref[0:1, :]
    for n in range(steps):
        out_ref[n : n + 1, :] = total[:, n * owned : (n + 1) * owned]


ANY = pl.BlockSpec(memory_space=pl.ANY)
VM = pl.BlockSpec(memory_space=pltpu.VMEM)
SM = pl.BlockSpec(memory_space=pltpu.SMEM)


def shards(
    checkpoint, terminal_adjoint, diffusivity, controls, owner_map, act_ids, slot_tiles, slot_count, free_list,
):
    cx, cy, cz = checkpoint.shape
    nx, ny = lax.axis_size("gx"), lax.axis_size("gy")
    f32 = jnp.float32

    def shape(*dims):
        return jax.ShapeDtypeStruct(dims, f32)

    def shift(value, axis, way):
        size = lax.axis_size(axis)
        pairs = [(i, i + way) for i in range(size) if 0 <= i + way < size]
        return lax.ppermute(value, axis, pairs)

    fields = (checkpoint, diffusivity, terminal_adjoint)
    yup, ydn, ids, row = pl.pallas_call(
        functools.partial(first_kernel, cx, cy),
        out_shape=[shape(cx, 2, 16, LANES)] * 2 + [shape(8, LANES), shape(nx // 4, LANES)],
        in_specs=[ANY] * 8,
        out_specs=[VM] * 4,
        scratch_shapes=[
            pltpu.VMEM((3, cx, 8, cz), f32),
            pltpu.VMEM((3, cx, 8, cz), f32),
            pltpu.SMEM(owner_map.shape, jnp.int32),
            pltpu.SMEM(controls.shape, f32),
            pltpu.SMEM(act_ids.shape, jnp.int32),
            pltpu.SMEM(slot_tiles.shape, jnp.int32),
            pltpu.SMEM(slot_count.shape, jnp.int32),
            pltpu.SemaphoreType.DMA((6,)),
            pltpu.SemaphoreType.DMA((5,)),
        ],
        compiler_params=pltpu.CompilerParams(vmem_limit_bytes=60 << 20),
        name="first",
    )(*fields, owner_map, controls, act_ids, slot_tiles, slot_count)
    yup, ydn = shift(yup, "gy", 1), shift(ydn, "gy", -1)
    line, sheet = lines(nx), sheets(nx, ny)
    rows = 4 * ny * FOLD
    got = lax.all_to_all(row, "gx", 0, 0, axis_index_groups=line, tiled=True)
    xup, xdn, table = pl.pallas_call(
        functools.partial(second_kernel, cx, cy, nx, ny),
        out_shape=[shape(LAYERS + 2, 2, cy, LANES)] * 2 + [shape(rows, LANES)],
        in_specs=[ANY] * 3 + [VM] * 4,
        out_specs=[VM] * 3,
        scratch_shapes=[pltpu.SemaphoreType.DMA((12,))],
        compiler_params=pltpu.CompilerParams(vmem_limit_bytes=32 << 20),
        name="second",
    )(*fields, yup, ydn, ids, got)
    xup, xdn = shift(xup, "gx", 1), shift(xdn, "gx", -1)
    table = lax.all_to_all(table, AXES, 0, 0, axis_index_groups=sheet, tiled=True)

    ext = pltpu.VMEM((cx + 2 * XO, 2, YR, LANES), f32)
    start_adjoint, message, flags = pl.pallas_call(
        functools.partial(window_kernel, cx, cy, nx, ny),
        out_shape=[shape(cx, cy, cz), shape(rows, LANES), shape(8, LANES)],
        in_specs=[VM] * 11,
        out_specs=[ANY, VM, VM],
        scratch_shapes=[ext] * 11
        + [
            pltpu.VMEM((16, LANES), jnp.int32),
            pltpu.SMEM((16, LANES), jnp.int32),
            pltpu.SMEM((160,), jnp.int32),
            pltpu.VMEM((152, LANES), f32),
            pltpu.VMEM((152, LANES), jnp.int32),
            pltpu.VMEM((3, 152, LANES), f32),
            pltpu.VMEM((4, 16, LANES), f32),
            pltpu.SemaphoreType.DMA,
            pltpu.VMEM((cx, 2, cy, LANES), f32),
            pltpu.SemaphoreType.DMA((2 * cx // PIECE,)),
        ],
        compiler_params=pltpu.CompilerParams(vmem_limit_bytes=48 << 20),
        name="window",
    )(*fields, yup, ydn, xup, xdn, ids, table, owner_map.reshape(-1, LANES), free_list)

    got = lax.all_to_all(message, AXES, 0, 0, axis_index_groups=sheet, tiled=True)
    part = pl.pallas_call(
        sum_kernel, out_shape=shape(nx // 4, LANES), in_specs=[VM], out_specs=VM, name="partial_sums"
    )(got)
    got = lax.all_to_all(part, "gx", 0, 0, axis_index_groups=line, tiled=True)
    gradient = pl.pallas_call(
        gradient_kernel, out_shape=shape(*controls.shape), in_specs=[VM] * 2, out_specs=VM, name="gradient"
    )(got, flags)
    return start_adjoint, gradient


def solution(mesh):
    placed = (
        P("gx", "gy", None),
        P("gx", "gy", None),
        P("gx", "gy", None),
        P(None, ("gx", "gy")),
        P(),
        P(("gx", "gy")),
        P(("gx", "gy")),
        P(("gx", "gy")),
        P(),
    )
    return jax.shard_map(
        shards,
        mesh=mesh,
        in_specs=placed,
        out_specs=(P("gx", "gy", None), P(None, ("gx", "gy"))),
        check_vma=False,
    )
```

```python
import functools

import jax
import jax.numpy as jnp
from jax import lax
from jax.experimental import pallas as pl
from jax.experimental.pallas import tpu as pltpu
from jax.sharding import PartitionSpec as P

TZ = 128
DT = 0.05
VEL = (1.0, 0.7, 0.4)
AXES = ("gx", "gy")

WIDE = (6, 5, 4)
LAYERS = sum(WIDE)
XO = 6
YO = 12
YR = 56
LANES = 128
LINE = 4
GROUP = 32
PIECE = 4
BATCH = 4
CODE = 1024


def corner_pieces():
    pieces, row = [], 0
    for field, wide in enumerate(WIDE):
        for layer in range(1, wide):
            pieces.append((field, layer, wide - layer, row))
            row += wide - layer
    return pieces, -(-row // 8) * 8


CORNER, CORNER_ROWS = corner_pieces()


def lines(nx):
    return [[LINE * y + c for c in range(LINE)] for y in range(nx // LINE)]


def sheets(nx, ny):
    return [[(LINE * y + c) * ny + j for y in range(nx // LINE) for j in range(ny)] for c in range(LINE)]


def first_kernel(
    cx, cy, ck_ref, kp_ref, ta_ref, own_ref, ctl_ref, act_ref, til_ref, cnt_ref,
    yup_ref, ydn_ref, ids_ref, row_ref, low, high, own_s, ctl_s, act_s, til_s, cnt_s, sems, small_sems,
):
    small = [
        pltpu.make_async_copy(source, place, small_sems.at[i])
        for i, (source, place) in enumerate(
            ((own_ref, own_s), (act_ref, act_s), (til_ref, til_s), (cnt_ref, cnt_s), (ctl_ref, ctl_s))
        )
    ]
    copies = []
    for f, field in enumerate((ck_ref, kp_ref, ta_ref)):
        copies.append(pltpu.make_async_copy(field.at[:, 0:8, :], low.at[f], sems.at[2 * f]))
        copies.append(pltpu.make_async_copy(field.at[:, cy - 8 : cy, :], high.at[f], sems.at[2 * f + 1]))
    for copy in small + copies:
        copy.start()
    lane = lax.broadcasted_iota(jnp.int32, (1, LANES), 1)
    for copy in small:
        copy.wait()
    row = jnp.zeros((1, LANES), jnp.float32)
    steps, owned = ctl_s.shape
    for n in range(steps):
        for k in range(owned):
            row = jnp.where(lane == n * owned + k, ctl_s[n, k], row)
    row_ref[...] = jnp.broadcast_to(row, row_ref.shape)
    ids = jnp.zeros((1, LANES), jnp.int32)
    for j in range(act_s.shape[0]):
        code = jnp.where(j < cnt_s[0], own_s[act_s[j]] * CODE + til_s[j] + 1, 0)
        ids = jnp.where(lane == j, code, ids)
    ids = ids.astype(jnp.float32)
    ids_ref[...] = jnp.broadcast_to(ids, ids_ref.shape)
    for copy in copies:
        copy.wait()
    halves = (slice(0, LANES), slice(LANES, 2 * LANES))

    def rows(x, carry):
        at = 0
        for f, wide in enumerate(WIDE):
            for h in range(2):
                yup_ref[x, h, at : at + wide, :] = high[f, x, 8 - wide : 8, halves[h]]
                ydn_ref[x, h, at : at + wide, :] = low[f, x, 0:wide, halves[h]]
            at += wide
        return carry

    lax.fori_loop(0, cx, rows, 0, unroll=True)
    yup_ref[0, 0, LAYERS : LAYERS + 1, :] = ids
    ydn_ref[0, 0, LAYERS : LAYERS + 1, :] = ids


def second_kernel(
    cx, cy, nx, ny, ck_ref, kp_ref, ta_ref, yup_ref, ydn_ref, ids_ref, got_ref,
    xup_ref, xdn_ref, tab_ref, sems,
):
    copies = []
    at = 0
    for field, wide in zip((ck_ref, kp_ref, ta_ref), WIDE):
        for h in range(2):
            half = slice(h * LANES, (h + 1) * LANES)
            for ref, x in ((xup_ref, cx - wide), (xdn_ref, 0)):
                copies.append(
                    pltpu.make_async_copy(
                        field.at[x : x + wide, :, half], ref.at[at : at + wide, h], sems.at[len(copies)]
                    )
                )
        at += wide
    for copy in copies:
        copy.start()
    for f, layer, count, start in CORNER:
        top = sum(WIDE[: f + 1])
        at = top - WIDE[f]
        for ref, x in ((xup_ref, cx - layer), (xdn_ref, layer - 1)):
            for h in range(2):
                ref[LAYERS, h, start : start + count, :] = yup_ref[x, h, top - count : top, :]
                ref[LAYERS + 1, h, start : start + count, :] = ydn_ref[x, h, at : at + count, :]
    for ref in (xup_ref, xdn_ref):
        ref[LAYERS, 0, cy - 1 : cy, :] = ids_ref[0:1, :]
        ref[LAYERS, 1, cy - 1 : cy, :] = yup_ref[0, 0, LAYERS : LAYERS + 1, :]
        ref[LAYERS + 1, 0, cy - 1 : cy, :] = ydn_ref[0, 0, LAYERS : LAYERS + 1, :]
    lane = lax.broadcasted_iota(jnp.int32, (8, LANES), 1)
    table = jnp.broadcast_to(got_ref[0:1, :], (8, LANES))
    for c in range(1, LINE):
        part = pltpu.roll(jnp.broadcast_to(got_ref[c : c + 1, :], (8, LANES)), c * GROUP, 1)
        table = jnp.where(lane < c * GROUP, table, part)
    for at in range(0, tab_ref.shape[0], 8):
        tab_ref[at : at + 8, :] = table
    for copy in copies:
        copy.wait()


def window_kernel(
    cx, cy, nx, ny, ck_ref, kp_ref, ta_ref,
    yup_ref, ydn_ref, xup_ref, xdn_ref, ids_ref, tab_ref, own_ref, free_ref,
    out_ref, msg_ref, flag_ref,
    s0, s1, s2, s3, kap, a4, a3, a2, a1, qa, qb,
    near_v, near_s, list_s, pick_v, which_v, amp_v, sum_v, sem, res, out_sems,
):
    gx = lax.axis_index("gx")
    gy = lax.axis_index("gy")
    halves = (slice(0, LANES), slice(LANES, 2 * LANES))
    lane = lax.broadcasted_iota(jnp.int32, (1, LANES), 1)

    spare = slice(LAYERS, LAYERS + 1)
    tail = slice(cy - 1, cy)
    near = (
        ((0, 0), ids_ref[0:1, :]),
        ((0, -1), yup_ref[0, 0, spare, :]),
        ((0, 1), ydn_ref[0, 0, spare, :]),
        ((-1, 0), xup_ref[LAYERS, 0, tail, :]),
        ((-1, -1), xup_ref[LAYERS, 1, tail, :]),
        ((-1, 1), xup_ref[LAYERS + 1, 0, tail, :]),
        ((1, 0), xdn_ref[LAYERS, 0, tail, :]),
        ((1, -1), xdn_ref[LAYERS, 1, tail, :]),
        ((1, 1), xdn_ref[LAYERS + 1, 0, tail, :]),
    )
    for i, ((a, b), codes) in enumerate(near):
        code = codes.astype(jnp.int32) - 1
        place, tile = lax.shift_right_arithmetic(code, 10), code & (CODE - 1)
        x = lax.shift_right_logical(tile, 6) + (XO + a * cx)
        y = (lax.shift_right_logical(tile, 1) & (cy - 1)) + (YO + b * cy)
        keep = code >= 0
        if a != 0:
            keep &= (x >= XO - 5) & (x < XO + cx + 5)
        if b != 0:
            keep &= (y >= YO - 5) & (y < YO + cy + 5)
        near_v[i : i + 1, :] = jnp.where(keep, place * 4096 + x * 128 + (tile & 1) * 64 + y, -1)
    ids = pltpu.make_async_copy(near_v, near_s, sem)
    ids.start()

    wide_lane = lax.broadcasted_iota(jnp.int32, (8, LANES), 1)
    sub = lax.broadcasted_iota(jnp.int32, (8, LANES), 0)
    owner = (gx * ny + gy) * 8 + sub
    found = jnp.zeros((8, LANES), jnp.int32)
    for r in range(own_ref.shape[0]):
        found = found + jnp.where(own_ref[r : r + 1, :] == owner, r * LANES + wide_lane, 0)
    actuator = jnp.broadcast_to(jnp.sum(found, axis=1, keepdims=True), (8, LANES))
    flags = jnp.zeros((8, LANES), jnp.float32)
    for n in range(free_ref.shape[0]):
        hit = jnp.zeros((8, LANES), jnp.float32)
        for c in range(free_ref.shape[1] // LANES):
            hit = jnp.where(free_ref[n : n + 1, c * LANES : (c + 1) * LANES] == actuator, 1.0, hit)
        hit = jnp.broadcast_to(jnp.max(hit, axis=1, keepdims=True), (8, LANES))
        flags = jnp.where(wide_lane == 8 * n + sub, hit, flags)
    flag_ref[...] = jnp.broadcast_to(jnp.sum(flags, axis=0, keepdims=True), (8, LANES))

    ids.wait()
    fields = ((ck_ref, s0), (kp_ref, kap), (ta_ref, a4))
    for f, (own, ext) in enumerate(fields):
        wide, at = WIDE[f], sum(WIDE[:f])

        def take(value, f=f):
            return DT * value if f == 1 else value

        def assemble(x, carry, own=own, ext=ext, wide=wide, at=at, take=take):
            for h in range(2):
                ext[XO + x, h, YO : YO + cy, :] = take(own[x, :, halves[h]])
                ext[XO + x, h, YO - wide : YO, :] = take(yup_ref[x, h, at : at + wide, :])
                ext[XO + x, h, YO + cy : YO + cy + wide, :] = take(ydn_ref[x, h, at : at + wide, :])
            return carry

        lax.fori_loop(0, cx, assemble, 0, unroll=True)
        for i in range(wide):
            for h in range(2):
                ext[XO - wide + i, h, YO : YO + cy, :] = take(xup_ref[at + i, h])
                ext[XO + cx + i, h, YO : YO + cy, :] = take(xdn_ref[at + i, h])
        for c, layer, count, start in CORNER:
            if c != f:
                continue
            for ref, x in ((xup_ref, XO - layer), (xdn_ref, XO + cx + layer - 1)):
                for h in range(2):
                    ext[x, h, YO - count : YO, :] = take(ref[LAYERS, h, start : start + count, :])
                    ext[x, h, YO + cy : YO + cy + count, :] = take(ref[LAYERS + 1, h, start : start + count, :])

    total = jnp.int32(0)
    own_total = jnp.int32(0)
    for i in range(len(near)):
        for j in range(16):
            entry = near_s[i, j]
            list_s[total] = entry
            total = total + (entry >= 0).astype(jnp.int32)
        if i == 0:
            own_total = total
    for j in range(BATCH):
        list_s[total + j] = 0
    batches = lax.div(total + BATCH - 1, BATCH)

    def locate(e):
        entry = list_s[e]
        return lax.shift_right_logical(entry, 7) & 31, lax.shift_right_logical(entry, 6) & 1, entry & 63

    def posted(e):
        place = lax.shift_right_logical(list_s[e], 12)
        owner = lax.shift_right_logical(place, 3)
        line, column = lax.div(owner, ny), lax.rem(owner, ny)
        return lax.div(line, LINE) * ny + column, lax.rem(line, LINE) * GROUP, place & 7

    def pick(batch, carry):
        for j in range(BATCH):
            pick_one(batch * BATCH + j)
        return carry

    def pick_one(e):
        at, first, k = posted(e)
        pick_v[pl.ds(e, 1), :] = tab_ref[pl.ds(at, 1), :]
        which_v[pl.ds(e, 1), :] = jnp.broadcast_to(first + k, (1, LANES))

    lax.fori_loop(0, batches, pick, 0)
    lanes = lax.broadcasted_iota(jnp.int32, pick_v.shape, 1)
    for n in range(3):
        chosen = jnp.where(lanes - 8 * n == which_v[...], pick_v[...], 0.0)
        amp_v[n] = jnp.broadcast_to(DT * jnp.sum(chosen, axis=1, keepdims=True), pick_v.shape)

    lo_x, hi_x, lo_y, hi_y = gx == 0, gx == nx - 1, gy == 0, gy == ny - 1

    def clear_outside(ref):
        @pl.when(lo_x)
        def _():
            ref[XO - 1] = jnp.zeros(ref.shape[1:], jnp.float32)

        @pl.when(hi_x)
        def _():
            ref[XO + cx] = jnp.zeros(ref.shape[1:], jnp.float32)

        @pl.when(lo_y)
        def _():
            ref[:, :, YO - 1 : YO, :] = jnp.zeros((ref.shape[0], 2, 1, LANES), jnp.float32)

        @pl.when(hi_y)
        def _():
            ref[:, :, YO + cy : YO + cy + 1, :] = jnp.zeros((ref.shape[0], 2, 1, LANES), jnp.float32)

    first = lax.broadcasted_iota(jnp.int32, (8, LANES), 1) == 0
    last = lax.broadcasted_iota(jnp.int32, (8, LANES), 1) == LANES - 1

    def spread(ref, x, h, y, tiles, extra=0):
        return [ref[x, h, pl.ds(y + t, 8, stride=tiles), :] for t in range(-extra, tiles + extra)]

    def depth(v0, v1):
        f0, f1 = pltpu.roll(v0, 1, 1), pltpu.roll(v1, 1, 1)
        b0, b1 = pltpu.roll(v0, LANES - 1, 1), pltpu.roll(v1, LANES - 1, 1)
        before = (jnp.where(first, 0.0, f0), jnp.where(first, f0, f1))
        after = (jnp.where(last, b1, b0), jnp.where(last, 0.0, b1))
        return before, after

    def forward(src, dst, lo, hi, y, tiles):
        def plane(x, carry):
            mid = [spread(src, x, h, y, tiles, 1) for h in range(2)]
            nxt = [spread(src, x + 1, h, y, tiles) for h in range(2)]
            prv = [spread(src, x - 1, h, y, tiles) for h in range(2)]
            kappa = [spread(kap, x, h, y, tiles) for h in range(2)]
            for t in range(tiles):
                before, after = depth(mid[0][t + 1], mid[1][t + 1])
                for h in range(2):
                    f = mid[h][t + 1]
                    pairs = ((nxt[h][t], prv[h][t]), (mid[h][t + 2], mid[h][t]), (after[h], before[h]))
                    (sx, sy, sz), (dx, dy, dz) = zip(*[(p + m, p - m) for p, m in pairs])
                    lap = (sx + sy) + (sz - 6.0 * f)
                    adv = (0.25 * DT * VEL[0]) * (sx * dx) + ((0.25 * DT * VEL[1]) * (sy * dy) + (0.25 * DT * VEL[2]) * (sz * dz))
                    dst[x, h, pl.ds(y + t, 8, stride=tiles), :] = f + (kappa[h][t] * lap - adv)
            return carry

        lax.fori_loop(lo, hi, plane, 0, unroll=True)

    def actuate(n, dst):
        def some(batch, carry):
            for j in range(BATCH):
                e = batch * BATCH + j
                x, h, y = locate(e)
                dst[x, h, pl.ds(y, 1), :] += amp_v[n, pl.ds(e, 1), :]
            return carry

        lax.fori_loop(0, batches, some, 0)
        clear_outside(dst)

    forward(s0, s1, XO - 5, XO, YO - 4, 5)
    forward(s0, s1, XO, XO + cx, YO - 5, 6)
    forward(s0, s1, XO + cx, XO + cx + 5, YO - 4, 5)
    actuate(0, s1)
    forward(s1, s2, XO - 4, XO + cx + 4, YO - 4, 5)
    actuate(1, s2)
    forward(s2, s3, XO - 3, XO + cx + 3, YO - 3, 5)
    actuate(2, s3)

    def scale(x, carry):
        for h in range(2):
            qa[x, h] = kap[x, h] * a4[x, h]
        return carry

    lax.fori_loop(XO - 4, XO + cx + 4, scale, 0, unroll=True)

    def step(adj, q, state, x, y, tiles, emit):
        mid = [spread(adj, x, h, y, tiles, 1) for h in range(2)]
        qmid = [spread(q, x, h, y, tiles, 1) for h in range(2)]
        for t in range(tiles):
            before, after = depth(mid[0][t + 1], mid[1][t + 1])
            qbefore, qafter = depth(qmid[0][t + 1], qmid[1][t + 1])
            for h in range(2):
                at = pl.ds(y + t, 8, stride=tiles)
                lap = (
                    (q[x + 1, h, at, :] + q[x - 1, h, at, :])
                    + (qmid[h][t + 2] + qmid[h][t])
                    + ((qafter[h] + qbefore[h]) - 6.0 * qmid[h][t + 1])
                )
                drift = (
                    (0.5 * DT * VEL[0]) * (adj[x + 1, h, at, :] - adj[x - 1, h, at, :])
                    + (0.5 * DT * VEL[1]) * (mid[h][t + 2] - mid[h][t])
                    + (0.5 * DT * VEL[2]) * (after[h] - before[h])
                )
                emit(h, t, at, mid[h][t + 1] + (lap + state[x, h, at, :] * drift))

    def backward(adj, q, state, dst, qdst, wide):
        y = YO - wide

        def plane(x, carry):
            def emit(h, t, at, value):
                dst[x, h, at, :] = value
                qdst[x, h, at, :] = kap[x, h, at, :] * value

            step(adj, q, state, x, y, 5, emit)
            return carry

        lax.fori_loop(XO - wide, XO + cx + wide, plane, 0, unroll=True)
        clear_outside(dst)

    backward(a4, qa, s3, a3, qb, 3)
    backward(a3, qb, s2, a2, qa, 2)
    backward(a2, qa, s1, a1, qb, 1)

    writes = []
    for part in range(0, cx, PIECE):
        for x in range(part, part + PIECE):

            def emit(h, t, at, value, x=x):
                res[x, h, pl.ds(t, 8, stride=cy // 8), :] = value

            step(a1, qb, s0, XO + x, YO, cy // 8, emit)
        for h in range(2):
            there = out_ref.at[part : part + PIECE, :, halves[h]]
            writes.append(pltpu.make_async_copy(res.at[part : part + PIECE, h], there, out_sems.at[len(writes)]))
            writes[-1].start()

    msg_ref[...] = jnp.zeros(msg_ref.shape, jnp.float32)

    def foot(e, carry):
        x, h, y = locate(e)
        for n, adj in enumerate((a1, a2, a3, a4)):
            sum_v[n, pl.ds(e, 1), :] = adj[x, h, pl.ds(y, 1), :]
        return carry

    lax.fori_loop(0, own_total, foot, 0)
    part = jnp.zeros((16, LANES), jnp.float32)
    for n in range(4):
        sums = DT * jnp.sum(sum_v[n], axis=1, keepdims=True)
        part = jnp.where(lanes[:16] - 8 * n == which_v[0:16, :], sums, part)
    sum_v[0] = part

    def post(e, carry):
        at, first, k = posted(e)
        msg_ref[pl.ds(at, 1), :] += sum_v[0, pl.ds(e, 1), :]
        return carry

    lax.fori_loop(0, own_total, post, 0)
    for write in writes:
        write.wait()


def sum_kernel(got_ref, out_ref):
    total = got_ref[0:8, :]
    for at in range(8, got_ref.shape[0], 8):
        total = total + got_ref[at : at + 8, :]
    total = jnp.broadcast_to(jnp.sum(total, axis=0, keepdims=True), (8, LANES))
    for c in range(LINE):
        out_ref[c : c + 1, :] = pltpu.roll(total, (LANES - GROUP * c) % LANES, 1)[0:1]


def gradient_kernel(got_ref, flag_ref, out_ref):
    steps, owned = out_ref.shape
    total = jnp.sum(got_ref[...], axis=0, keepdims=True) * flag_ref[0:1, :]
    for n in range(steps):
        out_ref[n : n + 1, :] = total[:, n * owned : (n + 1) * owned]


ANY = pl.BlockSpec(memory_space=pl.ANY)
VM = pl.BlockSpec(memory_space=pltpu.VMEM)
SM = pl.BlockSpec(memory_space=pltpu.SMEM)


def shards(
    checkpoint, terminal_adjoint, diffusivity, controls, owner_map, act_ids, slot_tiles, slot_count, free_list,
):
    cx, cy, cz = checkpoint.shape
    nx, ny = lax.axis_size("gx"), lax.axis_size("gy")
    f32 = jnp.float32

    def shape(*dims):
        return jax.ShapeDtypeStruct(dims, f32)

    def shift(value, axis, way):
        size = lax.axis_size(axis)
        pairs = [(i, i + way) for i in range(size) if 0 <= i + way < size]
        return lax.ppermute(value, axis, pairs)

    fields = (checkpoint, diffusivity, terminal_adjoint)
    yup, ydn, ids, row = pl.pallas_call(
        functools.partial(first_kernel, cx, cy),
        out_shape=[shape(cx, 2, 16, LANES)] * 2 + [shape(8, LANES), shape(LINE, LANES)],
        in_specs=[ANY] * 8,
        out_specs=[VM] * 4,
        scratch_shapes=[
            pltpu.VMEM((3, cx, 8, cz), f32),
            pltpu.VMEM((3, cx, 8, cz), f32),
            pltpu.SMEM(owner_map.shape, jnp.int32),
            pltpu.SMEM(controls.shape, f32),
            pltpu.SMEM(act_ids.shape, jnp.int32),
            pltpu.SMEM(slot_tiles.shape, jnp.int32),
            pltpu.SMEM(slot_count.shape, jnp.int32),
            pltpu.SemaphoreType.DMA((6,)),
            pltpu.SemaphoreType.DMA((5,)),
        ],
        compiler_params=pltpu.CompilerParams(vmem_limit_bytes=60 << 20),
        name="first",
    )(*fields, owner_map, controls, act_ids, slot_tiles, slot_count)
    yup, ydn = shift(yup, "gy", 1), shift(ydn, "gy", -1)
    line, sheet = lines(nx), sheets(nx, ny)
    rows = nx // LINE * ny
    got = lax.all_to_all(row, "gx", 0, 0, axis_index_groups=line, tiled=True)
    xup, xdn, table = pl.pallas_call(
        functools.partial(second_kernel, cx, cy, nx, ny),
        out_shape=[shape(LAYERS + 2, 2, cy, LANES)] * 2 + [shape(rows, LANES)],
        in_specs=[ANY] * 3 + [VM] * 4,
        out_specs=[VM] * 3,
        scratch_shapes=[pltpu.SemaphoreType.DMA((12,))],
        compiler_params=pltpu.CompilerParams(vmem_limit_bytes=32 << 20),
        name="second",
    )(*fields, yup, ydn, ids, got)
    xup, xdn = shift(xup, "gx", 1), shift(xdn, "gx", -1)
    table = lax.all_to_all(table, AXES, 0, 0, axis_index_groups=sheet, tiled=True)

    ext = pltpu.VMEM((cx + 2 * XO, 2, YR, LANES), f32)
    start_adjoint, message, flags = pl.pallas_call(
        functools.partial(window_kernel, cx, cy, nx, ny),
        out_shape=[shape(cx, cy, cz), shape(rows, LANES), shape(8, LANES)],
        in_specs=[VM] * 11,
        out_specs=[ANY, VM, VM],
        scratch_shapes=[ext] * 11
        + [
            pltpu.VMEM((16, LANES), jnp.int32),
            pltpu.SMEM((16, LANES), jnp.int32),
            pltpu.SMEM((160,), jnp.int32),
            pltpu.VMEM((152, LANES), f32),
            pltpu.VMEM((152, LANES), jnp.int32),
            pltpu.VMEM((3, 152, LANES), f32),
            pltpu.VMEM((4, 16, LANES), f32),
            pltpu.SemaphoreType.DMA,
            pltpu.VMEM((cx, 2, cy, LANES), f32),
            pltpu.SemaphoreType.DMA((2 * cx // PIECE,)),
        ],
        compiler_params=pltpu.CompilerParams(vmem_limit_bytes=48 << 20),
        name="window",
    )(*fields, yup, ydn, xup, xdn, ids, table, owner_map.reshape(-1, LANES), free_list)

    got = lax.all_to_all(message, AXES, 0, 0, axis_index_groups=sheet, tiled=True)
    part = pl.pallas_call(
        sum_kernel, out_shape=shape(LINE, LANES), in_specs=[VM], out_specs=VM, name="partial_sums"
    )(got)
    got = lax.all_to_all(part, "gx", 0, 0, axis_index_groups=line, tiled=True)
    gradient = pl.pallas_call(
        gradient_kernel, out_shape=shape(*controls.shape), in_specs=[VM] * 2, out_specs=VM, name="gradient"
    )(got, flags)
    return start_adjoint, gradient


def solution(mesh):
    placed = (
        P("gx", "gy", None),
        P("gx", "gy", None),
        P("gx", "gy", None),
        P(None, ("gx", "gy")),
        P(),
        P(("gx", "gy")),
        P(("gx", "gy")),
        P(("gx", "gy")),
        P(),
    )
    return jax.shard_map(
        shards,
        mesh=mesh,
        in_specs=placed,
        out_specs=(P("gx", "gy", None), P(None, ("gx", "gy"))),
        check_vma=False,
    )
```

```python
import functools

import jax
import jax.numpy as jnp
from jax import lax
from jax.experimental import pallas as pl
from jax.experimental.pallas import tpu as pltpu
from jax.sharding import PartitionSpec as P

TZ = 128
DT = 0.05
VEL = (1.0, 0.7, 0.4)
AXES = ("gx", "gy")

WIDE = (6, 5, 4)
LAYERS = sum(WIDE)
XO = 6
YO = 12
YR = 56
LANES = 128
FOLD = 2
GROUP = 32
PIECE = 4
BATCH = 4
CODE = 1024


def corner_pieces():
    pieces, row = [], 0
    for field, wide in enumerate(WIDE):
        for layer in range(1, wide):
            pieces.append((field, layer, wide - layer, row))
            row += wide - layer
    return pieces, -(-row // 8) * 8


CORNER, CORNER_ROWS = corner_pieces()


def lines(nx):
    return [[4 * y + c for y in range(nx // 4)] for c in range(4)]


def sheets(nx, ny):
    return [[(4 * y + c) * ny + j for c in range(4) for j in range(ny)] for y in range(nx // 4)]


def place_of(line, column, ny):
    y = lax.shift_right_logical(line, 2)
    return FOLD * ((line & 3) * ny + column) + (y & (FOLD - 1)), lax.div(y, FOLD) * GROUP


def first_kernel(
    cx, cy, ck_ref, kp_ref, ta_ref, own_ref, ctl_ref, act_ref, til_ref, cnt_ref,
    yup_ref, ydn_ref, ids_ref, row_ref, low, high, own_s, ctl_s, act_s, til_s, cnt_s, sems, small_sems,
):
    small = [
        pltpu.make_async_copy(source, place, small_sems.at[i])
        for i, (source, place) in enumerate(
            ((own_ref, own_s), (act_ref, act_s), (til_ref, til_s), (cnt_ref, cnt_s), (ctl_ref, ctl_s))
        )
    ]
    copies = []
    for f, field in enumerate((ck_ref, kp_ref, ta_ref)):
        copies.append(pltpu.make_async_copy(field.at[:, 0:8, :], low.at[f], sems.at[2 * f]))
        copies.append(pltpu.make_async_copy(field.at[:, cy - 8 : cy, :], high.at[f], sems.at[2 * f + 1]))
    for copy in small + copies:
        copy.start()
    lane = lax.broadcasted_iota(jnp.int32, (1, LANES), 1)
    for copy in small:
        copy.wait()
    row = jnp.zeros((1, LANES), jnp.float32)
    steps, owned = ctl_s.shape
    for n in range(steps):
        for k in range(owned):
            row = jnp.where(lane == n * owned + k, ctl_s[n, k], row)
    row_ref[...] = jnp.broadcast_to(row, row_ref.shape)
    ids = jnp.zeros((1, LANES), jnp.int32)
    for j in range(act_s.shape[0]):
        code = jnp.where(j < cnt_s[0], own_s[act_s[j]] * CODE + til_s[j] + 1, 0)
        ids = jnp.where(lane == j, code, ids)
    ids = ids.astype(jnp.float32)
    ids_ref[...] = jnp.broadcast_to(ids, ids_ref.shape)
    for copy in copies:
        copy.wait()
    halves = (slice(0, LANES), slice(LANES, 2 * LANES))

    def rows(x, carry):
        at = 0
        for f, wide in enumerate(WIDE):
            for h in range(2):
                yup_ref[x, h, at : at + wide, :] = high[f, x, 8 - wide : 8, halves[h]]
                ydn_ref[x, h, at : at + wide, :] = low[f, x, 0:wide, halves[h]]
            at += wide
        return carry

    lax.fori_loop(0, cx, rows, 0, unroll=True)
    yup_ref[0, 0, LAYERS : LAYERS + 1, :] = ids
    ydn_ref[0, 0, LAYERS : LAYERS + 1, :] = ids


def second_kernel(
    cx, cy, nx, ny, ck_ref, kp_ref, ta_ref, yup_ref, ydn_ref, ids_ref, got_ref,
    xup_ref, xdn_ref, tab_ref, sems,
):
    copies = []
    at = 0
    for field, wide in zip((ck_ref, kp_ref, ta_ref), WIDE):
        for h in range(2):
            half = slice(h * LANES, (h + 1) * LANES)
            for ref, x in ((xup_ref, cx - wide), (xdn_ref, 0)):
                copies.append(
                    pltpu.make_async_copy(
                        field.at[x : x + wide, :, half], ref.at[at : at + wide, h], sems.at[len(copies)]
                    )
                )
        at += wide
    for copy in copies:
        copy.start()
    for f, layer, count, start in CORNER:
        top = sum(WIDE[: f + 1])
        at = top - WIDE[f]
        for ref, x in ((xup_ref, cx - layer), (xdn_ref, layer - 1)):
            for h in range(2):
                ref[LAYERS, h, start : start + count, :] = yup_ref[x, h, top - count : top, :]
                ref[LAYERS + 1, h, start : start + count, :] = ydn_ref[x, h, at : at + count, :]
    for ref in (xup_ref, xdn_ref):
        ref[LAYERS, 0, cy - 1 : cy, :] = ids_ref[0:1, :]
        ref[LAYERS, 1, cy - 1 : cy, :] = yup_ref[0, 0, LAYERS : LAYERS + 1, :]
        ref[LAYERS + 1, 0, cy - 1 : cy, :] = ydn_ref[0, 0, LAYERS : LAYERS + 1, :]
    lane = lax.broadcasted_iota(jnp.int32, (FOLD, LANES), 1)
    table = got_ref[0:FOLD, :]
    for g in range(1, nx // 4 // FOLD):
        part = pltpu.roll(got_ref[g * FOLD : (g + 1) * FOLD, :], g * GROUP, 1)
        table = jnp.where(lane < g * GROUP, table, part)
    table = jnp.concatenate([table] * (8 // FOLD), axis=0)
    for at in range(0, tab_ref.shape[0], 8):
        tab_ref[at : at + 8, :] = table
    for copy in copies:
        copy.wait()


def window_kernel(
    cx, cy, nx, ny, ck_ref, kp_ref, ta_ref,
    yup_ref, ydn_ref, xup_ref, xdn_ref, ids_ref, tab_ref, own_ref, free_ref,
    out_ref, msg_ref, flag_ref,
    s0, s1, s2, s3, kap, a4, a3, a2, a1, qa, qb,
    near_v, near_s, list_s, pick_v, which_v, amp_v, sum_v, sem, res, out_sems,
):
    gx = lax.axis_index("gx")
    gy = lax.axis_index("gy")
    halves = (slice(0, LANES), slice(LANES, 2 * LANES))
    lane = lax.broadcasted_iota(jnp.int32, (1, LANES), 1)

    spare = slice(LAYERS, LAYERS + 1)
    tail = slice(cy - 1, cy)
    near = (
        ((0, 0), ids_ref[0:1, :]),
        ((0, -1), yup_ref[0, 0, spare, :]),
        ((0, 1), ydn_ref[0, 0, spare, :]),
        ((-1, 0), xup_ref[LAYERS, 0, tail, :]),
        ((-1, -1), xup_ref[LAYERS, 1, tail, :]),
        ((-1, 1), xup_ref[LAYERS + 1, 0, tail, :]),
        ((1, 0), xdn_ref[LAYERS, 0, tail, :]),
        ((1, -1), xdn_ref[LAYERS, 1, tail, :]),
        ((1, 1), xdn_ref[LAYERS + 1, 0, tail, :]),
    )
    for i, ((a, b), codes) in enumerate(near):
        code = codes.astype(jnp.int32) - 1
        place, tile = lax.shift_right_arithmetic(code, 10), code & (CODE - 1)
        x = lax.shift_right_logical(tile, 6) + (XO + a * cx)
        y = (lax.shift_right_logical(tile, 1) & (cy - 1)) + (YO + b * cy)
        keep = code >= 0
        if a != 0:
            keep &= (x >= XO - 5) & (x < XO + cx + 5)
        if b != 0:
            keep &= (y >= YO - 5) & (y < YO + cy + 5)
        near_v[i : i + 1, :] = jnp.where(keep, place * 4096 + x * 128 + (tile & 1) * 64 + y, -1)
    ids = pltpu.make_async_copy(near_v, near_s, sem)
    ids.start()

    wide_lane = lax.broadcasted_iota(jnp.int32, (8, LANES), 1)
    sub = lax.broadcasted_iota(jnp.int32, (8, LANES), 0)
    owner = (gx * ny + gy) * 8 + sub
    found = jnp.zeros((8, LANES), jnp.int32)
    for r in range(own_ref.shape[0]):
        found = found + jnp.where(own_ref[r : r + 1, :] == owner, r * LANES + wide_lane, 0)
    actuator = jnp.broadcast_to(jnp.sum(found, axis=1, keepdims=True), (8, LANES))
    flags = jnp.zeros((8, LANES), jnp.float32)
    for n in range(free_ref.shape[0]):
        hit = jnp.zeros((8, LANES), jnp.float32)
        for c in range(free_ref.shape[1] // LANES):
            hit = jnp.where(free_ref[n : n + 1, c * LANES : (c + 1) * LANES] == actuator, 1.0, hit)
        hit = jnp.broadcast_to(jnp.max(hit, axis=1, keepdims=True), (8, LANES))
        flags = jnp.where(wide_lane == 8 * n + sub, hit, flags)
    flag_ref[...] = jnp.broadcast_to(jnp.sum(flags, axis=0, keepdims=True), (8, LANES))

    ids.wait()
    fields = ((ck_ref, s0), (kp_ref, kap), (ta_ref, a4))
    for f, (own, ext) in enumerate(fields):
        wide, at = WIDE[f], sum(WIDE[:f])

        def take(value, f=f):
            return DT * value if f == 1 else value

        def assemble(x, carry, own=own, ext=ext, wide=wide, at=at, take=take):
            for h in range(2):
                ext[XO + x, h, YO : YO + cy, :] = take(own[x, :, halves[h]])
                ext[XO + x, h, YO - wide : YO, :] = take(yup_ref[x, h, at : at + wide, :])
                ext[XO + x, h, YO + cy : YO + cy + wide, :] = take(ydn_ref[x, h, at : at + wide, :])
            return carry

        lax.fori_loop(0, cx, assemble, 0, unroll=True)
        for i in range(wide):
            for h in range(2):
                ext[XO - wide + i, h, YO : YO + cy, :] = take(xup_ref[at + i, h])
                ext[XO + cx + i, h, YO : YO + cy, :] = take(xdn_ref[at + i, h])
        for c, layer, count, start in CORNER:
            if c != f:
                continue
            for ref, x in ((xup_ref, XO - layer), (xdn_ref, XO + cx + layer - 1)):
                for h in range(2):
                    ext[x, h, YO - count : YO, :] = take(ref[LAYERS, h, start : start + count, :])
                    ext[x, h, YO + cy : YO + cy + count, :] = take(ref[LAYERS + 1, h, start : start + count, :])

    total = jnp.int32(0)
    own_total = jnp.int32(0)
    for i in range(len(near)):
        for j in range(16):
            entry = near_s[i, j]
            list_s[total] = entry
            total = total + (entry >= 0).astype(jnp.int32)
        if i == 0:
            own_total = total
    for j in range(BATCH):
        list_s[total + j] = 0
    batches = lax.div(total + BATCH - 1, BATCH)

    def locate(e):
        entry = list_s[e]
        return lax.shift_right_logical(entry, 7) & 31, lax.shift_right_logical(entry, 6) & 1, entry & 63

    def posted(e):
        place = lax.shift_right_logical(list_s[e], 12)
        owner = lax.shift_right_logical(place, 3)
        at, first = place_of(lax.div(owner, ny), lax.rem(owner, ny), ny)
        return at, first, place & 7

    def pick(batch, carry):
        for j in range(BATCH):
            pick_one(batch * BATCH + j)
        return carry

    def pick_one(e):
        at, first, k = posted(e)
        pick_v[pl.ds(e, 1), :] = tab_ref[pl.ds(at, 1), :]
        which_v[pl.ds(e, 1), :] = jnp.broadcast_to(first + k, (1, LANES))

    lax.fori_loop(0, batches, pick, 0)
    lanes = lax.broadcasted_iota(jnp.int32, pick_v.shape, 1)
    for n in range(3):
        chosen = jnp.where(lanes - 8 * n == which_v[...], pick_v[...], 0.0)
        amp_v[n] = jnp.broadcast_to(DT * jnp.sum(chosen, axis=1, keepdims=True), pick_v.shape)

    lo_x, hi_x, lo_y, hi_y = gx == 0, gx == nx - 1, gy == 0, gy == ny - 1

    def clear_outside(ref):
        @pl.when(lo_x)
        def _():
            ref[XO - 1] = jnp.zeros(ref.shape[1:], jnp.float32)

        @pl.when(hi_x)
        def _():
            ref[XO + cx] = jnp.zeros(ref.shape[1:], jnp.float32)

        @pl.when(lo_y)
        def _():
            ref[:, :, YO - 1 : YO, :] = jnp.zeros((ref.shape[0], 2, 1, LANES), jnp.float32)

        @pl.when(hi_y)
        def _():
            ref[:, :, YO + cy : YO + cy + 1, :] = jnp.zeros((ref.shape[0], 2, 1, LANES), jnp.float32)

    first = lax.broadcasted_iota(jnp.int32, (8, LANES), 1) == 0
    last = lax.broadcasted_iota(jnp.int32, (8, LANES), 1) == LANES - 1

    def spread(ref, x, h, y, tiles, extra=0):
        return [ref[x, h, pl.ds(y + t, 8, stride=tiles), :] for t in range(-extra, tiles + extra)]

    def depth(v0, v1):
        f0, f1 = pltpu.roll(v0, 1, 1), pltpu.roll(v1, 1, 1)
        b0, b1 = pltpu.roll(v0, LANES - 1, 1), pltpu.roll(v1, LANES - 1, 1)
        before = (jnp.where(first, 0.0, f0), jnp.where(first, f0, f1))
        after = (jnp.where(last, b1, b0), jnp.where(last, 0.0, b1))
        return before, after

    def forward(src, dst, lo, hi, y, tiles):
        def plane(x, carry):
            mid = [spread(src, x, h, y, tiles, 1) for h in range(2)]
            nxt = [spread(src, x + 1, h, y, tiles) for h in range(2)]
            prv = [spread(src, x - 1, h, y, tiles) for h in range(2)]
            kappa = [spread(kap, x, h, y, tiles) for h in range(2)]
            for t in range(tiles):
                before, after = depth(mid[0][t + 1], mid[1][t + 1])
                for h in range(2):
                    f = mid[h][t + 1]
                    pairs = ((nxt[h][t], prv[h][t]), (mid[h][t + 2], mid[h][t]), (after[h], before[h]))
                    (sx, sy, sz), (dx, dy, dz) = zip(*[(p + m, p - m) for p, m in pairs])
                    lap = (sx + sy) + (sz - 6.0 * f)
                    adv = (0.25 * DT * VEL[0]) * (sx * dx) + ((0.25 * DT * VEL[1]) * (sy * dy) + (0.25 * DT * VEL[2]) * (sz * dz))
                    dst[x, h, pl.ds(y + t, 8, stride=tiles), :] = f + (kappa[h][t] * lap - adv)
            return carry

        lax.fori_loop(lo, hi, plane, 0, unroll=True)

    def actuate(n, dst):
        def some(batch, carry):
            for j in range(BATCH):
                e = batch * BATCH + j
                x, h, y = locate(e)
                dst[x, h, pl.ds(y, 1), :] += amp_v[n, pl.ds(e, 1), :]
            return carry

        lax.fori_loop(0, batches, some, 0)
        clear_outside(dst)

    forward(s0, s1, XO - 5, XO, YO - 4, 5)
    forward(s0, s1, XO, XO + cx, YO - 5, 6)
    forward(s0, s1, XO + cx, XO + cx + 5, YO - 4, 5)
    actuate(0, s1)
    forward(s1, s2, XO - 4, XO + cx + 4, YO - 4, 5)
    actuate(1, s2)
    forward(s2, s3, XO - 3, XO + cx + 3, YO - 3, 5)
    actuate(2, s3)

    def scale(x, carry):
        for h in range(2):
            qa[x, h] = kap[x, h] * a4[x, h]
        return carry

    lax.fori_loop(XO - 4, XO + cx + 4, scale, 0, unroll=True)

    def step(adj, q, state, x, y, tiles, emit):
        mid = [spread(adj, x, h, y, tiles, 1) for h in range(2)]
        qmid = [spread(q, x, h, y, tiles, 1) for h in range(2)]
        for t in range(tiles):
            before, after = depth(mid[0][t + 1], mid[1][t + 1])
            qbefore, qafter = depth(qmid[0][t + 1], qmid[1][t + 1])
            for h in range(2):
                at = pl.ds(y + t, 8, stride=tiles)
                lap = (
                    (q[x + 1, h, at, :] + q[x - 1, h, at, :])
                    + (qmid[h][t + 2] + qmid[h][t])
                    + ((qafter[h] + qbefore[h]) - 6.0 * qmid[h][t + 1])
                )
                drift = (
                    (0.5 * DT * VEL[0]) * (adj[x + 1, h, at, :] - adj[x - 1, h, at, :])
                    + (0.5 * DT * VEL[1]) * (mid[h][t + 2] - mid[h][t])
                    + (0.5 * DT * VEL[2]) * (after[h] - before[h])
                )
                emit(h, t, at, mid[h][t + 1] + (lap + state[x, h, at, :] * drift))

    def backward(adj, q, state, dst, qdst, wide):
        y = YO - wide

        def plane(x, carry):
            def emit(h, t, at, value):
                dst[x, h, at, :] = value
                qdst[x, h, at, :] = kap[x, h, at, :] * value

            step(adj, q, state, x, y, 5, emit)
            return carry

        lax.fori_loop(XO - wide, XO + cx + wide, plane, 0, unroll=True)
        clear_outside(dst)

    backward(a4, qa, s3, a3, qb, 3)
    backward(a3, qb, s2, a2, qa, 2)
    backward(a2, qa, s1, a1, qb, 1)

    writes = []
    for part in range(0, cx, PIECE):
        for x in range(part, part + PIECE):

            def emit(h, t, at, value, x=x):
                res[x, h, pl.ds(t, 8, stride=cy // 8), :] = value

            step(a1, qb, s0, XO + x, YO, cy // 8, emit)
        for h in range(2):
            there = out_ref.at[part : part + PIECE, :, halves[h]]
            writes.append(pltpu.make_async_copy(res.at[part : part + PIECE, h], there, out_sems.at[len(writes)]))
            writes[-1].start()

    msg_ref[...] = jnp.zeros(msg_ref.shape, jnp.float32)

    def foot(e, carry):
        x, h, y = locate(e)
        for n, adj in enumerate((a1, a2, a3, a4)):
            sum_v[n, pl.ds(e, 1), :] = adj[x, h, pl.ds(y, 1), :]
        at, first, k = posted(e)
        which_v[pl.ds(e, 1), :] = jnp.broadcast_to(k, (1, LANES))
        return carry

    lax.fori_loop(0, own_total, foot, 0)
    part = jnp.zeros((16, LANES), jnp.float32)
    for n in range(4):
        sums = DT * jnp.sum(sum_v[n], axis=1, keepdims=True)
        part = jnp.where(lanes[:16] - 8 * n == which_v[0:16, :], sums, part)
    sum_v[0] = part

    def post(e, carry):
        owner = lax.shift_right_logical(list_s[e], 15)
        msg_ref[pl.ds(owner, 1), :] += sum_v[0, pl.ds(e, 1), :]
        return carry

    lax.fori_loop(0, own_total, post, 0)
    for write in writes:
        write.wait()


def gradient_kernel(got_ref, flag_ref, out_ref):
    steps, owned = out_ref.shape
    total = jnp.sum(got_ref[...], axis=0, keepdims=True) * flag_ref[0:1, :]
    for n in range(steps):
        out_ref[n : n + 1, :] = total[:, n * owned : (n + 1) * owned]


ANY = pl.BlockSpec(memory_space=pl.ANY)
VM = pl.BlockSpec(memory_space=pltpu.VMEM)
SM = pl.BlockSpec(memory_space=pltpu.SMEM)


def shards(
    checkpoint, terminal_adjoint, diffusivity, controls, owner_map, act_ids, slot_tiles, slot_count, free_list,
):
    cx, cy, cz = checkpoint.shape
    nx, ny = lax.axis_size("gx"), lax.axis_size("gy")
    f32 = jnp.float32

    def shape(*dims):
        return jax.ShapeDtypeStruct(dims, f32)

    def shift(value, axis, way):
        size = lax.axis_size(axis)
        pairs = [(i, i + way) for i in range(size) if 0 <= i + way < size]
        return lax.ppermute(value, axis, pairs)

    fields = (checkpoint, diffusivity, terminal_adjoint)
    yup, ydn, ids, row = pl.pallas_call(
        functools.partial(first_kernel, cx, cy),
        out_shape=[shape(cx, 2, 16, LANES)] * 2 + [shape(8, LANES), shape(nx // 4, LANES)],
        in_specs=[ANY] * 8,
        out_specs=[VM] * 4,
        scratch_shapes=[
            pltpu.VMEM((3, cx, 8, cz), f32),
            pltpu.VMEM((3, cx, 8, cz), f32),
            pltpu.SMEM(owner_map.shape, jnp.int32),
            pltpu.SMEM(controls.shape, f32),
            pltpu.SMEM(act_ids.shape, jnp.int32),
            pltpu.SMEM(slot_tiles.shape, jnp.int32),
            pltpu.SMEM(slot_count.shape, jnp.int32),
            pltpu.SemaphoreType.DMA((6,)),
            pltpu.SemaphoreType.DMA((5,)),
        ],
        compiler_params=pltpu.CompilerParams(vmem_limit_bytes=60 << 20),
        name="first",
    )(*fields, owner_map, controls, act_ids, slot_tiles, slot_count)
    yup, ydn = shift(yup, "gy", 1), shift(ydn, "gy", -1)
    line, sheet = lines(nx), sheets(nx, ny)
    rows = 4 * ny * FOLD
    got = lax.all_to_all(row, "gx", 0, 0, axis_index_groups=line, tiled=True)
    xup, xdn, table = pl.pallas_call(
        functools.partial(second_kernel, cx, cy, nx, ny),
        out_shape=[shape(LAYERS + 2, 2, cy, LANES)] * 2 + [shape(rows, LANES)],
        in_specs=[ANY] * 3 + [VM] * 4,
        out_specs=[VM] * 3,
        scratch_shapes=[pltpu.SemaphoreType.DMA((12,))],
        compiler_params=pltpu.CompilerParams(vmem_limit_bytes=32 << 20),
        name="second",
    )(*fields, yup, ydn, ids, got)
    xup, xdn = shift(xup, "gx", 1), shift(xdn, "gx", -1)
    table = lax.all_to_all(table, AXES, 0, 0, axis_index_groups=sheet, tiled=True)

    ext = pltpu.VMEM((cx + 2 * XO, 2, YR, LANES), f32)
    start_adjoint, message, flags = pl.pallas_call(
        functools.partial(window_kernel, cx, cy, nx, ny),
        out_shape=[shape(cx, cy, cz), shape(nx * ny, LANES), shape(8, LANES)],
        in_specs=[VM] * 11,
        out_specs=[ANY, VM, VM],
        scratch_shapes=[ext] * 11
        + [
            pltpu.VMEM((16, LANES), jnp.int32),
            pltpu.SMEM((16, LANES), jnp.int32),
            pltpu.SMEM((160,), jnp.int32),
            pltpu.VMEM((152, LANES), f32),
            pltpu.VMEM((152, LANES), jnp.int32),
            pltpu.VMEM((3, 152, LANES), f32),
            pltpu.VMEM((4, 16, LANES), f32),
            pltpu.SemaphoreType.DMA,
            pltpu.VMEM((cx, 2, cy, LANES), f32),
            pltpu.SemaphoreType.DMA((2 * cx // PIECE,)),
        ],
        compiler_params=pltpu.CompilerParams(vmem_limit_bytes=48 << 20),
        name="window",
    )(*fields, yup, ydn, xup, xdn, ids, table, owner_map.reshape(-1, LANES), free_list)

    got = lax.all_to_all(message, AXES, 0, 0, tiled=True)
    gradient = pl.pallas_call(
        gradient_kernel, out_shape=shape(*controls.shape), in_specs=[VM] * 2, out_specs=VM, name="gradient"
    )(got, flags)
    return start_adjoint, gradient


def solution(mesh):
    placed = (
        P("gx", "gy", None),
        P("gx", "gy", None),
        P("gx", "gy", None),
        P(None, ("gx", "gy")),
        P(),
        P(("gx", "gy")),
        P(("gx", "gy")),
        P(("gx", "gy")),
        P(),
    )
    return jax.shard_map(
        shards,
        mesh=mesh,
        in_specs=placed,
        out_specs=(P("gx", "gy", None), P(None, ("gx", "gy"))),
        check_vma=False,
    )
```
